32 devices in a mesh: section: 4 (over z), tile: 4 (over x, core), rep: 2 (over y).
Axes of the slice: x: 2, y: 2, z: 4, core: 2. Of those that a mesh axis runs over, the one named last changes fastest.
Arguments:
- phase_shift: float32 [4, 4, 384, 384], P('section', 'tile'), may hold values from -3.140625 to 3.140625
- absorption: float32 [4, 4, 384, 384], P('section', 'tile'), may hold values from 0 to 0.5
- probe_wave: float32 [2, 256, 256], replicated, may hold values from -6 to 6
- positions: int32 [4, 2, 1, 2], P('tile', 'rep'), may hold values from 0 to 384
- counts: int32 [4, 2, 1, 256, 256], P('tile', 'rep'), may hold values from 0 to 7
Outputs:
- phase_gradient: float32 [4, 4, 384, 384], P('section', 'tile', 'rep')
- absorption_gradient: float32 [4, 4, 384, 384], P('section', 'tile', 'rep')
The draws below stay inside these ranges and needn't reach their ends.
All inputs are finite; a program needn't handle non-finite values.
Results may differ from the reference program's by a relative error of at most 0.00027.
Values sent between devices are 32-bit elements; how exact they have to be, the bound alone decides.
No kernel may reach another device: no remote copies, remote signals or barrier semaphores. Data moves between devices by JAX's collectives and lax.ppermute only.
A program may use at most 64 MiB of HBM per device.

```python
import math
import jax
import jax.numpy as jnp
from jax import lax

FR = 256
TL = 384
HALO = 128
F_DEV = 1
SLICES = 4
N_TILE = 4
N_REP = 2


def touch_ends(drawn, own_key, least, top_value):
    spot = [jax.random.randint(jax.random.fold_in(own_key, axis), (), 0, length) for axis, length in enumerate(drawn.shape)]
    main_axis = drawn.shape.index(max(drawn.shape))
    neighbour = spot[:main_axis] + [(spot[main_axis] + 1) % drawn.shape[main_axis]] + spot[main_axis + 1:]
    return drawn.at[tuple(spot)].set(least).at[tuple(neighbour)].set(top_value)


def steps_of(key, extent, pieces, least, high):
    factor_of, own = 1.0, jax.random.fold_in(key, 6)
    for dim, parts in pieces:
        draws = jnp.exp(jax.random.uniform(jax.random.fold_in(own, dim), (parts,), jnp.float32, least / len(pieces), high / len(pieces)))
        factor_of = factor_of * jnp.repeat(draws, extent[dim] // parts).reshape([-1 if axis == dim else 1 for axis in range(len(extent))])
    return factor_of


def scatter_about(stream_key, shape, width, reach, kind=jnp.bfloat16):
    array = jax.random.normal(stream_key, shape, jnp.float32) * width
    return jnp.minimum(jnp.maximum(array, -reach), reach).astype(kind)


def setup_inputs(seed: int = 0) -> dict:
    splits = jax.random.split(jax.random.key(seed), 6)
    phase_shift = jnp.clip(jax.random.uniform(splits[0], (SLICES, N_TILE, TL, TL), jnp.float32, -3.140625, 3.140625), -3.140625, 3.140625)
    absorption = jnp.clip(0.5 * jax.random.uniform(splits[1], (SLICES, N_TILE, TL, TL), jnp.float32) ** steps_of(splits[1], (SLICES, N_TILE, TL, TL), ((0, 4), (1, 4)), -0.2, 0.2), 0.0, 0.5)
    probe_wave = scatter_about(splits[2], (2, FR, FR), 1.0, 6.0, jnp.float32)
    positions = touch_ends(jax.random.randint(splits[3], (N_TILE, N_REP, F_DEV, 2), 0, TL + 2 * HALO - FR + 1), jax.random.fold_in(splits[3], 1), 0, TL + 2 * HALO - FR).astype(jnp.int32)
    counts = touch_ends(jax.random.randint(splits[4], (N_TILE, N_REP, F_DEV, FR, FR), 0, 8), jax.random.fold_in(splits[4], 1), 0, 7).astype(jnp.int32)
    return {"phase_shift": phase_shift, "absorption": absorption, "probe_wave": probe_wave, "positions": positions, "counts": counts}


dead_time = 0.1
background = 0.1
loss_weight = 0.1
fresnel = 0.5

def kernel_angles(length):
    indices = jnp.arange(length, dtype=jnp.int32)
    shifted = jnp.where(indices < length // 2, indices, indices - length).astype(jnp.float32)
    return math.pi * fresnel * shifted * shifted / length

def likelihood_seed(far_re, far_im, observed):
    intensity = far_re * far_re + far_im * far_im
    shifted_total = intensity + background
    denominator = 1.0 + dead_time * shifted_total
    model_rate = shifted_total / denominator
    slope_term = loss_weight * (1.0 - observed / model_rate) / (denominator * denominator)
    return (2.0 * slope_term * far_re, 2.0 * slope_term * far_im)

def reference(phase_shift, absorption, probe_wave, positions, counts):
    grid_side = math.isqrt(N_TILE)
    span = grid_side * TL
    padded_side = span + 2 * HALO

    def assemble(field_in):
        blocks = field_in.reshape(SLICES, grid_side, grid_side, TL, TL).transpose(0, 1, 3, 2, 4)
        blocks = blocks.reshape(SLICES, span, span)
        return jnp.pad(blocks, ((0, 0), (HALO, HALO), (HALO, HALO)))
    full_phase = assemble(phase_shift)
    full_absorb = assemble(absorption)
    damping = jnp.exp(-full_absorb)
    trans_re = damping * jnp.cos(full_phase)
    trans_im = damping * jnp.sin(full_phase)
    angles = kernel_angles(FR)
    kernel_line = lax.complex(jnp.cos(angles), jnp.sin(angles))
    kernel_plane = kernel_line[:, None] * kernel_line[None, :]
    probe_field = lax.complex(probe_wave[0], probe_wave[1])
    tile_ids = jnp.repeat(jnp.arange(N_TILE, dtype=jnp.int32), N_REP * F_DEV)
    flat_positions = positions.reshape(N_TILE * N_REP * F_DEV, 2).astype(jnp.int32)
    row_starts = (tile_ids // grid_side * TL + flat_positions[:, 0]).astype(jnp.int32)
    col_starts = (tile_ids % grid_side * TL + flat_positions[:, 1]).astype(jnp.int32)
    observed_all = counts.reshape(N_TILE * N_REP * F_DEV, FR, FR).astype(jnp.float32)

    def visit(totals, item):
        row_at, col_at, observed = item
        phase_totals = list(totals[0])
        absorb_totals = list(totals[1])
        wave_now = probe_field
        objects = []
        exit_waves = []
        for slice_no in range(SLICES):
            window_re = lax.dynamic_slice(trans_re[slice_no], (row_at, col_at), (FR, FR))
            window_im = lax.dynamic_slice(trans_im[slice_no], (row_at, col_at), (FR, FR))
            object_field = lax.complex(window_re, window_im)
            exit_wave = object_field * wave_now
            objects.append(object_field)
            exit_waves.append(exit_wave)
            if slice_no < SLICES - 1:
                wave_now = jnp.fft.ifft2(jnp.fft.fft2(exit_wave) * kernel_plane)
            else:
                wave_now = jnp.fft.fft2(exit_wave, norm='ortho')
        seed_re, seed_im = likelihood_seed(jnp.real(wave_now), jnp.imag(wave_now), observed)
        grad_wave = lax.complex(seed_re, seed_im)
        for slice_no in reversed(range(SLICES)):
            if slice_no < SLICES - 1:
                back_wave = jnp.fft.ifft2(jnp.fft.fft2(grad_wave) * jnp.conj(kernel_plane))
            else:
                back_wave = jnp.fft.ifft2(grad_wave, norm='ortho')
            product = jnp.conj(back_wave) * exit_waves[slice_no]
            phase_term = -jnp.imag(product)
            absorb_term = -jnp.real(product)
            current = lax.dynamic_slice(phase_totals[slice_no], (row_at, col_at), (FR, FR))
            phase_totals[slice_no] = lax.dynamic_update_slice(phase_totals[slice_no], current + phase_term, (row_at, col_at))
            current = lax.dynamic_slice(absorb_totals[slice_no], (row_at, col_at), (FR, FR))
            absorb_totals[slice_no] = lax.dynamic_update_slice(absorb_totals[slice_no], current + absorb_term, (row_at, col_at))
            grad_wave = jnp.conj(objects[slice_no]) * back_wave
        return ((tuple(phase_totals), tuple(absorb_totals)), None)
    empty_planes = tuple((jnp.zeros((padded_side, padded_side), jnp.float32) for slice_no in range(SLICES)))
    totals, unused = lax.scan(visit, (empty_planes, empty_planes), (row_starts, col_starts, observed_all))

    def disassemble(planes):
        inner = jnp.stack(planes)[:, HALO:HALO + span, HALO:HALO + span]
        inner = inner.reshape(SLICES, grid_side, TL, grid_side, TL).transpose(0, 1, 3, 2, 4)
        return inner.reshape(SLICES, N_TILE, TL, TL)
    return (disassemble(totals[0]), disassemble(totals[1]))
```

```python
import math

import jax
import jax.numpy as jnp
import ml_dtypes
import numpy as np
from jax import lax
from jax.experimental import pallas as pl
from jax.experimental.pallas import tpu as pltpu
from jax.sharding import PartitionSpec as P

HALO = 128
LANES = 128
AXES = ("section", "tile", "rep")

dead_time = 0.1
background = 0.1
loss_weight = 0.1
fresnel = 0.5

f32 = jnp.float32
bf16 = jnp.bfloat16

SMEM = pl.BlockSpec(memory_space=pltpu.SMEM)
VMEM = pl.BlockSpec(memory_space=pltpu.VMEM)
ANY = pl.BlockSpec(memory_space=pl.ANY)


def two_parts(matrix):
    high = matrix.astype(ml_dtypes.bfloat16)
    low = (matrix - high.astype(np.float64)).astype(ml_dtypes.bfloat16)
    return np.stack([high, low])


def from_left(matrix):
    return np.block([[matrix.real, -matrix.imag], [matrix.imag, matrix.real]])


def from_right(matrix):
    return np.block([[matrix.real, matrix.imag], [-matrix.imag, matrix.real]])


def wave_tables(length):
    half = length // 2
    indices = np.arange(length)
    shifted = np.where(indices < half, indices, indices - length)
    kernel = np.exp(1j * math.pi * fresnel * shifted.astype(np.float64) ** 2 / length)
    spread = np.fft.ifft(kernel)
    circulant = spread[(indices[:, None] - indices[None, :]) % length]
    first, second = circulant[:half, :half], circulant[:half, half:]
    plus, minus = (first + second) / 2, (first - second) / 2
    near = [from_left(plus), from_left(minus), from_right(plus), from_right(minus)]
    turns = np.outer(indices[:half], indices[:half]) % half
    even = np.exp(-2j * math.pi * turns / half) / math.sqrt(length)
    odd = even * np.exp(-2j * math.pi * indices[:half] / length)[None, :]
    far = [from_left(even), from_left(odd), from_right(even.T), from_right(odd.T)]
    back = [from_left(even.T), from_left(odd.T), from_right(even), from_right(odd)]
    sort = np.zeros((length, length))
    sort[np.arange(half), 2 * np.arange(half)] = 1
    sort[half + np.arange(half), 2 * np.arange(half) + 1] = 1
    tables = np.stack([two_parts(m) for m in near + far + back])
    return tables, np.stack([sort, sort.T]).astype(ml_dtypes.bfloat16)


def fitted(function, degree):
    top = math.pi**2
    fit = np.polynomial.chebyshev.Chebyshev.interpolate(function, degree, domain=[0.0, top])
    return [float(c) for c in fit.convert(kind=np.polynomial.Polynomial).coef]


def sine_ratio(u):
    angle = np.sqrt(np.maximum(u, 1e-12))
    return np.sin(angle) / angle


SINE = fitted(sine_ratio, 8)
COSINE = fitted(lambda u: np.cos(np.sqrt(np.maximum(u, 0.0))), 8)


def polynomial(coefficients, u):
    total = jnp.full_like(u, coefficients[-1])
    for c in coefficients[-2::-1]:
        total = total * u + c
    return total


def cos_sin(angle):
    square = angle * angle
    return polynomial(COSINE, square), angle * polynomial(SINE, square)


def halves(value):
    high = value.astype(bf16)
    return high, (value - high.astype(f32)).astype(bf16)


def dot(a, b):
    return jnp.dot(a, b, preferred_element_type=f32)


def left_by(tables, index, value):
    high, low = halves(value)
    return dot(tables[index, 0], high) + dot(tables[index, 1], high) + dot(tables[index, 0], low)


def right_by(tables, index, value):
    high, low = halves(value)
    return dot(high, tables[index, 0]) + dot(high, tables[index, 1]) + dot(low, tables[index, 0])


def propagate(tables, at, re, im, fold, unfold):
    half = re.shape[0] // 2
    re0, re1, im0, im1 = re[:half], re[half:], im[:half], im[half:]
    if fold:
        re0, re1, im0, im1 = re0 + re1, re0 - re1, im0 + im1, im0 - im1
    first = left_by(tables, at, jnp.concatenate([re0, im0], 0))
    second = left_by(tables, at + 1, jnp.concatenate([re1, im1], 0))
    if unfold:
        first, second = first + second, first - second
    re = jnp.concatenate([first[:half], second[:half]], 0)
    im = jnp.concatenate([first[half:], second[half:]], 0)
    re0, re1, im0, im1 = re[:, :half], re[:, half:], im[:, :half], im[:, half:]
    if fold:
        re0, re1, im0, im1 = re0 + re1, re0 - re1, im0 + im1, im0 - im1
    first = right_by(tables, at + 2, jnp.concatenate([re0, im0], 1))
    second = right_by(tables, at + 3, jnp.concatenate([re1, im1], 1))
    if unfold:
        first, second = first + second, first - second
    re = jnp.concatenate([first[:, :half], second[:, :half]], 1)
    im = jnp.concatenate([first[:, half:], second[:, half:]], 1)
    return re, im


def near_field(tables, re, im):
    return propagate(tables, 0, re, im, True, True)


def far_field(tables, re, im):
    return propagate(tables, 4, re, im, True, False)


def far_back(tables, re, im):
    return propagate(tables, 8, re, im, False, True)


def likelihood_seed(far_re, far_im, observed):
    intensity = far_re * far_re + far_im * far_im
    shifted_total = intensity + background
    denominator = 1.0 + dead_time * shifted_total
    model_rate = shifted_total / denominator
    slope_term = loss_weight * (1.0 - observed / model_rate) / (denominator * denominator)
    return (2.0 * slope_term * far_re, 2.0 * slope_term * far_im)


def lane_part(column):
    block = jnp.minimum(column // LANES, 2)
    return pl.multiple_of(block * LANES, LANES), column - block * LANES


def cut_columns(read, column, width):
    start, rest = lane_part(column)
    wide = read(start, width + LANES)
    return pltpu.roll(wide, (width + LANES) - rest, 1)[:, :width]


def cut_rows(read, row, height, total):
    block = jnp.minimum(row // 8, (total - height) // 8 - 1)
    tall = read(pl.multiple_of(block * 8, 8), height + 8)
    return pltpu.roll(tall, (height + 8) - (row - block * 8), 0)[:height]


def put_columns(target, plane, rows, value, column):
    start, rest = lane_part(column)
    wide = jnp.concatenate([value, jnp.zeros((value.shape[0], LANES), f32)], 1)
    wide = pltpu.roll(wide, rest, 1)
    here = (plane, rows, pl.ds(start, wide.shape[1]))
    target[here] = target[here] + wide


class Place:
    def __init__(self, grid_side):
        self.grid_side = grid_side
        self.ways = 1 if grid_side == 2 else 2

    def section(self):
        return lax.axis_index("section")

    def rep(self):
        return lax.axis_index("rep")

    def row(self):
        return lax.axis_index("tile") // self.grid_side

    def column(self):
        return lax.axis_index("tile") % self.grid_side

    def owner(self):
        return 1 + self.column() % 2

    def sent(self, index, way):
        return 1 - index if self.ways == 1 else way

    def received(self, index, way):
        return 1 - index if self.ways == 1 else 1 - way


def solution(mesh):
    sections, tiles, reps = (mesh.shape[a] for a in AXES)
    grid_side = math.isqrt(tiles)
    place = Place(grid_side)
    ways = place.ways

    def everywhere(target_of):
        pairs = []
        for s in range(sections):
            for t in range(tiles):
                for r in range(reps):
                    target = target_of(s, t // grid_side, t % grid_side, r)
                    if target is None:
                        continue
                    ts, ty, tx, tr = target
                    if not (0 <= ty < grid_side and 0 <= tx < grid_side):
                        continue
                    pairs.append(
                        ((s * tiles + t) * reps + r, (ts * tiles + ty * grid_side + tx) * reps + tr)
                    )
        return pairs

    def move(value, target_of):
        return lax.ppermute(value, AXES, everywhere(target_of))

    def trade_rows(values):
        if ways == 1:
            return [move(values[0], lambda s, y, x, r: (s, 1 - y, x, r))]
        return [
            move(values[0], lambda s, y, x, r: (s, y - 1, x, r)),
            move(values[1], lambda s, y, x, r: (s, y + 1, x, r)),
        ]

    def trade_columns(values):
        if ways == 1:
            return [move(values[0], lambda s, y, x, r: (s, y, 1 - x, r))]
        return [
            move(values[0], lambda s, y, x, r: (s, y, x - 1, r)),
            move(values[1], lambda s, y, x, r: (s, y, x + 1, r)),
        ]

    def owner_of(x):
        return 1 + x % 2

    def shards(phase_shift, absorption, probe_wave, positions, counts):
        width = phase_shift.shape[2]
        frame = probe_wave.shape[1]
        extent = width + 2 * HALO
        half_rows = width // reps
        edge = width + HALO
        phase = phase_shift.reshape(width, width)
        absorb = absorption.reshape(width, width)
        spot = positions.reshape(1, 2)
        observed = counts.reshape(frame, frame)
        sds = jax.ShapeDtypeStruct

        spots_rows = trade_rows([spot] * ways)
        spots_rep = move(
            jnp.concatenate([spot] + spots_rows, 0), lambda s, y, x, r: (s, y, x, 1 - r)
        )

        def edge_kernel(phase_ref, absorb_ref, *refs):
            outs, sem = refs[:ways], refs[ways]
            copies = []
            for way in range(ways):
                side = place.sent(place.column(), way)
                start = pl.multiple_of(side * (width - HALO), LANES)
                for plane, ref in enumerate((phase_ref, absorb_ref)):
                    copy = pltpu.make_async_copy(
                        ref.at[:, pl.ds(start, HALO)], outs[way].at[plane], sem.at[2 * way + plane]
                    )
                    copy.start()
                    copies.append(copy)
            for copy in copies:
                copy.wait()

        edges = pl.pallas_call(
            edge_kernel,
            out_shape=[sds((2, width, HALO), f32)] * ways,
            in_specs=[ANY, ANY],
            out_specs=[VMEM] * ways,
            scratch_shapes=[pltpu.SemaphoreType.DMA((2 * ways,))],
            name="edge_columns",
        )(phase, absorb)
        sides = trade_columns(edges)

        def strip_kernel(phase_ref, absorb_ref, *refs):
            side_refs, spot_refs = refs[:ways], refs[ways : 2 * ways]
            outs, wide = refs[2 * ways : 3 * ways], refs[3 * ways]
            for way in range(ways):
                below = place.sent(place.row(), way)
                first = pl.multiple_of(below * (width - HALO), 8)
                rows = pl.ds(first, HALO)
                column = spot_refs[way if ways == 1 else 1 - way][0, 1]
                for plane, ref in enumerate((phase_ref, absorb_ref)):
                    if ways == 1:
                        wide[:, :HALO] = jnp.zeros((HALO, HALO), f32)
                        wide[:, edge:] = jnp.zeros((HALO, HALO), f32)
                    wide[:, HALO:edge] = ref[rows, :]
                    for other in range(ways):
                        start = place.received(place.column(), other) * edge
                        wide[:, pl.ds(pl.multiple_of(start, LANES), HALO)] = side_refs[other][
                            plane, rows, :
                        ]
                    outs[way][plane] = cut_columns(
                        lambda start, count: wide[:, pl.ds(start, count)], column, frame
                    )

        strips = pl.pallas_call(
            strip_kernel,
            out_shape=[sds((2, HALO, frame), f32)] * ways,
            in_specs=[VMEM] * (2 + ways) + [SMEM] * ways,
            out_specs=[VMEM] * ways,
            scratch_shapes=[pltpu.VMEM((HALO, extent), f32)],
            name="halo_rows",
        )(phase, absorb, *sides, *spots_rows)
        rims = trade_rows(strips)

        def window_kernel(spot_ref, phase_ref, absorb_ref, *refs):
            side_refs, rim_refs = refs[:ways], refs[ways : 2 * ways]
            out, wide, rim = refs[2 * ways :]
            row, column = spot_ref[0, 0], spot_ref[0, 1]
            values = []
            for plane, ref in enumerate((phase_ref, absorb_ref)):
                wide[:HALO, :] = jnp.zeros((HALO, extent), f32)
                wide[edge:, :] = jnp.zeros((HALO, extent), f32)
                if ways == 1:
                    wide[HALO:edge, :HALO] = jnp.zeros((width, HALO), f32)
                    wide[HALO:edge, edge:] = jnp.zeros((width, HALO), f32)
                    rim[:HALO, :] = jnp.zeros((HALO, frame), f32)
                    rim[edge:, :] = jnp.zeros((HALO, frame), f32)
                rim[HALO:edge, :] = jnp.zeros((width, frame), f32)
                wide[HALO:edge, HALO:edge] = ref[...]
                for way in range(ways):
                    start = place.received(place.column(), way) * edge
                    wide[HALO:edge, pl.ds(pl.multiple_of(start, LANES), HALO)] = side_refs[way][
                        plane
                    ]
                    start = place.received(place.row(), way) * edge
                    rim[pl.ds(pl.multiple_of(start, 8), HALO), :] = rim_refs[way][plane]

                def rows_of(top, tall):
                    cut = cut_columns(
                        lambda start, count: wide[pl.ds(top, tall), pl.ds(start, count)],
                        column,
                        frame,
                    )
                    return cut + rim[pl.ds(top, tall), :]

                values.append(cut_rows(rows_of, row, frame, extent))
            cosine, sine = cos_sin(values[0])
            damping = jnp.exp(-values[1])
            out[0] = damping * cosine
            out[1] = damping * sine

        window = pl.pallas_call(
            window_kernel,
            out_shape=sds((2, frame, frame), f32),
            in_specs=[SMEM] + [VMEM] * (2 + 2 * ways),
            out_specs=VMEM,
            scratch_shapes=[pltpu.VMEM((extent, extent), f32), pltpu.VMEM((extent, frame), f32)],
            name="window",
        )(spot, phase, absorb, *sides, *rims)

        def to_owner(section_of):
            return move(
                window,
                lambda s, y, x, r: (owner_of(x), y, x, r) if s == section_of(x) else None,
            )

        first = to_owner(lambda x: 0)
        other = to_owner(lambda x: 3 - owner_of(x))
        last = to_owner(lambda x: 3)

        def frame_kernel(first_ref, own_ref, other_ref, last_ref, probe, seen, tables, sort, *refs):
            out_first, out_own, out_other, out_last, fields, exits = refs
            own_is_second = place.owner() == 1
            fields[0] = jnp.where(own_is_second, own_ref[...], other_ref[...])
            fields[1] = jnp.where(own_is_second, other_ref[...], own_ref[...])
            objects = [first_ref, fields.at[0], fields.at[1], last_ref]
            re, im = probe[0], probe[1]
            for number, field in enumerate(objects):
                o_re, o_im = field[0], field[1]
                exit_re, exit_im = o_re * re - o_im * im, o_re * im + o_im * re
                exits[number, 0], exits[number, 1] = exit_re, exit_im
                if number < 3:
                    re, im = near_field(tables, exit_re, exit_im)
            re, im = far_field(tables, exit_re, exit_im)
            counted = dot(sort[0], seen[...].astype(f32).astype(bf16)).astype(bf16)
            re, im = likelihood_seed(re, im, dot(counted, sort[1]))
            im = -im
            for number in reversed(range(4)):
                if number == 3:
                    re, im = far_back(tables, re, im)
                else:
                    re, im = near_field(tables, re, im)
                exit_re, exit_im = exits[number, 0], exits[number, 1]
                phase_term = -(re * exit_im + im * exit_re)
                absorb_term = im * exit_im - re * exit_re
                if number == 3:
                    out_last[0], out_last[1] = phase_term, absorb_term
                elif number == 0:
                    out_first[0], out_first[1] = phase_term, absorb_term
                else:
                    if number == 2:
                        kept = (phase_term, absorb_term)
                    else:
                        for plane, term in enumerate((phase_term, absorb_term)):
                            out_own[plane] = jnp.where(own_is_second, term, exits[3, plane])
                            out_other[plane] = jnp.where(own_is_second, exits[3, plane], term)
                    if number == 2:
                        exits[3, 0], exits[3, 1] = kept
                if number > 0:
                    o_re, o_im = objects[number][0], objects[number][1]
                    re, im = o_re * re - o_im * im, o_re * im + o_im * re

        tables, sort = wave_tables(frame)
        terms = pl.pallas_call(
            frame_kernel,
            out_shape=[sds((2, frame, frame), f32)] * 4,
            in_specs=[VMEM] * 8,
            out_specs=[VMEM] * 4,
            scratch_shapes=[
                pltpu.VMEM((2, 2, frame, frame), f32),
                pltpu.VMEM((4, 2, frame, frame), f32),
            ],
            compiler_params=pltpu.CompilerParams(vmem_limit_bytes=48 << 20),
            name="frame",
        )(first, window, other, last, probe_wave, observed, tables, sort)

        def from_owner(value, section_of):
            return move(
                value,
                lambda s, y, x, r: (section_of(x), y, x, r) if s == owner_of(x) else None,
            )

        back_first = from_owner(terms[0], lambda x: 0)
        back_other = from_owner(terms[2], lambda x: 3 - owner_of(x))
        back_last = from_owner(terms[3], lambda x: 3)

        pad = frame

        def parts_kernel(spot_ref, first_ref, own_ref, other_ref, last_ref, *refs):
            keep, give, straight, across, term, padded, sem = refs
            section, rep, owner = place.section(), place.rep(), place.owner()
            choice = jnp.where(
                section == 0, 0, jnp.where(section == 3, 3, jnp.where(section == owner, 1, 2))
            )
            for number, ref in enumerate((first_ref, own_ref, other_ref, last_ref)):

                @pl.when(choice == number)
                def _():
                    copy = pltpu.make_async_copy(ref, term, sem)
                    copy.start()
                    copy.wait()

            row = spot_ref[0, 0]
            zeros = jnp.zeros((2, pad, frame), f32)
            padded[:, :pad] = zeros
            padded[:, pad + frame :] = zeros
            padded[:, pad : pad + frame] = term[...]
            mine = pad + HALO + half_rows * rep - row
            others = pad + HALO + half_rows * (1 - rep) - row
            above = jnp.maximum(pad - row, 0)
            below = jnp.minimum(pad + edge - row, pad + frame + HALO)
            cuts = (
                (keep, mine, half_rows),
                (give, others, half_rows),
                (straight, jnp.where(rep == 1, above, below), HALO),
                (across, jnp.where(rep == 1, below, above), HALO),
            )
            for out, start, height in cuts:
                for plane in range(2):
                    out[plane] = cut_rows(
                        lambda top, tall: padded[plane, pl.ds(top, tall), :],
                        start,
                        height,
                        frame + 2 * pad,
                    )

        keep, give, straight, across = pl.pallas_call(
            parts_kernel,
            out_shape=[sds((2, half_rows, frame), f32)] * 2 + [sds((2, HALO, frame), f32)] * 2,
            in_specs=[SMEM] + [ANY] * 4,
            out_specs=[VMEM] * 4,
            scratch_shapes=[
                pltpu.VMEM((2, frame, frame), f32),
                pltpu.VMEM((2, frame + 2 * pad, frame), f32),
                pltpu.SemaphoreType.DMA,
            ],
            name="parts",
        )(spot, back_first, terms[1], back_other, back_last)

        given = move(give, lambda s, y, x, r: (s, y, x, 1 - r))
        came_straight = move(straight, lambda s, y, x, r: (s, y + 1 - 2 * r, x, r))
        came_across = move(across, lambda s, y, x, r: (s, y - 1 + 2 * r, x, 1 - r))

        def gather_kernel(spot_ref, partner_ref, *refs):
            spot_refs = refs[:ways]
            keep_ref, given_ref, straight_ref, across_ref = refs[ways : ways + 4]
            middle, outs, total = refs[ways + 4], refs[ways + 5 : 2 * ways + 5], refs[-1]
            rep = place.rep()
            total[...] = jnp.zeros(total.shape, f32)
            if ways == 1:
                straight_column, across_column = spot_refs[0][0, 1], partner_ref[1, 1]
            else:
                straight_column = jnp.where(rep == 1, spot_refs[0][0, 1], spot_refs[1][0, 1])
                across_column = jnp.where(rep == 1, partner_ref[1, 1], partner_ref[2, 1])
            low = pl.ds(pl.multiple_of(rep * (half_rows - HALO), 8), HALO)
            every = pl.ds(0, half_rows)
            for plane in range(2):
                put_columns(total, plane, every, keep_ref[plane], spot_ref[0, 1])
                put_columns(total, plane, every, given_ref[plane], partner_ref[0, 1])
                put_columns(total, plane, low, straight_ref[plane], straight_column)
                put_columns(total, plane, low, across_ref[plane], across_column)
            middle[...] = total[:, :, HALO:edge]
            for way in range(ways):
                start = place.sent(place.column(), way) * edge
                outs[way][...] = total[:, :, pl.ds(pl.multiple_of(start, LANES), HALO)]

        middle, *leaving = pl.pallas_call(
            gather_kernel,
            out_shape=[sds((2, half_rows, width), f32)] + [sds((2, half_rows, HALO), f32)] * ways,
            in_specs=[SMEM] * (2 + ways) + [VMEM] * 4,
            out_specs=[VMEM] * (1 + ways),
            scratch_shapes=[pltpu.VMEM((2, half_rows, extent), f32)],
            name="gather_terms",
        )(spot, spots_rep, *spots_rows, keep, given, came_straight, came_across)
        arrived = trade_columns(leaving)

        def finish_kernel(middle_ref, *refs):
            arrived_refs, outs = refs[:ways], refs[ways:]
            for plane in range(2):
                outs[plane][...] = middle_ref[plane]
                for way in range(ways):
                    start = place.received(place.column(), way) * (width - HALO)
                    here = (slice(None), pl.ds(pl.multiple_of(start, LANES), HALO))
                    outs[plane][here] = outs[plane][here] + arrived_refs[way][plane]

        result = pl.pallas_call(
            finish_kernel,
            out_shape=[sds((half_rows, width), f32)] * 2,
            in_specs=[VMEM] * (1 + ways),
            out_specs=[VMEM] * 2,
            name="finish",
        )(middle, *arrived)
        return tuple(plane[None, None] for plane in result)

    in_specs = (
        P("section", "tile", None, None),
        P("section", "tile", None, None),
        P(),
        P("tile", "rep", None, None),
        P("tile", "rep", None, None, None),
    )
    out_specs = (P("section", "tile", "rep", None), P("section", "tile", "rep", None))
    return jax.shard_map(shards, mesh=mesh, in_specs=in_specs, out_specs=out_specs, check_vma=False)
```

```python
import math

import jax
import jax.numpy as jnp
import ml_dtypes
import numpy as np
from jax import lax
from jax.experimental import pallas as pl
from jax.experimental.pallas import tpu as pltpu
from jax.sharding import PartitionSpec as P

HALO = 128
LANES = 128
AXES = ("section", "tile", "rep")

dead_time = 0.1
background = 0.1
loss_weight = 0.1
fresnel = 0.5

f32 = jnp.float32
bf16 = jnp.bfloat16

SMEM = pl.BlockSpec(memory_space=pltpu.SMEM)
VMEM = pl.BlockSpec(memory_space=pltpu.VMEM)
HBM = pl.BlockSpec(memory_space=pltpu.HBM)


def two_parts(matrix):
    high = matrix.astype(ml_dtypes.bfloat16)
    low = (matrix - high.astype(np.float64)).astype(ml_dtypes.bfloat16)
    return np.stack([high, low])


def from_left(matrix):
    return np.block([[matrix.real, -matrix.imag], [matrix.imag, matrix.real]])


def from_right(matrix):
    return np.block([[matrix.real, matrix.imag], [-matrix.imag, matrix.real]])


def wave_tables(length):
    half = length // 2
    indices = np.arange(length)
    shifted = np.where(indices < half, indices, indices - length)
    kernel = np.exp(1j * math.pi * fresnel * shifted.astype(np.float64) ** 2 / length)
    spread = np.fft.ifft(kernel)
    circulant = spread[(indices[:, None] - indices[None, :]) % length]
    first, second = circulant[:half, :half], circulant[:half, half:]
    plus, minus = (first + second) / 2, (first - second) / 2
    near = [from_left(plus), from_left(minus), from_right(plus), from_right(minus)]
    turns = np.outer(indices[:half], indices[:half]) % half
    even = np.exp(-2j * math.pi * turns / half) / math.sqrt(length)
    odd = even * np.exp(-2j * math.pi * indices[:half] / length)[None, :]
    far = [from_left(even), from_left(odd), from_right(even.T), from_right(odd.T)]
    back = [from_left(even.T), from_left(odd.T), from_right(even), from_right(odd)]
    sort = np.zeros((length, length))
    sort[np.arange(half), 2 * np.arange(half)] = 1
    sort[half + np.arange(half), 2 * np.arange(half) + 1] = 1
    tables = np.stack([two_parts(m) for m in near + far + back])
    return tables, np.stack([sort, sort.T]).astype(ml_dtypes.bfloat16)


def fitted(function, degree):
    top = math.pi**2
    fit = np.polynomial.chebyshev.Chebyshev.interpolate(function, degree, domain=[0.0, top])
    return [float(c) for c in fit.convert(kind=np.polynomial.Polynomial).coef]


def sine_ratio(u):
    angle = np.sqrt(np.maximum(u, 1e-12))
    return np.sin(angle) / angle


SINE = fitted(sine_ratio, 8)
COSINE = fitted(lambda u: np.cos(np.sqrt(np.maximum(u, 0.0))), 8)


def polynomial(coefficients, u):
    total = jnp.full_like(u, coefficients[-1])
    for c in coefficients[-2::-1]:
        total = total * u + c
    return total


def cos_sin(angle):
    square = angle * angle
    return polynomial(COSINE, square), angle * polynomial(SINE, square)


def halves(value):
    high = value.astype(bf16)
    return high, (value - high.astype(f32)).astype(bf16)


def dot(a, b):
    return jnp.dot(a, b, preferred_element_type=f32)


def left_by(tables, index, value):
    high, low = halves(value)
    return dot(tables[index, 0], high) + dot(tables[index, 1], high) + dot(tables[index, 0], low)


def right_by(tables, index, value):
    high, low = halves(value)
    return dot(high, tables[index, 0]) + dot(high, tables[index, 1]) + dot(low, tables[index, 0])


def propagate(tables, at, re, im, fold, unfold):
    half = re.shape[0] // 2
    re0, re1, im0, im1 = re[:half], re[half:], im[:half], im[half:]
    if fold:
        re0, re1, im0, im1 = re0 + re1, re0 - re1, im0 + im1, im0 - im1
    first = left_by(tables, at, jnp.concatenate([re0, im0], 0))
    second = left_by(tables, at + 1, jnp.concatenate([re1, im1], 0))
    if unfold:
        first, second = first + second, first - second
    re = jnp.concatenate([first[:half], second[:half]], 0)
    im = jnp.concatenate([first[half:], second[half:]], 0)
    re0, re1, im0, im1 = re[:, :half], re[:, half:], im[:, :half], im[:, half:]
    if fold:
        re0, re1, im0, im1 = re0 + re1, re0 - re1, im0 + im1, im0 - im1
    first = right_by(tables, at + 2, jnp.concatenate([re0, im0], 1))
    second = right_by(tables, at + 3, jnp.concatenate([re1, im1], 1))
    if unfold:
        first, second = first + second, first - second
    re = jnp.concatenate([first[:, :half], second[:, :half]], 1)
    im = jnp.concatenate([first[:, half:], second[:, half:]], 1)
    return re, im


def near_field(tables, re, im):
    return propagate(tables, 0, re, im, True, True)


def far_field(tables, re, im):
    return propagate(tables, 4, re, im, True, False)


def far_back(tables, re, im):
    return propagate(tables, 8, re, im, False, True)


def likelihood_seed(far_re, far_im, observed):
    intensity = far_re * far_re + far_im * far_im
    shifted_total = intensity + background
    denominator = 1.0 + dead_time * shifted_total
    model_rate = shifted_total / denominator
    slope_term = loss_weight * (1.0 - observed / model_rate) / (denominator * denominator)
    return (2.0 * slope_term * far_re, 2.0 * slope_term * far_im)


def in_band(index, offset, band):
    cell = index + (band // 2) * (2 * HALO)
    return (cell >= offset) & (cell < offset + 2 * HALO)


def lane_index(shape):
    return lax.broadcasted_iota(jnp.int32, shape, len(shape) - 1)


def row_index(shape):
    return lax.broadcasted_iota(jnp.int32, shape, len(shape) - 2)


def choose_columns(bands, offset):
    lane = lane_index(bands[1].shape)
    first = jnp.where(
        in_band(lane, offset, 0), bands[0], jnp.where(in_band(lane, offset, 2), bands[2], bands[4])
    )
    second = jnp.where(in_band(lane + HALO, offset, 1), bands[1], bands[3])
    return jnp.concatenate([first, second], 1)


def part_of_band(value, offset, band):
    start = (band % 2) * HALO
    half = value[:, start : start + HALO]
    return jnp.where(in_band(lane_index(half.shape) + start, offset, band), half, 0.0)


class Copies:
    def __init__(self, semaphores):
        self.semaphores = semaphores
        self.count = 0

    def start(self, source, target):
        copy = pltpu.make_async_copy(source, target, self.semaphores.at[self.count])
        self.count += 1
        copy.start()
        return copy


def wait_for(copies):
    for copy in copies:
        copy.wait()


class Place:
    def __init__(self, grid_side):
        self.grid_side = grid_side
        self.ways = 1 if grid_side == 2 else 2

    def section(self):
        return lax.axis_index("section")

    def rep(self):
        return lax.axis_index("rep")

    def row(self):
        return lax.axis_index("tile") // self.grid_side

    def column(self):
        return lax.axis_index("tile") % self.grid_side

    def owner(self):
        return 1 + self.column() % 2

    def sent(self, index, way):
        return 1 - index if self.ways == 1 else way

    def received(self, index, way):
        return 1 - index if self.ways == 1 else 1 - way


def solution(mesh):
    sections, tiles, reps = (mesh.shape[a] for a in AXES)
    grid_side = math.isqrt(tiles)
    place = Place(grid_side)
    ways = place.ways

    def everywhere(target_of):
        pairs = []
        for s in range(sections):
            for t in range(tiles):
                for r in range(reps):
                    target = target_of(s, t // grid_side, t % grid_side, r)
                    if target is None:
                        continue
                    ts, ty, tx, tr = target
                    if not (0 <= ty < grid_side and 0 <= tx < grid_side):
                        continue
                    pairs.append(
                        ((s * tiles + t) * reps + r, (ts * tiles + ty * grid_side + tx) * reps + tr)
                    )
        return pairs

    def move(value, target_of):
        return lax.ppermute(value, AXES, everywhere(target_of))

    def trade_rows(values):
        if ways == 1:
            return [move(values[0], lambda s, y, x, r: (s, 1 - y, x, r))]
        return [
            move(values[0], lambda s, y, x, r: (s, y - 1, x, r)),
            move(values[1], lambda s, y, x, r: (s, y + 1, x, r)),
        ]

    def trade_columns(values):
        if ways == 1:
            return [move(values[0], lambda s, y, x, r: (s, y, 1 - x, r))]
        return [
            move(values[0], lambda s, y, x, r: (s, y, x - 1, r)),
            move(values[1], lambda s, y, x, r: (s, y, x + 1, r)),
        ]

    def owner_of(x):
        return 1 + x % 2

    def shards(phase_shift, absorption, probe_wave, positions, counts):
        width = phase_shift.shape[2]
        frame = probe_wave.shape[1]
        half_rows = width // reps
        phase = phase_shift.reshape(width, width)
        absorb = absorption.reshape(width, width)
        spot = positions.reshape(1, 2)
        observed = counts.reshape(frame, frame)
        sds = jax.ShapeDtypeStruct
        small = pltpu.CompilerParams(vmem_limit_bytes=8 << 20)

        spots_rows = trade_rows([spot] * ways)
        spots_rep = move(
            jnp.concatenate([spot] + spots_rows, 0), lambda s, y, x, r: (s, y, x, 1 - r)
        )

        def edge(value, way):
            start = place.sent(place.column(), way) * (width - HALO)
            return lax.dynamic_slice_in_dim(value, start, HALO, 1)

        sides = [
            side
            for value in (phase, absorb)
            for side in trade_columns([edge(value, way) for way in range(ways)])
        ]

        def rows_of(refs, plane, rows):
            sides_here = [refs[2 + plane * ways + way][rows, :] for way in range(ways)]
            return refs[plane][rows, :], sides_here

        def bands_of(tile, margin):
            inner = [tile[:, i * HALO : (i + 1) * HALO] for i in range(3)]
            ends = []
            for side in range(2):
                if ways == 1:
                    there = place.received(place.column(), 0) == side
                    ends.append(jnp.where(there, margin[0], 0.0))
                else:
                    there = place.column() > 0 if side == 0 else place.column() < grid_side - 1
                    ends.append(jnp.where(there, margin[1 - side], 0.0))
            return [ends[0], *inner, ends[1]]

        def transmission(angle, loss):
            cosine, sine = cos_sin(angle)
            damping = jnp.exp(-loss)
            return damping * cosine, damping * sine

        def strip_kernel(*refs):
            loaded, spot_refs = refs[: 2 + 2 * ways], refs[2 + 2 * ways : 2 + 3 * ways]
            outs = refs[2 + 3 * ways :]
            for way in range(ways):
                below = place.sent(place.row(), way)
                rows = pl.ds(pl.multiple_of(below * (width - HALO), 8), HALO)
                column = spot_refs[way if ways == 1 else 1 - way][0, 1]
                cut = [
                    choose_columns(bands_of(*rows_of(loaded, plane, rows)), column)
                    for plane in range(2)
                ]
                outs[way][0], outs[way][1] = transmission(*cut)

        strips = pl.pallas_call(
            strip_kernel,
            out_shape=[sds((2, HALO, frame), f32)] * ways,
            in_specs=[VMEM] * (2 + 2 * ways) + [SMEM] * ways,
            out_specs=[VMEM] * ways,
            compiler_params=small,
            name="halo_rows",
        )(phase, absorb, *sides, *spots_rows)
        rims = trade_rows(strips)

        def window_kernel(spot_ref, *refs):
            loaded, (whole, part) = refs[:-2], refs[-2:]
            row, column = spot_ref[0, 0], spot_ref[0, 1]
            index = row_index((HALO, HALO))
            upper = in_band(index + HALO, row, 1)
            planes = []
            for plane in range(2):
                first = bands_of(*rows_of(loaded, plane, slice(0, HALO)))
                third = bands_of(*rows_of(loaded, plane, slice(2 * HALO, 3 * HALO)))
                bands = [jnp.where(upper, v, w) for v, w in zip(first, third)]
                planes.append(choose_columns(bands, column))
            whole[0], whole[1] = transmission(*planes)
            planes = []
            for plane in range(2):
                bands = bands_of(*rows_of(loaded, plane, slice(HALO, 2 * HALO)))
                planes.append(choose_columns(bands, column))
            real, imag = transmission(*planes)
            inside = in_band(row_index((HALO, frame)), row, 2)
            part[0], part[1] = jnp.where(inside, real, 1.0), jnp.where(inside, imag, 0.0)

        whole, part = pl.pallas_call(
            window_kernel,
            out_shape=[sds((2, HALO, frame), f32)] * 2,
            in_specs=[SMEM] + [VMEM] * (2 + 2 * ways),
            out_specs=[VMEM] * 2,
            compiler_params=small,
            name="window",
        )(spot, phase, absorb, *sides)

        def to_owner(value):
            return [
                move(
                    value,
                    lambda s, y, x, r: (owner_of(x), y, x, r) if s == section_of(x) else None,
                )
                for section_of in (lambda x: 0, lambda x: 3 - owner_of(x), lambda x: 3)
            ]

        wholes = to_owner(whole)

        def join_kernel(spot_ref, part_ref, *refs):
            rim_refs, out = refs[:ways], refs[ways]
            row = spot_ref[0, 0]
            index = row_index((HALO, frame))
            out[...] = part_ref[...]
            for way in range(ways):
                side = place.received(place.row(), way)
                there = jnp.where(side == 0, place.row() > 0, place.row() < grid_side - 1)
                shifted = index + jnp.where(side == 0, 0, 2 * (2 * HALO))
                near = (shifted >= row) & (shifted < row + jnp.where(there, 2 * HALO, 0))
                for plane in range(2):
                    out[plane] = jnp.where(near, rim_refs[way][plane], out[plane])

        joined = pl.pallas_call(
            join_kernel,
            out_shape=sds((2, HALO, frame), f32),
            in_specs=[SMEM] + [VMEM] * (1 + ways),
            out_specs=VMEM,
            compiler_params=small,
            name="join",
        )(spot, part, *rims)
        joineds = to_owner(joined)

        tables, sort = wave_tables(frame)

        def prepare_kernel(spot_ref, probe, seen, sort, rolled, counted):
            row, column = lax.rem(spot_ref[0, 0], frame), lax.rem(spot_ref[0, 1], frame)
            for plane in range(2):
                rolled[plane] = pltpu.roll(pltpu.roll(probe[plane], row, 0), column, 1)
            first = dot(sort[0], seen[...].astype(f32).astype(bf16)).astype(bf16)
            counted[...] = dot(first, sort[1])

        rolled, counted = pl.pallas_call(
            prepare_kernel,
            out_shape=[sds((2, frame, frame), f32), sds((frame, frame), f32)],
            in_specs=[SMEM] + [VMEM] * 3,
            out_specs=[VMEM] * 2,
            compiler_params=small,
            name="prepare",
        )(spot, probe_wave, observed, sort)

        def frame_kernel(probe, seen, tables, *refs):
            whole_refs, joined_refs, outs = refs[:4], refs[4:8], refs[8:12]
            fields, exits = refs[12:]
            own_is_second = place.owner() == 1
            for half, parts in ((slice(HALO, None), whole_refs), (slice(None, HALO), joined_refs)):
                for plane in range(2):
                    own, other = parts[1][plane], parts[2][plane]
                    fields[0, plane, half] = parts[0][plane]
                    fields[1, plane, half] = jnp.where(own_is_second, own, other)
                    fields[2, plane, half] = jnp.where(own_is_second, other, own)
                    fields[3, plane, half] = parts[3][plane]
            re, im = probe[0], probe[1]
            for number in range(4):
                o_re, o_im = fields[number, 0], fields[number, 1]
                exit_re, exit_im = o_re * re - o_im * im, o_re * im + o_im * re
                exits[number, 0], exits[number, 1] = exit_re, exit_im
                if number < 3:
                    re, im = near_field(tables, exit_re, exit_im)
            re, im = far_field(tables, exit_re, exit_im)
            re, im = likelihood_seed(re, im, seen[...])
            im = -im
            for number in reversed(range(4)):
                if number == 3:
                    re, im = far_back(tables, re, im)
                else:
                    re, im = near_field(tables, re, im)
                exit_re, exit_im = exits[number, 0], exits[number, 1]
                phase_term = -(re * exit_im + im * exit_re)
                absorb_term = im * exit_im - re * exit_re
                if number > 0:
                    o_re, o_im = fields[number, 0], fields[number, 1]
                    re, im = o_re * re - o_im * im, o_re * im + o_im * re
                if number in (0, 3):
                    outs[number][0], outs[number][1] = phase_term, absorb_term
                elif number == 2:
                    exits[2, 0], exits[2, 1] = phase_term, absorb_term
                else:
                    for plane, term in enumerate((phase_term, absorb_term)):
                        kept_term = exits[2, plane]
                        outs[1][plane] = jnp.where(own_is_second, term, kept_term)
                        outs[2][plane] = jnp.where(own_is_second, kept_term, term)

        terms = pl.pallas_call(
            frame_kernel,
            out_shape=[sds((2, frame, frame), f32)] * 4,
            in_specs=[VMEM] * 11,
            out_specs=[VMEM] * 4,
            scratch_shapes=[
                pltpu.VMEM((4, 2, frame, frame), f32),
                pltpu.VMEM((4, 2, frame, frame), f32),
            ],
            compiler_params=pltpu.CompilerParams(vmem_limit_bytes=16 << 20),
            name="frame",
        )(
            rolled, counted, tables,
            wholes[0], whole, wholes[1], wholes[2],
            joineds[0], joined, joineds[1], joineds[2],
        )

        def from_owner(value, section_of):
            return move(
                value,
                lambda s, y, x, r: (section_of(x), y, x, r) if s == owner_of(x) else None,
            )

        back = (
            from_owner(terms[0], lambda x: 0),
            terms[1],
            from_owner(terms[2], lambda x: 3 - owner_of(x)),
            from_owner(terms[3], lambda x: 3),
        )

        def load_term(refs, term):
            section, owner = place.section(), place.owner()
            choice = jnp.where(
                section == 0, 0, jnp.where(section == 3, 3, jnp.where(section == owner, 1, 2))
            )
            for number, ref in enumerate(refs):

                @pl.when(choice == number)
                def _():
                    term[...] = ref[...]

        def rows_for(term, plane, row, rep):
            index = row_index((frame, frame))
            middle = jnp.where(in_band(index, row, 2), term[plane], 0.0)
            later = middle[HALO // 2 :]
            earlier = jnp.where(in_band(index, row, 0), term[plane], 0.0)
            earlier = jnp.concatenate([earlier[HALO:], middle[: HALO // 2]], 0)
            return jnp.where(rep == 0, earlier, later)

        def parts_kernel(spot_ref, *refs):
            back_refs, (give, straight, across, term) = refs[:4], refs[4:]
            load_term(back_refs, term)
            rep, row = place.rep(), spot_ref[0, 0]
            index = row_index((HALO, frame))
            for plane in range(2):
                give[plane] = rows_for(term, plane, row, 1 - rep)
                first = term[plane, :HALO]
                above = jnp.where(in_band(index, row, 0), first, 0.0)
                below = jnp.where(in_band(index, row, 4), first, 0.0)
                straight[plane] = jnp.where(rep == 1, above, below)
                across[plane] = jnp.where(rep == 1, below, above)

        give, straight, across = pl.pallas_call(
            parts_kernel,
            out_shape=[sds((2, half_rows, frame), f32)] + [sds((2, HALO, frame), f32)] * 2,
            in_specs=[SMEM] + [VMEM] * 4,
            out_specs=[VMEM] * 3,
            scratch_shapes=[pltpu.VMEM((2, frame, frame), f32)],
            compiler_params=small,
            name="parts",
        )(spot, *back)

        given = move(give, lambda s, y, x, r: (s, y, x, 1 - r))
        came_straight = move(straight, lambda s, y, x, r: (s, y + 1 - 2 * r, x, r))
        came_across = move(across, lambda s, y, x, r: (s, y - 1 + 2 * r, x, 1 - r))

        def keep_kernel(spot_ref, *refs):
            back_refs, (mine, term) = refs[:4], refs[4:]
            load_term(back_refs, term)
            for plane in range(2):
                mine[plane] = rows_for(term, plane, spot_ref[0, 0], place.rep())

        kept = pl.pallas_call(
            keep_kernel,
            out_shape=sds((2, half_rows, frame), f32),
            in_specs=[SMEM] + [VMEM] * 4,
            out_specs=VMEM,
            scratch_shapes=[pltpu.VMEM((2, frame, frame), f32)],
            compiler_params=small,
            cost_estimate=pl.CostEstimate(flops=1 << 22, bytes_accessed=1 << 21, transcendentals=0),
            name="keep",
        )(spot, *back)

        def add_band(band, plane, refs):
            spot_ref, partner_ref, kept_ref, *spot_refs = refs[: 3 + ways]
            given, straight, across = refs[3 + ways : count]
            rep = place.rep()
            if ways == 1:
                straight_column, across_column = spot_refs[0][0, 1], partner_ref[1, 1]
            else:
                straight_column = jnp.where(rep == 1, spot_refs[0][0, 1], spot_refs[1][0, 1])
                across_column = jnp.where(rep == 1, partner_ref[1, 1], partner_ref[2, 1])
            total = part_of_band(kept_ref[plane], spot_ref[0, 1], band)
            total += part_of_band(given[plane], partner_ref[0, 1], band)
            strip = part_of_band(straight[plane], straight_column, band)
            strip += part_of_band(across[plane], across_column, band)
            gap = jnp.zeros((half_rows - HALO, HALO), f32)
            early, late = jnp.concatenate([strip, gap], 0), jnp.concatenate([gap, strip], 0)
            return total + jnp.where(rep == 1, late, early)

        pieces = (spot, spots_rep, kept, *spots_rows, given, came_straight, came_across)
        piece_specs = [SMEM, SMEM, VMEM] + [SMEM] * ways + [VMEM] * 3
        count = len(piece_specs)

        def edge_kernel(*refs):
            for way in range(ways):
                for plane in range(2):
                    if ways == 1:
                        value = jnp.where(
                            place.column() == 0,
                            add_band(4, plane, refs),
                            add_band(0, plane, refs),
                        )
                    else:
                        value = add_band(4 * way, plane, refs)
                    refs[count + way][plane] = value

        leaving = pl.pallas_call(
            edge_kernel,
            out_shape=[sds((2, half_rows, HALO), f32)] * ways,
            in_specs=piece_specs,
            out_specs=[VMEM] * ways,
            compiler_params=small,
            name="edge_terms",
        )(*pieces)
        arrived = trade_columns(leaving)

        def inner_kernel(*refs):
            outs, inner, total, semaphores = refs[count : count + 2], *refs[count + 2 :]
            copies = Copies(semaphores)
            started = []
            for plane in range(2):
                bands = [add_band(band, plane, refs) for band in (1, 2, 3)]
                for number, value in enumerate(bands):
                    total[plane, :, number * HALO : (number + 1) * HALO] = value
                started.append(copies.start(total.at[plane], outs[plane]))
                for way in range(ways):
                    first = place.received(place.column(), way) == 0
                    inner[way, plane] = jnp.where(first, bands[0], bands[2])
            wait_for(started)

        *results, inner = pl.pallas_call(
            inner_kernel,
            out_shape=[sds((half_rows, width), f32)] * 2
            + [sds((ways, 2, half_rows, HALO), f32)],
            in_specs=piece_specs,
            out_specs=[HBM] * 2 + [VMEM],
            scratch_shapes=[
                pltpu.VMEM((2, half_rows, width), f32),
                pltpu.SemaphoreType.DMA((2,)),
            ],
            compiler_params=small,
            cost_estimate=pl.CostEstimate(flops=1 << 22, bytes_accessed=1 << 21, transcendentals=0),
            name="inner_terms",
        )(*pieces)

        def finish_kernel(phase_in, absorb_in, inner_ref, *refs):
            arrived_refs, outs = refs[:ways], refs[ways : ways + 2]
            strips, semaphores = refs[ways + 2 :]
            copies = Copies(semaphores)
            leaving = []
            for way in range(ways):
                start = place.received(place.column(), way) * (width - HALO)
                for plane in range(2):
                    strips[way, plane] = arrived_refs[way][plane] + inner_ref[way, plane]
                    target = outs[plane].at[:, pl.ds(pl.multiple_of(start, LANES), HALO)]
                    leaving.append(copies.start(strips.at[way, plane], target))
            wait_for(leaving)

        result = pl.pallas_call(
            finish_kernel,
            out_shape=[sds((half_rows, width), f32)] * 2,
            in_specs=[HBM, HBM, VMEM] + [VMEM] * ways,
            out_specs=[HBM] * 2,
            scratch_shapes=[
                pltpu.VMEM((ways, 2, half_rows, HALO), f32),
                pltpu.SemaphoreType.DMA((2 * ways,)),
            ],
            input_output_aliases={0: 0, 1: 1},
            compiler_params=small,
            name="finish",
        )(*results, inner, *arrived)
        return tuple(plane[None, None] for plane in result)

    in_specs = (
        P("section", "tile", None, None),
        P("section", "tile", None, None),
        P(),
        P("tile", "rep", None, None),
        P("tile", "rep", None, None, None),
    )
    out_specs = (P("section", "tile", "rep", None), P("section", "tile", "rep", None))
    return jax.shard_map(shards, mesh=mesh, in_specs=in_specs, out_specs=out_specs, check_vma=False)
```

```python
import math

import jax
import jax.numpy as jnp
import ml_dtypes
import numpy as np
from jax import lax
from jax.experimental import pallas as pl
from jax.experimental.pallas import tpu as pltpu
from jax.sharding import PartitionSpec as P

HALO = 128
LANES = 128
AXES = ("section", "tile", "rep")

dead_time = 0.1
background = 0.1
loss_weight = 0.1
fresnel = 0.5

f32 = jnp.float32
bf16 = jnp.bfloat16

SMEM = pl.BlockSpec(memory_space=pltpu.SMEM)
VMEM = pl.BlockSpec(memory_space=pltpu.VMEM)
HBM = pl.BlockSpec(memory_space=pltpu.HBM)


def two_parts(matrix):
    high = matrix.astype(ml_dtypes.bfloat16)
    low = (matrix - high.astype(np.float64)).astype(ml_dtypes.bfloat16)
    return np.stack([high, low])


def from_left(matrix):
    return np.block([[matrix.real, -matrix.imag], [matrix.imag, matrix.real]])


def from_right(matrix):
    return np.block([[matrix.real, matrix.imag], [-matrix.imag, matrix.real]])


def wave_tables(length):
    half = length // 2
    indices = np.arange(length)
    shifted = np.where(indices < half, indices, indices - length)
    kernel = np.exp(1j * math.pi * fresnel * shifted.astype(np.float64) ** 2 / length)
    spread = np.fft.ifft(kernel)
    circulant = spread[(indices[:, None] - indices[None, :]) % length]
    first, second = circulant[:half, :half], circulant[:half, half:]
    plus, minus = (first + second) / 2, (first - second) / 2
    near = [from_left(plus), from_left(minus), from_right(plus), from_right(minus)]
    turns = np.outer(indices[:half], indices[:half]) % half
    even = np.exp(-2j * math.pi * turns / half) / math.sqrt(length)
    odd = even * np.exp(-2j * math.pi * indices[:half] / length)[None, :]
    far = [from_left(even), from_left(odd), from_right(even.T), from_right(odd.T)]
    back = [from_left(even.T), from_left(odd.T), from_right(even), from_right(odd)]
    sort = np.zeros((length, length))
    sort[np.arange(half), 2 * np.arange(half)] = 1
    sort[half + np.arange(half), 2 * np.arange(half) + 1] = 1
    tables = np.stack([two_parts(m) for m in near + far + back])
    return tables, np.stack([sort, sort.T]).astype(ml_dtypes.bfloat16)


def fitted(function, degree):
    top = math.pi**2
    fit = np.polynomial.chebyshev.Chebyshev.interpolate(function, degree, domain=[0.0, top])
    return [float(c) for c in fit.convert(kind=np.polynomial.Polynomial).coef]


def sine_ratio(u):
    angle = np.sqrt(np.maximum(u, 1e-12))
    return np.sin(angle) / angle


SINE = fitted(sine_ratio, 8)
COSINE = fitted(lambda u: np.cos(np.sqrt(np.maximum(u, 0.0))), 8)


def polynomial(coefficients, u):
    total = jnp.full_like(u, coefficients[-1])
    for c in coefficients[-2::-1]:
        total = total * u + c
    return total


def cos_sin(angle):
    square = angle * angle
    return polynomial(COSINE, square), angle * polynomial(SINE, square)


def halves(value):
    high = value.astype(bf16)
    return high, (value - high.astype(f32)).astype(bf16)


def dot(a, b):
    return jnp.dot(a, b, preferred_element_type=f32)


def left_by(tables, index, value):
    high, low = halves(value)
    return dot(tables[index, 0], high) + dot(tables[index, 1], high) + dot(tables[index, 0], low)


def right_by(tables, index, value):
    high, low = halves(value)
    return dot(high, tables[index, 0]) + dot(high, tables[index, 1]) + dot(low, tables[index, 0])


def propagate(tables, at, re, im, fold, unfold):
    half = re.shape[0] // 2
    re0, re1, im0, im1 = re[:half], re[half:], im[:half], im[half:]
    if fold:
        re0, re1, im0, im1 = re0 + re1, re0 - re1, im0 + im1, im0 - im1
    first = left_by(tables, at, jnp.concatenate([re0, im0], 0))
    second = left_by(tables, at + 1, jnp.concatenate([re1, im1], 0))
    if unfold:
        first, second = first + second, first - second
    re = jnp.concatenate([first[:half], second[:half]], 0)
    im = jnp.concatenate([first[half:], second[half:]], 0)
    re0, re1, im0, im1 = re[:, :half], re[:, half:], im[:, :half], im[:, half:]
    if fold:
        re0, re1, im0, im1 = re0 + re1, re0 - re1, im0 + im1, im0 - im1
    first = right_by(tables, at + 2, jnp.concatenate([re0, im0], 1))
    second = right_by(tables, at + 3, jnp.concatenate([re1, im1], 1))
    if unfold:
        first, second = first + second, first - second
    re = jnp.concatenate([first[:, :half], second[:, :half]], 1)
    im = jnp.concatenate([first[:, half:], second[:, half:]], 1)
    return re, im


def near_field(tables, re, im):
    return propagate(tables, 0, re, im, True, True)


def far_field(tables, re, im):
    return propagate(tables, 4, re, im, True, False)


def far_back(tables, re, im):
    return propagate(tables, 8, re, im, False, True)


def likelihood_seed(far_re, far_im, observed):
    intensity = far_re * far_re + far_im * far_im
    shifted_total = intensity + background
    denominator = 1.0 + dead_time * shifted_total
    model_rate = shifted_total / denominator
    slope_term = loss_weight * (1.0 - observed / model_rate) / (denominator * denominator)
    return (2.0 * slope_term * far_re, 2.0 * slope_term * far_im)


def in_band(index, offset, band):
    cell = index + (band // 2) * (2 * HALO)
    return (cell >= offset) & (cell < offset + 2 * HALO)


def lane_index(shape):
    return lax.broadcasted_iota(jnp.int32, shape, len(shape) - 1)


def row_index(shape):
    return lax.broadcasted_iota(jnp.int32, shape, len(shape) - 2)


def choose_columns(bands, offset):
    lane = lane_index(bands[1].shape)
    first = jnp.where(
        in_band(lane, offset, 0), bands[0], jnp.where(in_band(lane, offset, 2), bands[2], bands[4])
    )
    second = jnp.where(in_band(lane + HALO, offset, 1), bands[1], bands[3])
    return jnp.concatenate([first, second], 1)


def part_of_band(value, offset, band):
    start = (band % 2) * HALO
    half = value[:, start : start + HALO]
    return jnp.where(in_band(lane_index(half.shape) + start, offset, band), half, 0.0)


class Copies:
    def __init__(self, semaphores):
        self.semaphores = semaphores
        self.count = 0

    def start(self, source, target):
        copy = pltpu.make_async_copy(source, target, self.semaphores.at[self.count])
        self.count += 1
        copy.start()
        return copy


def wait_for(copies):
    for copy in copies:
        copy.wait()


class Place:
    def __init__(self, grid_side):
        self.grid_side = grid_side
        self.ways = 1 if grid_side == 2 else 2

    def section(self):
        return lax.axis_index("section")

    def rep(self):
        return lax.axis_index("rep")

    def row(self):
        return lax.axis_index("tile") // self.grid_side

    def column(self):
        return lax.axis_index("tile") % self.grid_side

    def owner(self):
        return 1 + self.column() % 2

    def sent(self, index, way):
        return 1 - index if self.ways == 1 else way

    def received(self, index, way):
        return 1 - index if self.ways == 1 else 1 - way


def solution(mesh):
    sections, tiles, reps = (mesh.shape[a] for a in AXES)
    grid_side = math.isqrt(tiles)
    place = Place(grid_side)
    ways = place.ways

    def everywhere(target_of):
        pairs = []
        for s in range(sections):
            for t in range(tiles):
                for r in range(reps):
                    target = target_of(s, t // grid_side, t % grid_side, r)
                    if target is None:
                        continue
                    ts, ty, tx, tr = target
                    if not (0 <= ty < grid_side and 0 <= tx < grid_side):
                        continue
                    pairs.append(
                        ((s * tiles + t) * reps + r, (ts * tiles + ty * grid_side + tx) * reps + tr)
                    )
        return pairs

    def move(value, target_of):
        return lax.ppermute(value, AXES, everywhere(target_of))

    def trade_rows(values):
        if ways == 1:
            return [move(values[0], lambda s, y, x, r: (s, 1 - y, x, r))]
        return [
            move(values[0], lambda s, y, x, r: (s, y - 1, x, r)),
            move(values[1], lambda s, y, x, r: (s, y + 1, x, r)),
        ]

    def trade_columns(values):
        if ways == 1:
            return [move(values[0], lambda s, y, x, r: (s, y, 1 - x, r))]
        return [
            move(values[0], lambda s, y, x, r: (s, y, x - 1, r)),
            move(values[1], lambda s, y, x, r: (s, y, x + 1, r)),
        ]

    def owner_of(x):
        return 1 + x % 2

    def near_of(x):
        return 3 * (x % 2)

    def middle_of(x):
        return 3 - owner_of(x)

    def far_of(x):
        return 3 - near_of(x)

    def shards(phase_shift, absorption, probe_wave, positions, counts):
        width = phase_shift.shape[2]
        frame = probe_wave.shape[1]
        half_rows = width // reps
        phase = phase_shift.reshape(width, width)
        absorb = absorption.reshape(width, width)
        spot = positions.reshape(1, 2)
        observed = counts.reshape(frame, frame)
        sds = jax.ShapeDtypeStruct
        small = pltpu.CompilerParams(vmem_limit_bytes=8 << 20)

        spots_rows = trade_rows([spot] * ways)
        def load_kernel(phase_ref, absorb_ref, tile, *refs):
            edges, copies = refs[:ways], Copies(refs[ways])
            wait_for([copies.start(phase_ref, tile.at[0]), copies.start(absorb_ref, tile.at[1])])
            for way in range(ways):
                start = place.sent(place.column(), way) * (width - HALO)
                edges[way][...] = tile[:, :, pl.ds(pl.multiple_of(start, LANES), HALO)]

        tile, *edges = pl.pallas_call(
            load_kernel,
            out_shape=[sds((2, width, width), f32)] + [sds((2, width, HALO), f32)] * ways,
            in_specs=[HBM] * 2,
            out_specs=[VMEM] * (1 + ways),
            scratch_shapes=[pltpu.SemaphoreType.DMA((2,))],
            compiler_params=small,
            name="load",
        )(phase, absorb)
        sides = trade_columns(edges)

        def rows_of(refs, plane, rows):
            return refs[0][plane, rows, :], [side[plane, rows, :] for side in refs[1:]]

        def bands_of(tile, margin):
            inner = [tile[:, i * HALO : (i + 1) * HALO] for i in range(3)]
            ends = []
            for side in range(2):
                if ways == 1:
                    there = place.received(place.column(), 0) == side
                    ends.append(jnp.where(there, margin[0], 0.0))
                else:
                    there = place.column() > 0 if side == 0 else place.column() < grid_side - 1
                    ends.append(jnp.where(there, margin[1 - side], 0.0))
            return [ends[0], *inner, ends[1]]

        def transmission(angle, loss):
            cosine, sine = cos_sin(angle)
            damping = jnp.exp(-loss)
            return damping * cosine, damping * sine

        def strip_kernel(*refs):
            loaded, spot_refs = refs[: 1 + ways], refs[1 + ways : 1 + 2 * ways]
            outs = refs[1 + 2 * ways :]
            for way in range(ways):
                below = place.sent(place.row(), way)
                rows = pl.ds(pl.multiple_of(below * (width - HALO), 8), HALO)
                column = spot_refs[way if ways == 1 else 1 - way][0, 1]
                cut = [
                    choose_columns(bands_of(*rows_of(loaded, plane, rows)), column)
                    for plane in range(2)
                ]
                outs[way][0], outs[way][1] = transmission(*cut)

        strips = pl.pallas_call(
            strip_kernel,
            out_shape=[sds((2, HALO, frame), f32)] * ways,
            in_specs=[VMEM] * (1 + ways) + [SMEM] * ways,
            out_specs=[VMEM] * ways,
            compiler_params=small,
            name="halo_rows",
        )(tile, *sides, *spots_rows)
        rims = trade_rows(strips)

        def window_kernel(spot_ref, *refs):
            loaded, (whole, part) = refs[:-2], refs[-2:]
            row, column = spot_ref[0, 0], spot_ref[0, 1]
            index = row_index((HALO, HALO))
            upper = in_band(index + HALO, row, 1)
            planes = []
            for plane in range(2):
                first = bands_of(*rows_of(loaded, plane, slice(0, HALO)))
                third = bands_of(*rows_of(loaded, plane, slice(2 * HALO, 3 * HALO)))
                bands = [jnp.where(upper, v, w) for v, w in zip(first, third)]
                planes.append(choose_columns(bands, column))
            whole[0], whole[1] = transmission(*planes)
            planes = []
            for plane in range(2):
                bands = bands_of(*rows_of(loaded, plane, slice(HALO, 2 * HALO)))
                planes.append(choose_columns(bands, column))
            real, imag = transmission(*planes)
            inside = in_band(row_index((HALO, frame)), row, 2)
            part[0], part[1] = jnp.where(inside, real, 1.0), jnp.where(inside, imag, 0.0)

        whole, part = pl.pallas_call(
            window_kernel,
            out_shape=[sds((2, HALO, frame), f32)] * 2,
            in_specs=[SMEM] + [VMEM] * (1 + ways),
            out_specs=[VMEM] * 2,
            compiler_params=small,
            name="window",
        )(spot, tile, *sides)

        def to_owner(value):
            return [
                move(
                    value,
                    lambda s, y, x, r: (owner_of(x), y, x, r) if s == section_of(x) else None,
                )
                for section_of in (near_of, middle_of, far_of)
            ]

        wholes = to_owner(whole)

        def join_kernel(spot_ref, part_ref, *refs):
            rim_refs, out = refs[:ways], refs[ways]
            row = spot_ref[0, 0]
            index = row_index((HALO, frame))
            out[...] = part_ref[...]
            for way in range(ways):
                side = place.received(place.row(), way)
                there = jnp.where(side == 0, place.row() > 0, place.row() < grid_side - 1)
                shifted = index + jnp.where(side == 0, 0, 2 * (2 * HALO))
                near = (shifted >= row) & (shifted < row + jnp.where(there, 2 * HALO, 0))
                for plane in range(2):
                    out[plane] = jnp.where(near, rim_refs[way][plane], out[plane])

        joined = pl.pallas_call(
            join_kernel,
            out_shape=sds((2, HALO, frame), f32),
            in_specs=[SMEM] + [VMEM] * (1 + ways),
            out_specs=VMEM,
            compiler_params=small,
            name="join",
        )(spot, part, *rims)
        joineds = to_owner(joined)

        tables, sort = wave_tables(frame)

        def prepare_kernel(spot_ref, probe, seen, sort, rolled, counted):
            row, column = lax.rem(spot_ref[0, 0], frame), lax.rem(spot_ref[0, 1], frame)
            for plane in range(2):
                rolled[plane] = pltpu.roll(pltpu.roll(probe[plane], row, 0), column, 1)
            first = dot(sort[0], seen[...].astype(f32).astype(bf16)).astype(bf16)
            counted[...] = dot(first, sort[1])

        rolled, counted = pl.pallas_call(
            prepare_kernel,
            out_shape=[sds((2, frame, frame), f32), sds((frame, frame), f32)],
            in_specs=[SMEM] + [VMEM] * 3,
            out_specs=[VMEM] * 2,
            compiler_params=small,
            name="prepare",
        )(spot, probe_wave, observed, sort)
        places, counted = lax.optimization_barrier(
            (jnp.concatenate([spot] + spots_rows, 0), counted)
        )
        spots_rep = move(places, lambda s, y, x, r: (s, y, x, 1 - r))

        def frame_kernel(probe, seen, tables, *refs):
            whole_refs, joined_refs, outs = refs[:4], refs[4:8], refs[8:12]
            fields, exits = refs[12:]
            own_is_second = place.owner() == 1
            for half, parts in ((slice(HALO, None), whole_refs), (slice(None, HALO), joined_refs)):
                for plane in range(2):
                    near, own, middle, far = (part[plane] for part in parts)
                    fields[0, plane, half] = jnp.where(own_is_second, near, far)
                    fields[1, plane, half] = jnp.where(own_is_second, own, middle)
                    fields[2, plane, half] = jnp.where(own_is_second, middle, own)
                    fields[3, plane, half] = jnp.where(own_is_second, far, near)
            re, im = probe[0], probe[1]
            for number in range(4):
                o_re, o_im = fields[number, 0], fields[number, 1]
                exit_re, exit_im = o_re * re - o_im * im, o_re * im + o_im * re
                exits[number, 0], exits[number, 1] = exit_re, exit_im
                if number < 3:
                    re, im = near_field(tables, exit_re, exit_im)
            re, im = far_field(tables, exit_re, exit_im)
            re, im = likelihood_seed(re, im, seen[...])
            im = -im
            for number in reversed(range(4)):
                if number == 3:
                    re, im = far_back(tables, re, im)
                else:
                    re, im = near_field(tables, re, im)
                exit_re, exit_im = exits[number, 0], exits[number, 1]
                phase_term = -(re * exit_im + im * exit_re)
                absorb_term = im * exit_im - re * exit_re
                if number > 0:
                    o_re, o_im = fields[number, 0], fields[number, 1]
                    re, im = o_re * re - o_im * im, o_re * im + o_im * re
                exits[number, 0], exits[number, 1] = phase_term, absorb_term
            for plane in range(2):
                one, two, three, four = (exits[number, plane] for number in range(4))
                outs[0][plane] = jnp.where(own_is_second, one, four)
                outs[1][plane] = jnp.where(own_is_second, two, three)
                outs[2][plane] = jnp.where(own_is_second, three, two)
                outs[3][plane] = jnp.where(own_is_second, four, one)

        terms = pl.pallas_call(
            frame_kernel,
            out_shape=[sds((2, frame, frame), f32)] * 4,
            in_specs=[VMEM] * 11,
            out_specs=[VMEM] * 4,
            scratch_shapes=[
                pltpu.VMEM((4, 2, frame, frame), f32),
                pltpu.VMEM((4, 2, frame, frame), f32),
            ],
            compiler_params=pltpu.CompilerParams(vmem_limit_bytes=16 << 20),
            name="frame",
        )(
            rolled, counted, tables,
            wholes[0], whole, wholes[1], wholes[2],
            joineds[0], joined, joineds[1], joineds[2],
        )

        def from_owner(value, section_of):
            return move(
                value,
                lambda s, y, x, r: (section_of(x), y, x, r) if s == owner_of(x) else None,
            )

        far_terms = from_owner(terms[3], far_of)
        back = (
            far_terms,
            from_owner(terms[0], near_of),
            from_owner(terms[2], middle_of),
            terms[1],
        )

        def load_term(refs, term):
            section, owner = place.section(), place.owner()
            near = 3 * (owner - 1)
            choice = jnp.where(
                section == 3 - near, 0, jnp.where(section == near, 1, jnp.where(section == owner, 3, 2))
            )
            for number, ref in enumerate(refs):

                @pl.when(choice == number)
                def _():
                    term[...] = ref[...]

        def rows_for(term, plane, row, rep):
            index = row_index((frame, frame))
            middle = jnp.where(in_band(index, row, 2), term[plane], 0.0)
            later = middle[HALO // 2 :]
            earlier = jnp.where(in_band(index, row, 0), term[plane], 0.0)
            earlier = jnp.concatenate([earlier[HALO:], middle[: HALO // 2]], 0)
            return jnp.where(rep == 0, earlier, later)

        def parts_kernel(spot_ref, *refs):
            back_refs, (give, straight, across, term) = refs[:4], refs[4:]
            load_term(back_refs, term)
            rep, row = place.rep(), spot_ref[0, 0]
            index = row_index((HALO, frame))
            for plane in range(2):
                give[plane] = rows_for(term, plane, row, 1 - rep)
                first = term[plane, :HALO]
                above = jnp.where(in_band(index, row, 0), first, 0.0)
                below = jnp.where(in_band(index, row, 4), first, 0.0)
                straight[plane] = jnp.where(rep == 1, above, below)
                across[plane] = jnp.where(rep == 1, below, above)

        give, straight, across = pl.pallas_call(
            parts_kernel,
            out_shape=[sds((2, half_rows, frame), f32)] + [sds((2, HALO, frame), f32)] * 2,
            in_specs=[SMEM] + [VMEM] * 4,
            out_specs=[VMEM] * 3,
            scratch_shapes=[pltpu.VMEM((2, frame, frame), f32)],
            compiler_params=small,
            name="parts",
        )(spot, *back)

        given = move(give, lambda s, y, x, r: (s, y, x, 1 - r))
        came_straight = move(straight, lambda s, y, x, r: (s, y + 1 - 2 * r, x, r))
        came_across = move(across, lambda s, y, x, r: (s, y - 1 + 2 * r, x, 1 - r))

        def keep_kernel(spot_ref, *refs):
            back_refs, (mine, term) = refs[:4], refs[4:]
            load_term(back_refs, term)
            for plane in range(2):
                mine[plane] = rows_for(term, plane, spot_ref[0, 0], place.rep())

        kept = pl.pallas_call(
            keep_kernel,
            out_shape=sds((2, half_rows, frame), f32),
            in_specs=[SMEM] + [VMEM] * 4,
            out_specs=VMEM,
            scratch_shapes=[pltpu.VMEM((2, frame, frame), f32)],
            compiler_params=small,
            cost_estimate=pl.CostEstimate(flops=1 << 22, bytes_accessed=1 << 21, transcendentals=0),
            name="keep",
        )(spot, *back)

        def add_band(band, plane, refs):
            spot_ref, partner_ref, kept_ref, *spot_refs = refs[: 3 + ways]
            given, straight, across = refs[3 + ways : count]
            rep = place.rep()
            if ways == 1:
                straight_column, across_column = spot_refs[0][0, 1], partner_ref[1, 1]
            else:
                straight_column = jnp.where(rep == 1, spot_refs[0][0, 1], spot_refs[1][0, 1])
                across_column = jnp.where(rep == 1, partner_ref[1, 1], partner_ref[2, 1])
            total = part_of_band(kept_ref[plane], spot_ref[0, 1], band)
            total += part_of_band(given[plane], partner_ref[0, 1], band)
            strip = part_of_band(straight[plane], straight_column, band)
            strip += part_of_band(across[plane], across_column, band)
            gap = jnp.zeros((half_rows - HALO, HALO), f32)
            early, late = jnp.concatenate([strip, gap], 0), jnp.concatenate([gap, strip], 0)
            return total + jnp.where(rep == 1, late, early)

        pieces = (spot, spots_rep, kept, *spots_rows, given, came_straight, came_across)
        piece_specs = [SMEM, SMEM, VMEM] + [SMEM] * ways + [VMEM] * 3
        count = len(piece_specs)

        def edge_kernel(*refs):
            for way in range(ways):
                for plane in range(2):
                    if ways == 1:
                        value = jnp.where(
                            place.column() == 0,
                            add_band(4, plane, refs),
                            add_band(0, plane, refs),
                        )
                    else:
                        value = add_band(4 * way, plane, refs)
                    refs[count + way][plane] = value

        leaving = pl.pallas_call(
            edge_kernel,
            out_shape=[sds((2, half_rows, HALO), f32)] * ways,
            in_specs=piece_specs,
            out_specs=[VMEM] * ways,
            compiler_params=small,
            name="edge_terms",
        )(*pieces)
        arrived = trade_columns(leaving)

        def inner_kernel(*refs):
            outs, inner, total, semaphores = refs[count : count + 2], *refs[count + 2 :]
            copies = Copies(semaphores)
            started = []
            for plane in range(2):
                bands = [add_band(band, plane, refs) for band in (1, 2, 3)]
                for number, value in enumerate(bands):
                    total[plane, :, number * HALO : (number + 1) * HALO] = value
                started.append(copies.start(total.at[plane], outs[plane]))
                for way in range(ways):
                    first = place.received(place.column(), way) == 0
                    inner[way, plane] = jnp.where(first, bands[0], bands[2])
            wait_for(started)

        *results, inner = pl.pallas_call(
            inner_kernel,
            out_shape=[sds((half_rows, width), f32)] * 2
            + [sds((ways, 2, half_rows, HALO), f32)],
            in_specs=piece_specs,
            out_specs=[HBM] * 2 + [VMEM],
            scratch_shapes=[
                pltpu.VMEM((2, half_rows, width), f32),
                pltpu.SemaphoreType.DMA((2,)),
            ],
            compiler_params=small,
            cost_estimate=pl.CostEstimate(flops=1 << 22, bytes_accessed=1 << 21, transcendentals=0),
            name="inner_terms",
        )(*pieces)

        def finish_kernel(phase_in, absorb_in, inner_ref, *refs):
            arrived_refs, outs = refs[:ways], refs[ways : ways + 2]
            strips, semaphores = refs[ways + 2 :]
            copies = Copies(semaphores)
            leaving = []
            for way in range(ways):
                start = place.received(place.column(), way) * (width - HALO)
                for plane in range(2):
                    strips[way, plane] = arrived_refs[way][plane] + inner_ref[way, plane]
                    target = outs[plane].at[:, pl.ds(pl.multiple_of(start, LANES), HALO)]
                    leaving.append(copies.start(strips.at[way, plane], target))
            wait_for(leaving)

        result = pl.pallas_call(
            finish_kernel,
            out_shape=[sds((half_rows, width), f32)] * 2,
            in_specs=[HBM, HBM, VMEM] + [VMEM] * ways,
            out_specs=[HBM] * 2,
            scratch_shapes=[
                pltpu.VMEM((ways, 2, half_rows, HALO), f32),
                pltpu.SemaphoreType.DMA((2 * ways,)),
            ],
            input_output_aliases={0: 0, 1: 1},
            compiler_params=small,
            name="finish",
        )(*results, inner, *arrived)
        return tuple(plane[None, None] for plane in result)

    in_specs = (
        P("section", "tile", None, None),
        P("section", "tile", None, None),
        P(),
        P("tile", "rep", None, None),
        P("tile", "rep", None, None, None),
    )
    out_specs = (P("section", "tile", "rep", None), P("section", "tile", "rep", None))
    return jax.shard_map(shards, mesh=mesh, in_specs=in_specs, out_specs=out_specs, check_vma=False)
```

```python
import math

import jax
import jax.numpy as jnp
import ml_dtypes
import numpy as np
from jax import lax
from jax.experimental import pallas as pl
from jax.experimental.pallas import tpu as pltpu
from jax.sharding import PartitionSpec as P

HALO = 128
LANES = 128
AXES = ("section", "tile", "rep")

dead_time = 0.1
background = 0.1
loss_weight = 0.1
fresnel = 0.5

f32 = jnp.float32
bf16 = jnp.bfloat16

SMEM = pl.BlockSpec(memory_space=pltpu.SMEM)
VMEM = pl.BlockSpec(memory_space=pltpu.VMEM)
HBM = pl.BlockSpec(memory_space=pltpu.HBM)


def two_parts(matrix):
    high = matrix.astype(ml_dtypes.bfloat16)
    low = (matrix - high.astype(np.float64)).astype(ml_dtypes.bfloat16)
    return np.stack([high, low])


def from_left(matrix):
    return np.block([[matrix.real, -matrix.imag], [matrix.imag, matrix.real]])


def from_right(matrix):
    return np.block([[matrix.real, matrix.imag], [-matrix.imag, matrix.real]])


def wave_tables(length):
    half = length // 2
    indices = np.arange(length)
    shifted = np.where(indices < half, indices, indices - length)
    kernel = np.exp(1j * math.pi * fresnel * shifted.astype(np.float64) ** 2 / length)
    spread = np.fft.ifft(kernel)
    circulant = spread[(indices[:, None] - indices[None, :]) % length]
    first, second = circulant[:half, :half], circulant[:half, half:]
    plus, minus = (first + second) / 2, (first - second) / 2
    near = [from_left(plus), from_left(minus), from_right(plus), from_right(minus)]
    turns = np.outer(indices[:half], indices[:half]) % half
    even = np.exp(-2j * math.pi * turns / half) / math.sqrt(length)
    odd = even * np.exp(-2j * math.pi * indices[:half] / length)[None, :]
    far = [from_left(even), from_left(odd), from_right(even.T), from_right(odd.T)]
    back = [from_left(even.T), from_left(odd.T), from_right(even), from_right(odd)]
    sort = np.zeros((length, length))
    sort[np.arange(half), 2 * np.arange(half)] = 1
    sort[half + np.arange(half), 2 * np.arange(half) + 1] = 1
    tables = np.stack([two_parts(m) for m in near + far + back])
    return tables, np.stack([sort, sort.T]).astype(ml_dtypes.bfloat16)


def fitted(function, degree):
    top = math.pi**2
    fit = np.polynomial.chebyshev.Chebyshev.interpolate(function, degree, domain=[0.0, top])
    return [float(c) for c in fit.convert(kind=np.polynomial.Polynomial).coef]


def sine_ratio(u):
    angle = np.sqrt(np.maximum(u, 1e-12))
    return np.sin(angle) / angle


SINE = fitted(sine_ratio, 8)
COSINE = fitted(lambda u: np.cos(np.sqrt(np.maximum(u, 0.0))), 8)


def polynomial(coefficients, u):
    total = jnp.full_like(u, coefficients[-1])
    for c in coefficients[-2::-1]:
        total = total * u + c
    return total


def cos_sin(angle):
    square = angle * angle
    return polynomial(COSINE, square), angle * polynomial(SINE, square)


def halves(value):
    high = value.astype(bf16)
    return high, (value - high.astype(f32)).astype(bf16)


def dot(a, b):
    return jnp.dot(a, b, preferred_element_type=f32)


def left_by(tables, index, value):
    high, low = halves(value)
    return dot(tables[index, 0], high) + dot(tables[index, 1], high) + dot(tables[index, 0], low)


def right_by(tables, index, value):
    high, low = halves(value)
    return dot(high, tables[index, 0]) + dot(high, tables[index, 1]) + dot(low, tables[index, 0])


def propagate(tables, at, re, im, fold, unfold):
    half = re.shape[0] // 2
    re0, re1, im0, im1 = re[:half], re[half:], im[:half], im[half:]
    if fold:
        re0, re1, im0, im1 = re0 + re1, re0 - re1, im0 + im1, im0 - im1
    first = left_by(tables, at, jnp.concatenate([re0, im0], 0))
    second = left_by(tables, at + 1, jnp.concatenate([re1, im1], 0))
    if unfold:
        first, second = first + second, first - second
    re = jnp.concatenate([first[:half], second[:half]], 0)
    im = jnp.concatenate([first[half:], second[half:]], 0)
    re0, re1, im0, im1 = re[:, :half], re[:, half:], im[:, :half], im[:, half:]
    if fold:
        re0, re1, im0, im1 = re0 + re1, re0 - re1, im0 + im1, im0 - im1
    first = right_by(tables, at + 2, jnp.concatenate([re0, im0], 1))
    second = right_by(tables, at + 3, jnp.concatenate([re1, im1], 1))
    if unfold:
        first, second = first + second, first - second
    re = jnp.concatenate([first[:, :half], second[:, :half]], 1)
    im = jnp.concatenate([first[:, half:], second[:, half:]], 1)
    return re, im


def near_field(tables, re, im):
    return propagate(tables, 0, re, im, True, True)


def far_field(tables, re, im):
    return propagate(tables, 4, re, im, True, False)


def far_back(tables, re, im):
    return propagate(tables, 8, re, im, False, True)


def likelihood_seed(far_re, far_im, observed):
    intensity = far_re * far_re + far_im * far_im
    shifted_total = intensity + background
    denominator = 1.0 + dead_time * shifted_total
    model_rate = shifted_total / denominator
    slope_term = loss_weight * (1.0 - observed / model_rate) / (denominator * denominator)
    return (2.0 * slope_term * far_re, 2.0 * slope_term * far_im)


def in_band(index, offset, band):
    cell = index + (band // 2) * (2 * HALO)
    return (cell >= offset) & (cell < offset + 2 * HALO)


def row_at(ref, number=0):
    return ref[2 * number, :1, :1]


def column_at(ref, number=0):
    return ref[2 * number + 1, :1, :1]


def lane_index(shape):
    return lax.broadcasted_iota(jnp.int32, shape, len(shape) - 1)


def row_index(shape):
    return lax.broadcasted_iota(jnp.int32, shape, len(shape) - 2)


def choose_columns(bands, offset):
    lane = lane_index(bands[1].shape)
    first = jnp.where(
        in_band(lane, offset, 0), bands[0], jnp.where(in_band(lane, offset, 2), bands[2], bands[4])
    )
    second = jnp.where(in_band(lane + HALO, offset, 1), bands[1], bands[3])
    return jnp.concatenate([first, second], 1)


def part_of_band(value, offset, band):
    start = (band % 2) * HALO
    half = value[:, start : start + HALO]
    return jnp.where(in_band(lane_index(half.shape) + start, offset, band), half, 0.0)


class Copies:
    def __init__(self, semaphores):
        self.semaphores = semaphores
        self.count = 0

    def start(self, source, target):
        copy = pltpu.make_async_copy(source, target, self.semaphores.at[self.count])
        self.count += 1
        copy.start()
        return copy


def wait_for(copies):
    for copy in copies:
        copy.wait()


class Place:
    def __init__(self, grid_side):
        self.grid_side = grid_side
        self.ways = 1 if grid_side == 2 else 2

    def section(self):
        return lax.axis_index("section")

    def rep(self):
        return lax.axis_index("rep")

    def row(self):
        return lax.axis_index("tile") // self.grid_side

    def column(self):
        return lax.axis_index("tile") % self.grid_side

    def owner(self):
        return 1 + self.column() % 2

    def sent(self, index, way):
        return 1 - index if self.ways == 1 else way

    def received(self, index, way):
        return 1 - index if self.ways == 1 else 1 - way


def solution(mesh):
    sections, tiles, reps = (mesh.shape[a] for a in AXES)
    grid_side = math.isqrt(tiles)
    place = Place(grid_side)
    ways = place.ways

    def everywhere(target_of):
        pairs = []
        for s in range(sections):
            for t in range(tiles):
                for r in range(reps):
                    target = target_of(s, t // grid_side, t % grid_side, r)
                    if target is None:
                        continue
                    ts, ty, tx, tr = target
                    if not (0 <= ty < grid_side and 0 <= tx < grid_side):
                        continue
                    pairs.append(
                        ((s * tiles + t) * reps + r, (ts * tiles + ty * grid_side + tx) * reps + tr)
                    )
        return pairs

    def move(value, target_of):
        return lax.ppermute(value, AXES, everywhere(target_of))

    def trade_rows(values):
        if ways == 1:
            return [move(values[0], lambda s, y, x, r: (s, 1 - y, x, r))]
        return [
            move(values[0], lambda s, y, x, r: (s, y - 1, x, r)),
            move(values[1], lambda s, y, x, r: (s, y + 1, x, r)),
        ]

    def trade_columns(values):
        if ways == 1:
            return [move(values[0], lambda s, y, x, r: (s, y, 1 - x, r))]
        return [
            move(values[0], lambda s, y, x, r: (s, y, x - 1, r)),
            move(values[1], lambda s, y, x, r: (s, y, x + 1, r)),
        ]

    def owner_of(x):
        return 1 + x % 2

    def near_of(x):
        return 3 * (x % 2)

    def middle_of(x):
        return 3 - owner_of(x)

    def far_of(x):
        return 3 - near_of(x)

    def shards(phase_shift, absorption, probe_wave, positions, counts):
        width = phase_shift.shape[2]
        frame = probe_wave.shape[1]
        half_rows = width // reps
        phase = phase_shift.reshape(width, width)
        absorb = absorption.reshape(width, width)
        spot = positions.reshape(1, 2)
        spot_tiles = jnp.broadcast_to(positions.reshape(2, 1, 1), (2, 8, LANES))
        observed = counts.reshape(frame, frame)
        sds = jax.ShapeDtypeStruct
        small = pltpu.CompilerParams(vmem_limit_bytes=8 << 20)

        spots_rows = trade_rows([spot_tiles] * ways)
        def load_kernel(phase_ref, absorb_ref, tile, *refs):
            edges, copies = refs[:ways], Copies(refs[ways])
            wait_for([copies.start(phase_ref, tile.at[0]), copies.start(absorb_ref, tile.at[1])])
            for way in range(ways):
                start = place.sent(place.column(), way) * (width - HALO)
                edges[way][...] = tile[:, :, pl.ds(pl.multiple_of(start, LANES), HALO)]

        tile, *edges = pl.pallas_call(
            load_kernel,
            out_shape=[sds((2, width, width), f32)] + [sds((2, width, HALO), f32)] * ways,
            in_specs=[HBM] * 2,
            out_specs=[VMEM] * (1 + ways),
            scratch_shapes=[pltpu.SemaphoreType.DMA((2,))],
            compiler_params=small,
            name="load",
        )(phase, absorb)
        sides = trade_columns(edges)

        def rows_of(refs, plane, rows):
            return refs[0][plane, rows, :], [side[plane, rows, :] for side in refs[1:]]

        def bands_of(tile, margin):
            inner = [tile[:, i * HALO : (i + 1) * HALO] for i in range(3)]
            ends = []
            for side in range(2):
                if ways == 1:
                    there = place.received(place.column(), 0) == side
                    ends.append(jnp.where(there, margin[0], 0.0))
                else:
                    there = place.column() > 0 if side == 0 else place.column() < grid_side - 1
                    ends.append(jnp.where(there, margin[1 - side], 0.0))
            return [ends[0], *inner, ends[1]]

        def transmission(angle, loss):
            cosine, sine = cos_sin(angle)
            damping = jnp.exp(-loss)
            return damping * cosine, damping * sine

        def strip_kernel(*refs):
            loaded, spot_refs = refs[: 1 + ways], refs[1 + ways : 1 + 2 * ways]
            outs = refs[1 + 2 * ways :]
            for way in range(ways):
                below = place.sent(place.row(), way)
                rows = pl.ds(pl.multiple_of(below * (width - HALO), 8), HALO)
                column = column_at(spot_refs[way if ways == 1 else 1 - way])
                cut = [
                    choose_columns(bands_of(*rows_of(loaded, plane, rows)), column)
                    for plane in range(2)
                ]
                outs[way][0], outs[way][1] = transmission(*cut)

        strips = pl.pallas_call(
            strip_kernel,
            out_shape=[sds((2, HALO, frame), f32)] * ways,
            in_specs=[VMEM] * (1 + 2 * ways),
            out_specs=[VMEM] * ways,
            compiler_params=small,
            name="halo_rows",
        )(tile, *sides, *spots_rows)
        rims = trade_rows(strips)

        def window_kernel(spot_ref, *refs):
            loaded, (whole, part) = refs[:-2], refs[-2:]
            row, column = row_at(spot_ref), column_at(spot_ref)
            index = row_index((HALO, HALO))
            upper = in_band(index + HALO, row, 1)
            planes = []
            for plane in range(2):
                first = bands_of(*rows_of(loaded, plane, slice(0, HALO)))
                third = bands_of(*rows_of(loaded, plane, slice(2 * HALO, 3 * HALO)))
                bands = [jnp.where(upper, v, w) for v, w in zip(first, third)]
                planes.append(choose_columns(bands, column))
            whole[0], whole[1] = transmission(*planes)
            planes = []
            for plane in range(2):
                bands = bands_of(*rows_of(loaded, plane, slice(HALO, 2 * HALO)))
                planes.append(choose_columns(bands, column))
            real, imag = transmission(*planes)
            inside = in_band(row_index((HALO, frame)), row, 2)
            part[0], part[1] = jnp.where(inside, real, 1.0), jnp.where(inside, imag, 0.0)

        whole, part = pl.pallas_call(
            window_kernel,
            out_shape=[sds((2, HALO, frame), f32)] * 2,
            in_specs=[VMEM] * (2 + ways),
            out_specs=[VMEM] * 2,
            compiler_params=small,
            name="window",
        )(spot_tiles, tile, *sides)

        def to_owner(value):
            return [
                move(
                    value,
                    lambda s, y, x, r: (owner_of(x), y, x, r) if s == section_of(x) else None,
                )
                for section_of in (near_of, middle_of, far_of)
            ]

        wholes = to_owner(whole)

        def join_kernel(spot_ref, part_ref, *refs):
            rim_refs, out = refs[:ways], refs[ways]
            row = row_at(spot_ref)
            index = row_index((HALO, frame))
            out[...] = part_ref[...]
            for way in range(ways):
                side = place.received(place.row(), way)
                there = jnp.where(side == 0, place.row() > 0, place.row() < grid_side - 1)
                shifted = index + jnp.where(side == 0, 0, 2 * (2 * HALO))
                near = (shifted >= row) & (shifted < row + jnp.where(there, 2 * HALO, 0))
                for plane in range(2):
                    out[plane] = jnp.where(near, rim_refs[way][plane], out[plane])

        joined = pl.pallas_call(
            join_kernel,
            out_shape=sds((2, HALO, frame), f32),
            in_specs=[VMEM] * (2 + ways),
            out_specs=VMEM,
            compiler_params=small,
            name="join",
        )(spot_tiles, part, *rims)
        joineds = to_owner(joined)

        tables, sort = wave_tables(frame)

        def prepare_kernel(spot_ref, probe, seen, sort, rolled, counted):
            row, column = lax.rem(spot_ref[0, 0], frame), lax.rem(spot_ref[0, 1], frame)
            for plane in range(2):
                rolled[plane] = pltpu.roll(pltpu.roll(probe[plane], row, 0), column, 1)
            first = dot(sort[0], seen[...].astype(f32).astype(bf16)).astype(bf16)
            counted[...] = dot(first, sort[1])

        rolled, counted = pl.pallas_call(
            prepare_kernel,
            out_shape=[sds((2, frame, frame), f32), sds((frame, frame), f32)],
            in_specs=[SMEM] + [VMEM] * 3,
            out_specs=[VMEM] * 2,
            compiler_params=small,
            name="prepare",
        )(spot, probe_wave, observed, sort)
        places, counted = lax.optimization_barrier(
            (jnp.concatenate([spot_tiles] + spots_rows, 0), counted)
        )
        spots_rep = move(places, lambda s, y, x, r: (s, y, x, 1 - r))

        def frame_kernel(partner_ref, probe, seen, tables, *refs):
            whole_refs, joined_refs, outs = refs[:4], refs[4:8], refs[8:12]
            fields, exits = refs[12:]
            own_is_second = place.owner() == 1
            for half, parts in ((slice(HALO, None), whole_refs), (slice(None, HALO), joined_refs)):
                for plane in range(2):
                    near, own, middle, far = (part[plane] for part in parts)
                    fields[0, plane, half] = jnp.where(own_is_second, near, far)
                    fields[1, plane, half] = jnp.where(own_is_second, own, middle)
                    fields[2, plane, half] = jnp.where(own_is_second, middle, own)
                    fields[3, plane, half] = jnp.where(own_is_second, far, near)
            re, im = probe[0], probe[1]
            for number in range(4):
                o_re, o_im = fields[number, 0], fields[number, 1]
                exit_re, exit_im = o_re * re - o_im * im, o_re * im + o_im * re
                exits[number, 0], exits[number, 1] = exit_re, exit_im
                if number < 3:
                    re, im = near_field(tables, exit_re, exit_im)
            re, im = far_field(tables, exit_re, exit_im)
            re, im = likelihood_seed(re, im, seen[...])
            im = -im
            for number in reversed(range(4)):
                if number == 3:
                    re, im = far_back(tables, re, im)
                else:
                    re, im = near_field(tables, re, im)
                exit_re, exit_im = exits[number, 0], exits[number, 1]
                phase_term = -(re * exit_im + im * exit_re)
                absorb_term = im * exit_im - re * exit_re
                if number > 0:
                    o_re, o_im = fields[number, 0], fields[number, 1]
                    re, im = o_re * re - o_im * im, o_re * im + o_im * re
                exits[number, 0], exits[number, 1] = phase_term, absorb_term
            for plane in range(2):
                one, two, three, four = (exits[number, plane] for number in range(4))
                outs[0][plane] = jnp.where(own_is_second, one, four)
                outs[1][plane] = jnp.where(own_is_second, two, three)
                outs[2][plane] = jnp.where(own_is_second, three, two)
                outs[3][plane] = jnp.where(own_is_second, four, one)

        terms = pl.pallas_call(
            frame_kernel,
            out_shape=[sds((2, frame, frame), f32)] * 4,
            in_specs=[VMEM] * 12,
            out_specs=[VMEM] * 4,
            scratch_shapes=[
                pltpu.VMEM((4, 2, frame, frame), f32),
                pltpu.VMEM((4, 2, frame, frame), f32),
            ],
            compiler_params=pltpu.CompilerParams(vmem_limit_bytes=16 << 20),
            name="frame",
        )(
            spots_rep, rolled, counted, tables,
            wholes[0], whole, wholes[1], wholes[2],
            joineds[0], joined, joineds[1], joineds[2],
        )

        def from_owner(value, section_of):
            return move(
                value,
                lambda s, y, x, r: (section_of(x), y, x, r) if s == owner_of(x) else None,
            )

        far_terms = from_owner(terms[3], far_of)
        back = (
            far_terms,
            from_owner(terms[0], near_of),
            from_owner(terms[2], middle_of),
            terms[1],
        )

        def load_term(refs, term):
            section, owner = place.section(), place.owner()
            near = 3 * (owner - 1)
            choice = jnp.where(
                section == 3 - near, 0, jnp.where(section == near, 1, jnp.where(section == owner, 3, 2))
            )
            for number, ref in enumerate(refs):

                @pl.when(choice == number)
                def _():
                    term[...] = ref[...]

        def rows_for(term, plane, row, rep):
            index = row_index((frame, frame))
            middle = jnp.where(in_band(index, row, 2), term[plane], 0.0)
            later = middle[HALO // 2 :]
            earlier = jnp.where(in_band(index, row, 0), term[plane], 0.0)
            earlier = jnp.concatenate([earlier[HALO:], middle[: HALO // 2]], 0)
            return jnp.where(rep == 0, earlier, later)

        def parts_kernel(spot_ref, *refs):
            back_refs, (give, straight, across, term) = refs[:-4], refs[-4:]
            if len(back_refs) > 1:
                load_term(back_refs, term)
            else:
                term = back_refs[0]
            rep, row = place.rep(), row_at(spot_ref)
            index = row_index((HALO, frame))
            for plane in range(2):
                give[plane] = rows_for(term, plane, row, 1 - rep)
                first = term[plane, :HALO]
                above = jnp.where(in_band(index, row, 0), first, 0.0)
                below = jnp.where(in_band(index, row, 4), first, 0.0)
                straight[plane] = jnp.where(rep == 1, above, below)
                across[plane] = jnp.where(rep == 1, below, above)

        def exchange(terms_here, owners, name):
            give, straight, across = pl.pallas_call(
                parts_kernel,
                out_shape=[sds((2, half_rows, frame), f32)] + [sds((2, HALO, frame), f32)] * 2,
                in_specs=[VMEM] * (1 + len(terms_here)),
                out_specs=[VMEM] * 3,
                scratch_shapes=[pltpu.VMEM((2, frame, frame), f32)],
                compiler_params=small,
                name=name,
            )(spot_tiles, *terms_here)

            def of_those(target_of):
                return lambda s, y, x, r: (
                    target_of(s, y, x, r) if (s == owner_of(x)) == owners else None
                )

            return (
                move(give, of_those(lambda s, y, x, r: (s, y, x, 1 - r))),
                move(straight, of_those(lambda s, y, x, r: (s, y + 1 - 2 * r, x, r))),
                move(across, of_those(lambda s, y, x, r: (s, y - 1 + 2 * r, x, 1 - r))),
            )

        came_early = exchange(terms[1:2], True, "own_parts")
        came_late = exchange(back[:3], False, "parts")

        def keep_kernel(spot_ref, *refs):
            back_refs, (mine, term) = refs[:4], refs[4:]
            load_term(back_refs, term)
            for plane in range(2):
                mine[plane] = rows_for(term, plane, row_at(spot_ref), place.rep())

        kept = pl.pallas_call(
            keep_kernel,
            out_shape=sds((2, half_rows, frame), f32),
            in_specs=[VMEM] * 5,
            out_specs=VMEM,
            scratch_shapes=[pltpu.VMEM((2, frame, frame), f32)],
            compiler_params=small,
            cost_estimate=pl.CostEstimate(flops=1 << 22, bytes_accessed=1 << 21, transcendentals=0),
            name="keep",
        )(spot_tiles, *back)

        def add_band(band, plane, refs):
            spot_ref, partner_ref, kept_ref, *spot_refs = refs[: 3 + ways]
            early, late = refs[3 + ways : 6 + ways], refs[6 + ways : count]
            is_owner = place.section() == place.owner()
            given, straight, across = (
                jnp.where(is_owner, a[plane], b[plane]) for a, b in zip(early, late)
            )
            rep = place.rep()
            if ways == 1:
                straight_column, across_column = column_at(spot_refs[0]), column_at(partner_ref, 1)
            else:
                straight_column = jnp.where(rep == 1, column_at(spot_refs[0]), column_at(spot_refs[1]))
                across_column = jnp.where(
                    rep == 1, column_at(partner_ref, 1), column_at(partner_ref, 2)
                )
            total = part_of_band(kept_ref[plane], column_at(spot_ref), band)
            total += part_of_band(given, column_at(partner_ref), band)
            strip = part_of_band(straight, straight_column, band)
            strip += part_of_band(across, across_column, band)
            gap = jnp.zeros((half_rows - HALO, HALO), f32)
            early, late = jnp.concatenate([strip, gap], 0), jnp.concatenate([gap, strip], 0)
            return total + jnp.where(rep == 1, late, early)

        pieces = (spot_tiles, spots_rep, kept, *spots_rows, *came_early, *came_late)
        piece_specs = [VMEM] * (9 + ways)
        count = len(piece_specs)

        def edge_kernel(*refs):
            for way in range(ways):
                for plane in range(2):
                    if ways == 1:
                        value = jnp.where(
                            place.column() == 0,
                            add_band(4, plane, refs),
                            add_band(0, plane, refs),
                        )
                    else:
                        value = add_band(4 * way, plane, refs)
                    refs[count + way][plane] = value

        leaving = pl.pallas_call(
            edge_kernel,
            out_shape=[sds((2, half_rows, HALO), f32)] * ways,
            in_specs=piece_specs,
            out_specs=[VMEM] * ways,
            compiler_params=small,
            name="edge_terms",
        )(*pieces)
        arrived = trade_columns(leaving)

        def inner_kernel(*refs):
            outs, inner, total, semaphores = refs[count : count + 2], *refs[count + 2 :]
            copies = Copies(semaphores)
            started = []
            for plane in range(2):
                bands = [add_band(band, plane, refs) for band in (1, 2, 3)]
                for number, value in enumerate(bands):
                    total[plane, :, number * HALO : (number + 1) * HALO] = value
                started.append(copies.start(total.at[plane], outs[plane]))
                for way in range(ways):
                    first = place.received(place.column(), way) == 0
                    inner[way, plane] = jnp.where(first, bands[0], bands[2])
            wait_for(started)

        *results, inner = pl.pallas_call(
            inner_kernel,
            out_shape=[sds((half_rows, width), f32)] * 2
            + [sds((ways, 2, half_rows, HALO), f32)],
            in_specs=piece_specs,
            out_specs=[HBM] * 2 + [VMEM],
            scratch_shapes=[
                pltpu.VMEM((2, half_rows, width), f32),
                pltpu.SemaphoreType.DMA((2,)),
            ],
            compiler_params=small,
            cost_estimate=pl.CostEstimate(flops=1 << 22, bytes_accessed=1 << 21, transcendentals=0),
            name="inner_terms",
        )(*pieces)

        def finish_kernel(phase_in, absorb_in, inner_ref, *refs):
            arrived_refs, outs = refs[:ways], refs[ways : ways + 2]
            strips, semaphores = refs[ways + 2 :]
            copies = Copies(semaphores)
            leaving = []
            for way in range(ways):
                start = place.received(place.column(), way) * (width - HALO)
                for plane in range(2):
                    strips[way, plane] = arrived_refs[way][plane] + inner_ref[way, plane]
                    target = outs[plane].at[:, pl.ds(pl.multiple_of(start, LANES), HALO)]
                    leaving.append(copies.start(strips.at[way, plane], target))
            wait_for(leaving)

        result = pl.pallas_call(
            finish_kernel,
            out_shape=[sds((half_rows, width), f32)] * 2,
            in_specs=[HBM, HBM, VMEM] + [VMEM] * ways,
            out_specs=[HBM] * 2,
            scratch_shapes=[
                pltpu.VMEM((ways, 2, half_rows, HALO), f32),
                pltpu.SemaphoreType.DMA((2 * ways,)),
            ],
            input_output_aliases={0: 0, 1: 1},
            compiler_params=small,
            name="finish",
        )(*results, inner, *arrived)
        return tuple(plane[None, None] for plane in result)

    in_specs = (
        P("section", "tile", None, None),
        P("section", "tile", None, None),
        P(),
        P("tile", "rep", None, None),
        P("tile", "rep", None, None, None),
    )
    out_specs = (P("section", "tile", "rep", None), P("section", "tile", "rep", None))
    return jax.shard_map(shards, mesh=mesh, in_specs=in_specs, out_specs=out_specs, check_vma=False)
```

```python
import math

import jax
import jax.numpy as jnp
import ml_dtypes
import numpy as np
from jax import lax
from jax.experimental import pallas as pl
from jax.experimental.pallas import tpu as pltpu
from jax.sharding import PartitionSpec as P

HALO = 128
LANES = 128
AXES = ("section", "tile", "rep")

dead_time = 0.1
background = 0.1
loss_weight = 0.1
fresnel = 0.5

f32 = jnp.float32
bf16 = jnp.bfloat16

SMEM = pl.BlockSpec(memory_space=pltpu.SMEM)
VMEM = pl.BlockSpec(memory_space=pltpu.VMEM)
HBM = pl.BlockSpec(memory_space=pltpu.HBM)


def two_parts(matrix):
    high = matrix.astype(ml_dtypes.bfloat16)
    low = (matrix - high.astype(np.float64)).astype(ml_dtypes.bfloat16)
    return np.stack([high, low])


def from_left(matrix):
    return np.block([[matrix.real, -matrix.imag], [matrix.imag, matrix.real]])


def from_right(matrix):
    return np.block([[matrix.real, matrix.imag], [-matrix.imag, matrix.real]])


def wave_tables(length):
    half = length // 2
    indices = np.arange(length)
    shifted = np.where(indices < half, indices, indices - length)
    kernel = np.exp(1j * math.pi * fresnel * shifted.astype(np.float64) ** 2 / length)
    spread = np.fft.ifft(kernel)
    circulant = spread[(indices[:, None] - indices[None, :]) % length]
    first, second = circulant[:half, :half], circulant[:half, half:]
    plus, minus = (first + second) / 2, (first - second) / 2
    near = [from_left(plus), from_left(minus), from_right(plus), from_right(minus)]
    turns = np.outer(indices[:half], indices[:half]) % half
    even = np.exp(-2j * math.pi * turns / half) / math.sqrt(length)
    odd = even * np.exp(-2j * math.pi * indices[:half] / length)[None, :]
    far = [from_left(even), from_left(odd), from_right(even.T), from_right(odd.T)]
    back = [from_left(even.T), from_left(odd.T), from_right(even), from_right(odd)]
    sort = np.zeros((length, length))
    sort[np.arange(half), 2 * np.arange(half)] = 1
    sort[half + np.arange(half), 2 * np.arange(half) + 1] = 1
    tables = np.stack([two_parts(m) for m in near + far + back])
    return tables, np.stack([sort, sort.T]).astype(ml_dtypes.bfloat16)


def fitted(function, degree):
    top = math.pi**2
    fit = np.polynomial.chebyshev.Chebyshev.interpolate(function, degree, domain=[0.0, top])
    return [float(c) for c in fit.convert(kind=np.polynomial.Polynomial).coef]


def sine_ratio(u):
    angle = np.sqrt(np.maximum(u, 1e-12))
    return np.sin(angle) / angle


SINE = fitted(sine_ratio, 8)
COSINE = fitted(lambda u: np.cos(np.sqrt(np.maximum(u, 0.0))), 8)


def polynomial(coefficients, u):
    total = jnp.full_like(u, coefficients[-1])
    for c in coefficients[-2::-1]:
        total = total * u + c
    return total


def cos_sin(angle):
    square = angle * angle
    return polynomial(COSINE, square), angle * polynomial(SINE, square)


def halves(value):
    high = value.astype(bf16)
    return high, (value - high.astype(f32)).astype(bf16)


def dot(a, b):
    return jnp.dot(a, b, preferred_element_type=f32)


def left_by(tables, index, value):
    high, low = halves(value)
    return dot(tables[index, 0], high) + dot(tables[index, 1], high) + dot(tables[index, 0], low)


def right_by(tables, index, value):
    high, low = halves(value)
    return dot(high, tables[index, 0]) + dot(high, tables[index, 1]) + dot(low, tables[index, 0])


def propagate(tables, at, re, im, fold, unfold):
    half = re.shape[0] // 2
    re0, re1, im0, im1 = re[:half], re[half:], im[:half], im[half:]
    if fold:
        re0, re1, im0, im1 = re0 + re1, re0 - re1, im0 + im1, im0 - im1
    first = left_by(tables, at, jnp.concatenate([re0, im0], 0))
    second = left_by(tables, at + 1, jnp.concatenate([re1, im1], 0))
    if unfold:
        first, second = first + second, first - second
    re = jnp.concatenate([first[:half], second[:half]], 0)
    im = jnp.concatenate([first[half:], second[half:]], 0)
    re0, re1, im0, im1 = re[:, :half], re[:, half:], im[:, :half], im[:, half:]
    if fold:
        re0, re1, im0, im1 = re0 + re1, re0 - re1, im0 + im1, im0 - im1
    first = right_by(tables, at + 2, jnp.concatenate([re0, im0], 1))
    second = right_by(tables, at + 3, jnp.concatenate([re1, im1], 1))
    if unfold:
        first, second = first + second, first - second
    re = jnp.concatenate([first[:, :half], second[:, :half]], 1)
    im = jnp.concatenate([first[:, half:], second[:, half:]], 1)
    return re, im


def near_field(tables, re, im):
    return propagate(tables, 0, re, im, True, True)


def far_field(tables, re, im):
    return propagate(tables, 4, re, im, True, False)


def far_back(tables, re, im):
    return propagate(tables, 8, re, im, False, True)


def likelihood_seed(far_re, far_im, observed):
    intensity = far_re * far_re + far_im * far_im
    shifted_total = intensity + background
    denominator = 1.0 + dead_time * shifted_total
    model_rate = shifted_total / denominator
    slope_term = loss_weight * (1.0 - observed / model_rate) / (denominator * denominator)
    return (2.0 * slope_term * far_re, 2.0 * slope_term * far_im)


def in_band(index, offset, band):
    cell = index + (band // 2) * (2 * HALO)
    return (cell >= offset) & (cell < offset + 2 * HALO)


def row_at(ref, number=0):
    return ref[2 * number, :1, :1]


def column_at(ref, number=0):
    return ref[2 * number + 1, :1, :1]


def lane_index(shape):
    return lax.broadcasted_iota(jnp.int32, shape, len(shape) - 1)


def row_index(shape):
    return lax.broadcasted_iota(jnp.int32, shape, len(shape) - 2)


def choose_columns(bands, offset):
    lane = lane_index(bands[1].shape)
    first = jnp.where(
        in_band(lane, offset, 0), bands[0], jnp.where(in_band(lane, offset, 2), bands[2], bands[4])
    )
    second = jnp.where(in_band(lane + HALO, offset, 1), bands[1], bands[3])
    return jnp.concatenate([first, second], 1)


def part_of_band(value, offset, band):
    start = (band % 2) * HALO
    half = value[:, start : start + HALO]
    return jnp.where(in_band(lane_index(half.shape) + start, offset, band), half, 0.0)


class Copies:
    def __init__(self, semaphores):
        self.semaphores = semaphores
        self.count = 0

    def start(self, source, target):
        copy = pltpu.make_async_copy(source, target, self.semaphores.at[self.count])
        self.count += 1
        copy.start()
        return copy


def wait_for(copies):
    for copy in copies:
        copy.wait()


class Place:
    def __init__(self, grid_side):
        self.grid_side = grid_side
        self.ways = 1 if grid_side == 2 else 2

    def section(self):
        return lax.axis_index("section")

    def rep(self):
        return lax.axis_index("rep")

    def row(self):
        return lax.axis_index("tile") // self.grid_side

    def column(self):
        return lax.axis_index("tile") % self.grid_side

    def owner(self):
        return 1 + self.column() % 2

    def sent(self, index, way):
        return 1 - index if self.ways == 1 else way

    def received(self, index, way):
        return 1 - index if self.ways == 1 else 1 - way


def solution(mesh):
    sections, tiles, reps = (mesh.shape[a] for a in AXES)
    grid_side = math.isqrt(tiles)
    place = Place(grid_side)
    ways = place.ways

    def everywhere(target_of):
        pairs = []
        for s in range(sections):
            for t in range(tiles):
                for r in range(reps):
                    target = target_of(s, t // grid_side, t % grid_side, r)
                    if target is None:
                        continue
                    ts, ty, tx, tr = target
                    if not (0 <= ty < grid_side and 0 <= tx < grid_side):
                        continue
                    pairs.append(
                        ((s * tiles + t) * reps + r, (ts * tiles + ty * grid_side + tx) * reps + tr)
                    )
        return pairs

    def move(value, target_of):
        return lax.ppermute(value, AXES, everywhere(target_of))

    def trade_rows(values):
        if ways == 1:
            return [move(values[0], lambda s, y, x, r: (s, 1 - y, x, r))]
        return [
            move(values[0], lambda s, y, x, r: (s, y - 1, x, r)),
            move(values[1], lambda s, y, x, r: (s, y + 1, x, r)),
        ]

    def trade_columns(values):
        if ways == 1:
            return [move(values[0], lambda s, y, x, r: (s, y, 1 - x, r))]
        return [
            move(values[0], lambda s, y, x, r: (s, y, x - 1, r)),
            move(values[1], lambda s, y, x, r: (s, y, x + 1, r)),
        ]

    def owner_of(x):
        return 1 + x % 2

    def near_of(x):
        return 3 * (x % 2)

    def middle_of(x):
        return 3 - owner_of(x)

    def far_of(x):
        return 3 - near_of(x)

    def shards(phase_shift, absorption, probe_wave, positions, counts):
        width = phase_shift.shape[2]
        frame = probe_wave.shape[1]
        half_rows = width // reps
        phase = phase_shift.reshape(width, width)
        absorb = absorption.reshape(width, width)
        spot = positions.reshape(1, 2)
        def tiles_of(spots):
            return jnp.broadcast_to(spots.reshape(-1, 1, 1), (spots.size, 8, LANES))

        spot_tiles = tiles_of(spot)
        observed = counts.reshape(frame, frame)
        sds = jax.ShapeDtypeStruct
        small = pltpu.CompilerParams(vmem_limit_bytes=8 << 20)

        spots_rows = [tiles_of(spots) for spots in trade_rows([spot] * ways)]
        def load_kernel(phase_ref, absorb_ref, tile, *refs):
            edges, copies = refs[:ways], Copies(refs[ways])
            wait_for([copies.start(phase_ref, tile.at[0]), copies.start(absorb_ref, tile.at[1])])
            for way in range(ways):
                start = place.sent(place.column(), way) * (width - HALO)
                edges[way][...] = tile[:, :, pl.ds(pl.multiple_of(start, LANES), HALO)]

        tile, *edges = pl.pallas_call(
            load_kernel,
            out_shape=[sds((2, width, width), f32)] + [sds((2, width, HALO), f32)] * ways,
            in_specs=[HBM] * 2,
            out_specs=[VMEM] * (1 + ways),
            scratch_shapes=[pltpu.SemaphoreType.DMA((2,))],
            compiler_params=small,
            name="load",
        )(phase, absorb)
        edges, spots_rows = lax.optimization_barrier((edges, spots_rows))
        sides = trade_columns(edges)

        def rows_of(refs, plane, rows):
            return refs[0][plane, rows, :], [side[plane, rows, :] for side in refs[1:]]

        def bands_of(tile, margin):
            inner = [tile[:, i * HALO : (i + 1) * HALO] for i in range(3)]
            ends = []
            for side in range(2):
                if ways == 1:
                    there = place.received(place.column(), 0) == side
                    ends.append(jnp.where(there, margin[0], 0.0))
                else:
                    there = place.column() > 0 if side == 0 else place.column() < grid_side - 1
                    ends.append(jnp.where(there, margin[1 - side], 0.0))
            return [ends[0], *inner, ends[1]]

        def transmission(angle, loss):
            cosine, sine = cos_sin(angle)
            damping = jnp.exp(-loss)
            return damping * cosine, damping * sine

        def strip_kernel(*refs):
            loaded, spot_refs = refs[: 1 + ways], refs[1 + ways : 1 + 2 * ways]
            outs = refs[1 + 2 * ways :]
            for way in range(ways):
                below = place.sent(place.row(), way)
                rows = pl.ds(pl.multiple_of(below * (width - HALO), 8), HALO)
                column = column_at(spot_refs[way if ways == 1 else 1 - way])
                cut = [
                    choose_columns(bands_of(*rows_of(loaded, plane, rows)), column)
                    for plane in range(2)
                ]
                outs[way][0], outs[way][1] = transmission(*cut)

        strips = pl.pallas_call(
            strip_kernel,
            out_shape=[sds((2, HALO, frame), f32)] * ways,
            in_specs=[VMEM] * (1 + 2 * ways),
            out_specs=[VMEM] * ways,
            compiler_params=small,
            name="halo_rows",
        )(tile, *sides, *spots_rows)
        rims = trade_rows(strips)

        def window_kernel(spot_ref, *refs):
            loaded, (whole, part) = refs[:-2], refs[-2:]
            row, column = row_at(spot_ref), column_at(spot_ref)
            index = row_index((HALO, HALO))
            upper = in_band(index + HALO, row, 1)
            planes = []
            for plane in range(2):
                first = bands_of(*rows_of(loaded, plane, slice(0, HALO)))
                third = bands_of(*rows_of(loaded, plane, slice(2 * HALO, 3 * HALO)))
                bands = [jnp.where(upper, v, w) for v, w in zip(first, third)]
                planes.append(choose_columns(bands, column))
            whole[0], whole[1] = transmission(*planes)
            planes = []
            for plane in range(2):
                bands = bands_of(*rows_of(loaded, plane, slice(HALO, 2 * HALO)))
                planes.append(choose_columns(bands, column))
            real, imag = transmission(*planes)
            inside = in_band(row_index((HALO, frame)), row, 2)
            part[0], part[1] = jnp.where(inside, real, 1.0), jnp.where(inside, imag, 0.0)

        whole, part = pl.pallas_call(
            window_kernel,
            out_shape=[sds((2, HALO, frame), f32)] * 2,
            in_specs=[VMEM] * (2 + ways),
            out_specs=[VMEM] * 2,
            compiler_params=small,
            name="window",
        )(spot_tiles, tile, *sides)

        def to_owner(value):
            return [
                move(
                    value,
                    lambda s, y, x, r: (owner_of(x), y, x, r) if s == section_of(x) else None,
                )
                for section_of in (near_of, middle_of, far_of)
            ]

        wholes = to_owner(whole)

        def join_kernel(spot_ref, part_ref, *refs):
            rim_refs, out = refs[:ways], refs[ways]
            row = row_at(spot_ref)
            index = row_index((HALO, frame))
            out[...] = part_ref[...]
            for way in range(ways):
                side = place.received(place.row(), way)
                there = jnp.where(side == 0, place.row() > 0, place.row() < grid_side - 1)
                shifted = index + jnp.where(side == 0, 0, 2 * (2 * HALO))
                near = (shifted >= row) & (shifted < row + jnp.where(there, 2 * HALO, 0))
                for plane in range(2):
                    out[plane] = jnp.where(near, rim_refs[way][plane], out[plane])

        joined = pl.pallas_call(
            join_kernel,
            out_shape=sds((2, HALO, frame), f32),
            in_specs=[VMEM] * (2 + ways),
            out_specs=VMEM,
            compiler_params=small,
            name="join",
        )(spot_tiles, part, *rims)
        joined, probe_late = lax.optimization_barrier((joined, probe_wave))
        joineds = to_owner(joined)

        tables, sort = wave_tables(frame)

        def prepare_kernel(spot_ref, probe, seen, sort, rolled, counted):
            row, column = lax.rem(spot_ref[0, 0], frame), lax.rem(spot_ref[0, 1], frame)
            for plane in range(2):
                rolled[plane] = pltpu.roll(pltpu.roll(probe[plane], row, 0), column, 1)
            first = dot(sort[0], seen[...].astype(f32).astype(bf16)).astype(bf16)
            counted[...] = dot(first, sort[1])

        rolled, counted = pl.pallas_call(
            prepare_kernel,
            out_shape=[sds((2, frame, frame), f32), sds((frame, frame), f32)],
            in_specs=[SMEM] + [VMEM] * 3,
            out_specs=[VMEM] * 2,
            compiler_params=small,
            name="prepare",
        )(spot, probe_late, observed, sort)
        places, counted = lax.optimization_barrier(
            (jnp.concatenate([spot_tiles] + spots_rows, 0), counted)
        )
        spots_rep = move(places, lambda s, y, x, r: (s, y, x, 1 - r))

        def frame_kernel(partner_ref, probe, seen, tables, *refs):
            whole_refs, joined_refs, outs = refs[:4], refs[4:8], refs[8:12]
            fields, exits = refs[12:]
            own_is_second = place.owner() == 1
            for half, parts in ((slice(HALO, None), whole_refs), (slice(None, HALO), joined_refs)):
                for plane in range(2):
                    near, own, middle, far = (part[plane] for part in parts)
                    fields[0, plane, half] = jnp.where(own_is_second, near, far)
                    fields[1, plane, half] = jnp.where(own_is_second, own, middle)
                    fields[2, plane, half] = jnp.where(own_is_second, middle, own)
                    fields[3, plane, half] = jnp.where(own_is_second, far, near)
            re, im = probe[0], probe[1]
            for number in range(4):
                o_re, o_im = fields[number, 0], fields[number, 1]
                exit_re, exit_im = o_re * re - o_im * im, o_re * im + o_im * re
                exits[number, 0], exits[number, 1] = exit_re, exit_im
                if number < 3:
                    re, im = near_field(tables, exit_re, exit_im)
            re, im = far_field(tables, exit_re, exit_im)
            re, im = likelihood_seed(re, im, seen[...])
            im = -im
            for number in reversed(range(4)):
                if number == 3:
                    re, im = far_back(tables, re, im)
                else:
                    re, im = near_field(tables, re, im)
                exit_re, exit_im = exits[number, 0], exits[number, 1]
                phase_term = -(re * exit_im + im * exit_re)
                absorb_term = im * exit_im - re * exit_re
                if number > 0:
                    o_re, o_im = fields[number, 0], fields[number, 1]
                    re, im = o_re * re - o_im * im, o_re * im + o_im * re
                exits[number, 0], exits[number, 1] = phase_term, absorb_term
            for plane in range(2):
                one, two, three, four = (exits[number, plane] for number in range(4))
                outs[0][plane] = jnp.where(own_is_second, one, four)
                outs[1][plane] = jnp.where(own_is_second, two, three)
                outs[2][plane] = jnp.where(own_is_second, three, two)
                outs[3][plane] = jnp.where(own_is_second, four, one)

        terms = pl.pallas_call(
            frame_kernel,
            out_shape=[sds((2, frame, frame), f32)] * 4,
            in_specs=[VMEM] * 12,
            out_specs=[VMEM] * 4,
            scratch_shapes=[
                pltpu.VMEM((4, 2, frame, frame), f32),
                pltpu.VMEM((4, 2, frame, frame), f32),
            ],
            compiler_params=pltpu.CompilerParams(vmem_limit_bytes=16 << 20),
            name="frame",
        )(
            spots_rep, rolled, counted, tables,
            wholes[0], whole, wholes[1], wholes[2],
            joineds[0], joined, joineds[1], joineds[2],
        )

        def from_owner(value, section_of):
            return move(
                value,
                lambda s, y, x, r: (section_of(x), y, x, r) if s == owner_of(x) else None,
            )

        far_terms = from_owner(terms[3], far_of)
        back = (
            far_terms,
            from_owner(terms[0], near_of),
            from_owner(terms[2], middle_of),
            terms[1],
        )

        def load_term(refs, term):
            section, owner = place.section(), place.owner()
            near = 3 * (owner - 1)
            choice = jnp.where(
                section == 3 - near, 0, jnp.where(section == near, 1, jnp.where(section == owner, 3, 2))
            )
            for number, ref in enumerate(refs):

                @pl.when(choice == number)
                def _():
                    term[...] = ref[...]

        def rows_for(term, plane, row, rep):
            index = row_index((frame, frame))
            middle = jnp.where(in_band(index, row, 2), term[plane], 0.0)
            later = middle[HALO // 2 :]
            earlier = jnp.where(in_band(index, row, 0), term[plane], 0.0)
            earlier = jnp.concatenate([earlier[HALO:], middle[: HALO // 2]], 0)
            return jnp.where(rep == 0, earlier, later)

        def split_strips(term, row, straight, across):
            rep = place.rep()
            index = row_index((HALO, frame))
            for plane in range(2):
                first = term[plane, :HALO]
                above = jnp.where(in_band(index, row, 0), first, 0.0)
                below = jnp.where(in_band(index, row, 4), first, 0.0)
                straight[plane] = jnp.where(rep == 1, above, below)
                across[plane] = jnp.where(rep == 1, below, above)

        def own_kernel(spot_ref, own, straight, across):
            split_strips(own, row_at(spot_ref), straight, across)

        def parts_kernel(spot_ref, *refs):
            back_refs, (give, straight, across, term) = refs[:-4], refs[-4:]
            load_term(back_refs, term)
            for plane in range(2):
                give[plane] = rows_for(term, plane, row_at(spot_ref), 1 - place.rep())
            split_strips(term, row_at(spot_ref), straight, across)

        def exchange(straight, across, owners):
            def of_those(target_of):
                return lambda s, y, x, r: (
                    target_of(s, y, x, r) if (s == owner_of(x)) == owners else None
                )

            return (
                move(straight, of_those(lambda s, y, x, r: (s, y + 1 - 2 * r, x, r))),
                move(across, of_those(lambda s, y, x, r: (s, y - 1 + 2 * r, x, 1 - r))),
            )

        strip = sds((2, HALO, frame), f32)
        own_strips = pl.pallas_call(
            own_kernel,
            out_shape=[strip] * 2,
            in_specs=[VMEM] * 2,
            out_specs=[VMEM] * 2,
            compiler_params=small,
            name="own_parts",
        )(spot_tiles, terms[1])
        came_early = exchange(*own_strips, True)
        back, came_early = lax.optimization_barrier((back, came_early))
        give, *strips = pl.pallas_call(
            parts_kernel,
            out_shape=[sds((2, half_rows, frame), f32), strip, strip],
            in_specs=[VMEM] * 5,
            out_specs=[VMEM] * 3,
            scratch_shapes=[pltpu.VMEM((2, frame, frame), f32)],
            compiler_params=small,
            name="parts",
        )(spot_tiles, *back)

        came_late = exchange(*strips, False)
        given = move(give, lambda s, y, x, r: (s, y, x, 1 - r))

        def keep_kernel(spot_ref, *refs):
            back_refs, (mine, term) = refs[:4], refs[4:]
            load_term(back_refs, term)
            for plane in range(2):
                mine[plane] = rows_for(term, plane, row_at(spot_ref), place.rep())

        kept = pl.pallas_call(
            keep_kernel,
            out_shape=sds((2, half_rows, frame), f32),
            in_specs=[VMEM] * 5,
            out_specs=VMEM,
            scratch_shapes=[pltpu.VMEM((2, frame, frame), f32)],
            compiler_params=small,
            cost_estimate=pl.CostEstimate(flops=1 << 22, bytes_accessed=1 << 21, transcendentals=0),
            name="keep",
        )(spot_tiles, *back)

        def add_band(band, plane, refs):
            spot_ref, partner_ref, kept_ref, *spot_refs = refs[: 3 + ways]
            given, early, late = refs[3 + ways], refs[4 + ways : 6 + ways], refs[6 + ways : count]
            is_owner = place.section() == place.owner()
            straight, across = (
                jnp.where(is_owner, a[plane], b[plane]) for a, b in zip(early, late)
            )
            rep = place.rep()
            if ways == 1:
                straight_column, across_column = column_at(spot_refs[0]), column_at(partner_ref, 1)
            else:
                straight_column = jnp.where(rep == 1, column_at(spot_refs[0]), column_at(spot_refs[1]))
                across_column = jnp.where(
                    rep == 1, column_at(partner_ref, 1), column_at(partner_ref, 2)
                )
            total = part_of_band(kept_ref[plane], column_at(spot_ref), band)
            total += part_of_band(given[plane], column_at(partner_ref), band)
            strip = part_of_band(straight, straight_column, band)
            strip += part_of_band(across, across_column, band)
            gap = jnp.zeros((half_rows - HALO, HALO), f32)
            early, late = jnp.concatenate([strip, gap], 0), jnp.concatenate([gap, strip], 0)
            return total + jnp.where(rep == 1, late, early)

        pieces = (spot_tiles, spots_rep, kept, *spots_rows, given, *came_early, *came_late)
        piece_specs = [VMEM] * (8 + ways)
        count = len(piece_specs)

        def edge_kernel(*refs):
            for way in range(ways):
                for plane in range(2):
                    if ways == 1:
                        value = jnp.where(
                            place.column() == 0,
                            add_band(4, plane, refs),
                            add_band(0, plane, refs),
                        )
                    else:
                        value = add_band(4 * way, plane, refs)
                    refs[count + way][plane] = value

        leaving = pl.pallas_call(
            edge_kernel,
            out_shape=[sds((2, half_rows, HALO), f32)] * ways,
            in_specs=piece_specs,
            out_specs=[VMEM] * ways,
            compiler_params=small,
            name="edge_terms",
        )(*pieces)
        arrived = trade_columns(leaving)

        def inner_kernel(*refs):
            outs, inner, total, semaphores = refs[count : count + 2], *refs[count + 2 :]
            copies = Copies(semaphores)
            started = []
            for plane in range(2):
                bands = [add_band(band, plane, refs) for band in (1, 2, 3)]
                for number, value in enumerate(bands):
                    total[plane, :, number * HALO : (number + 1) * HALO] = value
                started.append(copies.start(total.at[plane], outs[plane]))
                for way in range(ways):
                    first = place.received(place.column(), way) == 0
                    inner[way, plane] = jnp.where(first, bands[0], bands[2])
            wait_for(started)

        *results, inner = pl.pallas_call(
            inner_kernel,
            out_shape=[sds((half_rows, width), f32)] * 2
            + [sds((ways, 2, half_rows, HALO), f32)],
            in_specs=piece_specs,
            out_specs=[HBM] * 2 + [VMEM],
            scratch_shapes=[
                pltpu.VMEM((2, half_rows, width), f32),
                pltpu.SemaphoreType.DMA((2,)),
            ],
            compiler_params=small,
            cost_estimate=pl.CostEstimate(flops=1 << 22, bytes_accessed=1 << 21, transcendentals=0),
            name="inner_terms",
        )(*pieces)

        def finish_kernel(phase_in, absorb_in, inner_ref, *refs):
            arrived_refs, outs = refs[:ways], refs[ways : ways + 2]
            strips, semaphores = refs[ways + 2 :]
            copies = Copies(semaphores)
            leaving = []
            for way in range(ways):
                start = place.received(place.column(), way) * (width - HALO)
                for plane in range(2):
                    strips[way, plane] = arrived_refs[way][plane] + inner_ref[way, plane]
                    target = outs[plane].at[:, pl.ds(pl.multiple_of(start, LANES), HALO)]
                    leaving.append(copies.start(strips.at[way, plane], target))
            wait_for(leaving)

        result = pl.pallas_call(
            finish_kernel,
            out_shape=[sds((half_rows, width), f32)] * 2,
            in_specs=[HBM, HBM, VMEM] + [VMEM] * ways,
            out_specs=[HBM] * 2,
            scratch_shapes=[
                pltpu.VMEM((ways, 2, half_rows, HALO), f32),
                pltpu.SemaphoreType.DMA((2 * ways,)),
            ],
            input_output_aliases={0: 0, 1: 1},
            compiler_params=small,
            name="finish",
        )(*results, inner, *arrived)
        return tuple(plane[None, None] for plane in result)

    in_specs = (
        P("section", "tile", None, None),
        P("section", "tile", None, None),
        P(),
        P("tile", "rep", None, None),
        P("tile", "rep", None, None, None),
    )
    out_specs = (P("section", "tile", "rep", None), P("section", "tile", "rep", None))
    return jax.shard_map(shards, mesh=mesh, in_specs=in_specs, out_specs=out_specs, check_vma=False)
```

```python
import math

import jax
import jax.numpy as jnp
import ml_dtypes
import numpy as np
from jax import lax
from jax.experimental import pallas as pl
from jax.experimental.pallas import tpu as pltpu
from jax.sharding import PartitionSpec as P

HALO = 128
LANES = 128
AXES = ("section", "tile", "rep")

dead_time = 0.1
background = 0.1
loss_weight = 0.1
fresnel = 0.5

f32 = jnp.float32
bf16 = jnp.bfloat16

SMEM = pl.BlockSpec(memory_space=pltpu.SMEM)
VMEM = pl.BlockSpec(memory_space=pltpu.VMEM)
HBM = pl.BlockSpec(memory_space=pltpu.HBM)


def two_parts(matrix):
    high = matrix.astype(ml_dtypes.bfloat16)
    low = (matrix - high.astype(np.float64)).astype(ml_dtypes.bfloat16)
    return np.stack([high, low])


def from_left(matrix):
    return np.block([[matrix.real, -matrix.imag], [matrix.imag, matrix.real]])


def from_right(matrix):
    return np.block([[matrix.real, matrix.imag], [-matrix.imag, matrix.real]])


def wave_tables(length):
    half = length // 2
    indices = np.arange(length)
    shifted = np.where(indices < half, indices, indices - length)
    kernel = np.exp(1j * math.pi * fresnel * shifted.astype(np.float64) ** 2 / length)
    spread = np.fft.ifft(kernel)
    circulant = spread[(indices[:, None] - indices[None, :]) % length]
    first, second = circulant[:half, :half], circulant[:half, half:]
    plus, minus = (first + second) / 2, (first - second) / 2
    near = [from_left(plus), from_left(minus), from_right(plus), from_right(minus)]
    turns = np.outer(indices[:half], indices[:half]) % half
    even = np.exp(-2j * math.pi * turns / half) / math.sqrt(length)
    odd = even * np.exp(-2j * math.pi * indices[:half] / length)[None, :]
    far = [from_left(even), from_left(odd), from_right(even.T), from_right(odd.T)]
    back = [from_left(even.T), from_left(odd.T), from_right(even), from_right(odd)]
    sort = np.zeros((length, length))
    sort[np.arange(half), 2 * np.arange(half)] = 1
    sort[half + np.arange(half), 2 * np.arange(half) + 1] = 1
    tables = np.stack([two_parts(m) for m in near + far + back])
    return tables, np.stack([sort, sort.T]).astype(ml_dtypes.bfloat16)


def fitted(function, degree):
    top = math.pi**2
    fit = np.polynomial.chebyshev.Chebyshev.interpolate(function, degree, domain=[0.0, top])
    return [float(c) for c in fit.convert(kind=np.polynomial.Polynomial).coef]


def sine_ratio(u):
    angle = np.sqrt(np.maximum(u, 1e-12))
    return np.sin(angle) / angle


SINE = fitted(sine_ratio, 8)
COSINE = fitted(lambda u: np.cos(np.sqrt(np.maximum(u, 0.0))), 8)


def polynomial(coefficients, u):
    total = jnp.full_like(u, coefficients[-1])
    for c in coefficients[-2::-1]:
        total = total * u + c
    return total


def cos_sin(angle):
    square = angle * angle
    return polynomial(COSINE, square), angle * polynomial(SINE, square)


def halves(value):
    high = value.astype(bf16)
    return high, (value - high.astype(f32)).astype(bf16)


def dot(a, b):
    return jnp.dot(a, b, preferred_element_type=f32)


def left_by(tables, index, value):
    high, low = halves(value)
    return dot(tables[index, 0], high) + dot(tables[index, 1], high) + dot(tables[index, 0], low)


def right_by(tables, index, value):
    high, low = halves(value)
    return dot(high, tables[index, 0]) + dot(high, tables[index, 1]) + dot(low, tables[index, 0])


def propagate(tables, at, re, im, fold, unfold):
    half = re.shape[0] // 2
    re0, re1, im0, im1 = re[:half], re[half:], im[:half], im[half:]
    if fold:
        re0, re1, im0, im1 = re0 + re1, re0 - re1, im0 + im1, im0 - im1
    first = left_by(tables, at, jnp.concatenate([re0, im0], 0))
    second = left_by(tables, at + 1, jnp.concatenate([re1, im1], 0))
    if unfold:
        first, second = first + second, first - second
    re = jnp.concatenate([first[:half], second[:half]], 0)
    im = jnp.concatenate([first[half:], second[half:]], 0)
    re0, re1, im0, im1 = re[:, :half], re[:, half:], im[:, :half], im[:, half:]
    if fold:
        re0, re1, im0, im1 = re0 + re1, re0 - re1, im0 + im1, im0 - im1
    first = right_by(tables, at + 2, jnp.concatenate([re0, im0], 1))
    second = right_by(tables, at + 3, jnp.concatenate([re1, im1], 1))
    if unfold:
        first, second = first + second, first - second
    re = jnp.concatenate([first[:, :half], second[:, :half]], 1)
    im = jnp.concatenate([first[:, half:], second[:, half:]], 1)
    return re, im


def near_field(tables, re, im):
    return propagate(tables, 0, re, im, True, True)


def far_field(tables, re, im):
    return propagate(tables, 4, re, im, True, False)


def far_back(tables, re, im):
    return propagate(tables, 8, re, im, False, True)


def likelihood_seed(far_re, far_im, observed):
    intensity = far_re * far_re + far_im * far_im
    shifted_total = intensity + background
    denominator = 1.0 + dead_time * shifted_total
    model_rate = shifted_total / denominator
    slope_term = loss_weight * (1.0 - observed / model_rate) / (denominator * denominator)
    return (2.0 * slope_term * far_re, 2.0 * slope_term * far_im)


def in_band(index, offset, band):
    cell = index + (band // 2) * (2 * HALO)
    return (cell >= offset) & (cell < offset + 2 * HALO)


def row_at(ref, number=0):
    return ref[2 * number, :1, :1]


def column_at(ref, number=0):
    return ref[2 * number + 1, :1, :1]


def lane_index(shape):
    return lax.broadcasted_iota(jnp.int32, shape, len(shape) - 1)


def row_index(shape):
    return lax.broadcasted_iota(jnp.int32, shape, len(shape) - 2)


def choose_columns(bands, offset):
    lane = lane_index(bands[1].shape)
    first = jnp.where(
        in_band(lane, offset, 0), bands[0], jnp.where(in_band(lane, offset, 2), bands[2], bands[4])
    )
    second = jnp.where(in_band(lane + HALO, offset, 1), bands[1], bands[3])
    return jnp.concatenate([first, second], 1)


def part_of_band(value, offset, band):
    start = (band % 2) * HALO
    half = value[:, start : start + HALO]
    return jnp.where(in_band(lane_index(half.shape) + start, offset, band), half, 0.0)


class Copies:
    def __init__(self, semaphores):
        self.semaphores = semaphores
        self.count = 0

    def start(self, source, target):
        copy = pltpu.make_async_copy(source, target, self.semaphores.at[self.count])
        self.count += 1
        copy.start()
        return copy


def wait_for(copies):
    for copy in copies:
        copy.wait()


class Place:
    def __init__(self, grid_side):
        self.grid_side = grid_side
        self.ways = 1 if grid_side == 2 else 2

    def section(self):
        return lax.axis_index("section")

    def rep(self):
        return lax.axis_index("rep")

    def row(self):
        return lax.axis_index("tile") // self.grid_side

    def column(self):
        return lax.axis_index("tile") % self.grid_side

    def owner(self):
        return 1 + self.column() % 2

    def sent(self, index, way):
        return 1 - index if self.ways == 1 else way

    def received(self, index, way):
        return 1 - index if self.ways == 1 else 1 - way


def solution(mesh):
    sections, tiles, reps = (mesh.shape[a] for a in AXES)
    grid_side = math.isqrt(tiles)
    place = Place(grid_side)
    ways = place.ways

    def everywhere(target_of):
        pairs = []
        for s in range(sections):
            for t in range(tiles):
                for r in range(reps):
                    target = target_of(s, t // grid_side, t % grid_side, r)
                    if target is None:
                        continue
                    ts, ty, tx, tr = target
                    if not (0 <= ty < grid_side and 0 <= tx < grid_side):
                        continue
                    pairs.append(
                        ((s * tiles + t) * reps + r, (ts * tiles + ty * grid_side + tx) * reps + tr)
                    )
        return pairs

    def move(value, target_of):
        return lax.ppermute(value, AXES, everywhere(target_of))

    def trade_rows(values):
        if ways == 1:
            return [move(values[0], lambda s, y, x, r: (s, 1 - y, x, r))]
        return [
            move(values[0], lambda s, y, x, r: (s, y - 1, x, r)),
            move(values[1], lambda s, y, x, r: (s, y + 1, x, r)),
        ]

    def trade_columns(values):
        if ways == 1:
            return [move(values[0], lambda s, y, x, r: (s, y, 1 - x, r))]
        return [
            move(values[0], lambda s, y, x, r: (s, y, x - 1, r)),
            move(values[1], lambda s, y, x, r: (s, y, x + 1, r)),
        ]

    def owner_of(x):
        return 1 + x % 2

    def near_of(x):
        return 3 * (x % 2)

    def middle_of(x):
        return 3 - owner_of(x)

    def far_of(x):
        return 3 - near_of(x)

    def shards(phase_shift, absorption, probe_wave, positions, counts):
        width = phase_shift.shape[2]
        frame = probe_wave.shape[1]
        half_rows = width // reps
        phase = phase_shift.reshape(width, width)
        absorb = absorption.reshape(width, width)
        spot = positions.reshape(1, 2)
        def tiles_of(spots):
            return jnp.broadcast_to(spots.reshape(-1, 1, 1), (spots.size, 8, LANES))

        spot_tiles = tiles_of(spot)
        observed = counts.reshape(frame, frame)
        sds = jax.ShapeDtypeStruct
        small = pltpu.CompilerParams(vmem_limit_bytes=8 << 20)

        spots_rows = [tiles_of(spots) for spots in trade_rows([spot] * ways)]
        tile = jnp.stack([phase, absorb])

        def load_kernel(tile, *edges):
            for way in range(ways):
                start = place.sent(place.column(), way) * (width - HALO)
                edges[way][...] = tile[:, :, pl.ds(pl.multiple_of(start, LANES), HALO)]

        edges = pl.pallas_call(
            load_kernel,
            out_shape=[sds((2, width, HALO), f32)] * ways,
            in_specs=[VMEM],
            out_specs=[VMEM] * ways,
            compiler_params=small,
            name="edges",
        )(tile)
        edges, spots_rows = lax.optimization_barrier((edges, spots_rows))
        sides = trade_columns(edges)

        def rows_of(refs, plane, rows):
            return refs[0][plane, rows, :], [side[plane, rows, :] for side in refs[1:]]

        def bands_of(tile, margin):
            inner = [tile[:, i * HALO : (i + 1) * HALO] for i in range(3)]
            ends = []
            for side in range(2):
                if ways == 1:
                    there = place.received(place.column(), 0) == side
                    ends.append(jnp.where(there, margin[0], 0.0))
                else:
                    there = place.column() > 0 if side == 0 else place.column() < grid_side - 1
                    ends.append(jnp.where(there, margin[1 - side], 0.0))
            return [ends[0], *inner, ends[1]]

        def transmission(angle, loss):
            cosine, sine = cos_sin(angle)
            damping = jnp.exp(-loss)
            return damping * cosine, damping * sine

        def strip_kernel(*refs):
            loaded, spot_refs = refs[: 1 + ways], refs[1 + ways : 1 + 2 * ways]
            outs = refs[1 + 2 * ways :]
            for way in range(ways):
                below = place.sent(place.row(), way)
                rows = pl.ds(pl.multiple_of(below * (width - HALO), 8), HALO)
                column = column_at(spot_refs[way if ways == 1 else 1 - way])
                cut = [
                    choose_columns(bands_of(*rows_of(loaded, plane, rows)), column)
                    for plane in range(2)
                ]
                outs[way][0], outs[way][1] = transmission(*cut)

        strips = pl.pallas_call(
            strip_kernel,
            out_shape=[sds((2, HALO, frame), f32)] * ways,
            in_specs=[VMEM] * (1 + 2 * ways),
            out_specs=[VMEM] * ways,
            compiler_params=small,
            name="halo_rows",
        )(tile, *sides, *spots_rows)
        rims = trade_rows(strips)

        def window_kernel(spot_ref, *refs):
            loaded, (whole, part) = refs[:-2], refs[-2:]
            row, column = row_at(spot_ref), column_at(spot_ref)
            index = row_index((HALO, HALO))
            upper = in_band(index + HALO, row, 1)
            planes = []
            for plane in range(2):
                first = bands_of(*rows_of(loaded, plane, slice(0, HALO)))
                third = bands_of(*rows_of(loaded, plane, slice(2 * HALO, 3 * HALO)))
                bands = [jnp.where(upper, v, w) for v, w in zip(first, third)]
                planes.append(choose_columns(bands, column))
            whole[0], whole[1] = transmission(*planes)
            planes = []
            for plane in range(2):
                bands = bands_of(*rows_of(loaded, plane, slice(HALO, 2 * HALO)))
                planes.append(choose_columns(bands, column))
            real, imag = transmission(*planes)
            inside = in_band(row_index((HALO, frame)), row, 2)
            part[0], part[1] = jnp.where(inside, real, 1.0), jnp.where(inside, imag, 0.0)

        whole, part = pl.pallas_call(
            window_kernel,
            out_shape=[sds((2, HALO, frame), f32)] * 2,
            in_specs=[VMEM] * (2 + ways),
            out_specs=[VMEM] * 2,
            compiler_params=small,
            name="window",
        )(spot_tiles, tile, *sides)

        def to_owner(value):
            return [
                move(
                    value,
                    lambda s, y, x, r: (owner_of(x), y, x, r) if s == section_of(x) else None,
                )
                for section_of in (near_of, middle_of, far_of)
            ]

        wholes = to_owner(whole)

        def join_kernel(spot_ref, part_ref, *refs):
            rim_refs, out = refs[:ways], refs[ways]
            row = row_at(spot_ref)
            index = row_index((HALO, frame))
            out[...] = part_ref[...]
            for way in range(ways):
                side = place.received(place.row(), way)
                there = jnp.where(side == 0, place.row() > 0, place.row() < grid_side - 1)
                shifted = index + jnp.where(side == 0, 0, 2 * (2 * HALO))
                near = (shifted >= row) & (shifted < row + jnp.where(there, 2 * HALO, 0))
                for plane in range(2):
                    out[plane] = jnp.where(near, rim_refs[way][plane], out[plane])

        joined = pl.pallas_call(
            join_kernel,
            out_shape=sds((2, HALO, frame), f32),
            in_specs=[VMEM] * (2 + ways),
            out_specs=VMEM,
            compiler_params=small,
            name="join",
        )(spot_tiles, part, *rims)
        joined, probe_late = lax.optimization_barrier((joined, probe_wave))
        joineds = to_owner(joined)

        tables, sort = wave_tables(frame)

        def prepare_kernel(spot_ref, probe, seen, sort, rolled, counted):
            row, column = lax.rem(spot_ref[0, 0], frame), lax.rem(spot_ref[0, 1], frame)
            for plane in range(2):
                rolled[plane] = pltpu.roll(pltpu.roll(probe[plane], row, 0), column, 1)
            first = dot(sort[0], seen[...].astype(f32).astype(bf16)).astype(bf16)
            counted[...] = dot(first, sort[1])

        rolled, counted = pl.pallas_call(
            prepare_kernel,
            out_shape=[sds((2, frame, frame), f32), sds((frame, frame), f32)],
            in_specs=[SMEM] + [VMEM] * 3,
            out_specs=[VMEM] * 2,
            compiler_params=small,
            name="prepare",
        )(spot, probe_late, observed, sort)
        places, counted = lax.optimization_barrier(
            (jnp.concatenate([spot_tiles] + spots_rows, 0), counted)
        )
        spots_rep = move(places, lambda s, y, x, r: (s, y, x, 1 - r))

        def frame_kernel(partner_ref, probe, seen, tables, *refs):
            whole_refs, joined_refs, outs = refs[:4], refs[4:8], refs[8:12]
            fields, exits = refs[12:]
            own_is_second = place.owner() == 1
            far, middle, own, near = zip(joined_refs[::-1], whole_refs)
            choices = ((near, far), (own, middle), (middle, own), (far, near))

            def field(number, plane):
                first, second = choices[number]
                return jnp.concatenate(
                    [jnp.where(own_is_second, a[plane], b[plane]) for a, b in zip(first, second)], 0
                )

            re, im = probe[0], probe[1]
            for number in range(4):
                o_re, o_im = field(number, 0), field(number, 1)
                fields[number, 0], fields[number, 1] = o_re, o_im
                exit_re, exit_im = o_re * re - o_im * im, o_re * im + o_im * re
                exits[number, 0], exits[number, 1] = exit_re, exit_im
                if number < 3:
                    re, im = near_field(tables, exit_re, exit_im)
            re, im = far_field(tables, exit_re, exit_im)
            re, im = likelihood_seed(re, im, seen[...])
            im = -im
            for number in reversed(range(4)):
                if number == 3:
                    re, im = far_back(tables, re, im)
                else:
                    re, im = near_field(tables, re, im)
                exit_re, exit_im = exits[number, 0], exits[number, 1]
                found = -(re * exit_im + im * exit_re), im * exit_im - re * exit_re
                if number > 0:
                    o_re, o_im = fields[number, 0], fields[number, 1]
                    re, im = o_re * re - o_im * im, o_re * im + o_im * re
                one, other = (0, 3) if number in (0, 3) else (1, 2)
                for plane, term in enumerate(found):
                    if number >= 2:
                        outs[one][plane] = term
                        outs[other][plane] = term
                    else:
                        kept_term = outs[one][plane]
                        outs[one][plane] = jnp.where(own_is_second, term, kept_term)
                        outs[other][plane] = jnp.where(own_is_second, kept_term, term)

        terms = pl.pallas_call(
            frame_kernel,
            out_shape=[sds((2, frame, frame), f32)] * 4,
            in_specs=[VMEM] * 12,
            out_specs=[VMEM] * 4,
            scratch_shapes=[
                pltpu.VMEM((4, 2, frame, frame), f32),
                pltpu.VMEM((4, 2, frame, frame), f32),
            ],
            compiler_params=pltpu.CompilerParams(vmem_limit_bytes=16 << 20),
            name="frame",
        )(
            spots_rep, rolled, counted, tables,
            wholes[2], wholes[1], whole, wholes[0],
            joineds[0], joined, joineds[1], joineds[2],
        )

        def from_owner(value, section_of):
            return move(
                value,
                lambda s, y, x, r: (section_of(x), y, x, r) if s == owner_of(x) else None,
            )

        far_terms = from_owner(terms[3], far_of)
        back = (
            far_terms,
            from_owner(terms[0], near_of),
            from_owner(terms[2], middle_of),
            terms[1],
        )

        def load_term(refs, term):
            section, owner = place.section(), place.owner()
            near = 3 * (owner - 1)
            choice = jnp.where(
                section == 3 - near, 0, jnp.where(section == near, 1, jnp.where(section == owner, 3, 2))
            )
            for number, ref in enumerate(refs):

                @pl.when(choice == number)
                def _():
                    term[...] = ref[...]

        def rows_for(term, plane, row, rep):
            index = row_index((frame, frame))
            middle = jnp.where(in_band(index, row, 2), term[plane], 0.0)
            later = middle[HALO // 2 :]
            earlier = jnp.where(in_band(index, row, 0), term[plane], 0.0)
            earlier = jnp.concatenate([earlier[HALO:], middle[: HALO // 2]], 0)
            return jnp.where(rep == 0, earlier, later)

        def split_strips(term, row, straight, across):
            rep = place.rep()
            index = row_index((HALO, frame))
            for plane in range(2):
                first = term[plane, :HALO]
                above = jnp.where(in_band(index, row, 0), first, 0.0)
                below = jnp.where(in_band(index, row, 4), first, 0.0)
                straight[plane] = jnp.where(rep == 1, above, below)
                across[plane] = jnp.where(rep == 1, below, above)

        def own_kernel(spot_ref, own, straight, across):
            split_strips(own, row_at(spot_ref), straight, across)

        def parts_kernel(spot_ref, *refs):
            back_refs, (give, straight, across, term) = refs[:-4], refs[-4:]
            load_term(back_refs, term)
            for plane in range(2):
                give[plane] = rows_for(term, plane, row_at(spot_ref), 1 - place.rep())
            split_strips(term, row_at(spot_ref), straight, across)

        def exchange(straight, across, owners):
            def of_those(target_of):
                return lambda s, y, x, r: (
                    target_of(s, y, x, r) if (s == owner_of(x)) == owners else None
                )

            return (
                move(straight, of_those(lambda s, y, x, r: (s, y + 1 - 2 * r, x, r))),
                move(across, of_those(lambda s, y, x, r: (s, y - 1 + 2 * r, x, 1 - r))),
            )

        strip = sds((2, HALO, frame), f32)
        own_strips = pl.pallas_call(
            own_kernel,
            out_shape=[strip] * 2,
            in_specs=[VMEM] * 2,
            out_specs=[VMEM] * 2,
            compiler_params=small,
            name="own_parts",
        )(spot_tiles, terms[1])
        came_early = exchange(*own_strips, True)
        back, came_early = lax.optimization_barrier((back, came_early))
        give, *strips = pl.pallas_call(
            parts_kernel,
            out_shape=[sds((2, half_rows, frame), f32), strip, strip],
            in_specs=[VMEM] * 5,
            out_specs=[VMEM] * 3,
            scratch_shapes=[pltpu.VMEM((2, frame, frame), f32)],
            compiler_params=small,
            name="parts",
        )(spot_tiles, *back)

        came_late = exchange(*strips, False)
        given = move(give, lambda s, y, x, r: (s, y, x, 1 - r))

        def keep_kernel(spot_ref, *refs):
            back_refs, (mine, term) = refs[:4], refs[4:]
            load_term(back_refs, term)
            for plane in range(2):
                mine[plane] = rows_for(term, plane, row_at(spot_ref), place.rep())

        kept = pl.pallas_call(
            keep_kernel,
            out_shape=sds((2, half_rows, frame), f32),
            in_specs=[VMEM] * 5,
            out_specs=VMEM,
            scratch_shapes=[pltpu.VMEM((2, frame, frame), f32)],
            compiler_params=small,
            cost_estimate=pl.CostEstimate(flops=1 << 22, bytes_accessed=1 << 21, transcendentals=0),
            name="keep",
        )(spot_tiles, *back)

        def add_band(band, plane, refs):
            spot_ref, partner_ref, kept_ref, *spot_refs = refs[: 3 + ways]
            given, early, late = refs[3 + ways], refs[4 + ways : 6 + ways], refs[6 + ways : count]
            is_owner = place.section() == place.owner()
            straight, across = (
                jnp.where(is_owner, a[plane], b[plane]) for a, b in zip(early, late)
            )
            rep = place.rep()
            if ways == 1:
                straight_column, across_column = column_at(spot_refs[0]), column_at(partner_ref, 1)
            else:
                straight_column = jnp.where(rep == 1, column_at(spot_refs[0]), column_at(spot_refs[1]))
                across_column = jnp.where(
                    rep == 1, column_at(partner_ref, 1), column_at(partner_ref, 2)
                )
            total = part_of_band(kept_ref[plane], column_at(spot_ref), band)
            total += part_of_band(given[plane], column_at(partner_ref), band)
            strip = part_of_band(straight, straight_column, band)
            strip += part_of_band(across, across_column, band)
            gap = jnp.zeros((half_rows - HALO, HALO), f32)
            early, late = jnp.concatenate([strip, gap], 0), jnp.concatenate([gap, strip], 0)
            return total + jnp.where(rep == 1, late, early)

        pieces = (spot_tiles, spots_rep, kept, *spots_rows, given, *came_early, *came_late)
        piece_specs = [VMEM] * (8 + ways)
        count = len(piece_specs)

        def edge_kernel(*refs):
            for way in range(ways):
                for plane in range(2):
                    if ways == 1:
                        value = jnp.where(
                            place.column() == 0,
                            add_band(4, plane, refs),
                            add_band(0, plane, refs),
                        )
                    else:
                        value = add_band(4 * way, plane, refs)
                    refs[count + way][plane] = value

        leaving = pl.pallas_call(
            edge_kernel,
            out_shape=[sds((2, half_rows, HALO), f32)] * ways,
            in_specs=piece_specs,
            out_specs=[VMEM] * ways,
            compiler_params=small,
            name="edge_terms",
        )(*pieces)
        arrived = trade_columns(leaving)

        def inner_kernel(*refs):
            outs, inner, total, semaphores = refs[count : count + 2], *refs[count + 2 :]
            copies = Copies(semaphores)
            started = []
            for plane in range(2):
                bands = [add_band(band, plane, refs) for band in (1, 2, 3)]
                for number, value in enumerate(bands):
                    total[plane, :, number * HALO : (number + 1) * HALO] = value
                started.append(copies.start(total.at[plane], outs[plane]))
                for way in range(ways):
                    first = place.received(place.column(), way) == 0
                    inner[way, plane] = jnp.where(first, bands[0], bands[2])
            wait_for(started)

        *results, inner = pl.pallas_call(
            inner_kernel,
            out_shape=[sds((half_rows, width), f32)] * 2
            + [sds((ways, 2, half_rows, HALO), f32)],
            in_specs=piece_specs,
            out_specs=[HBM] * 2 + [VMEM],
            scratch_shapes=[
                pltpu.VMEM((2, half_rows, width), f32),
                pltpu.SemaphoreType.DMA((2,)),
            ],
            compiler_params=small,
            cost_estimate=pl.CostEstimate(flops=1 << 22, bytes_accessed=1 << 21, transcendentals=0),
            name="inner_terms",
        )(*pieces)

        def finish_kernel(phase_in, absorb_in, inner_ref, *refs):
            arrived_refs, outs = refs[:ways], refs[ways : ways + 2]
            strips, semaphores = refs[ways + 2 :]
            copies = Copies(semaphores)
            leaving = []
            for way in range(ways):
                start = place.received(place.column(), way) * (width - HALO)
                for plane in range(2):
                    strips[way, plane] = arrived_refs[way][plane] + inner_ref[way, plane]
                    target = outs[plane].at[:, pl.ds(pl.multiple_of(start, LANES), HALO)]
                    leaving.append(copies.start(strips.at[way, plane], target))
            wait_for(leaving)

        result = pl.pallas_call(
            finish_kernel,
            out_shape=[sds((half_rows, width), f32)] * 2,
            in_specs=[HBM, HBM, VMEM] + [VMEM] * ways,
            out_specs=[HBM] * 2,
            scratch_shapes=[
                pltpu.VMEM((ways, 2, half_rows, HALO), f32),
                pltpu.SemaphoreType.DMA((2 * ways,)),
            ],
            input_output_aliases={0: 0, 1: 1},
            compiler_params=small,
            name="finish",
        )(*results, inner, *arrived)
        return tuple(plane[None, None] for plane in result)

    in_specs = (
        P("section", "tile", None, None),
        P("section", "tile", None, None),
        P(),
        P("tile", "rep", None, None),
        P("tile", "rep", None, None, None),
    )
    out_specs = (P("section", "tile", "rep", None), P("section", "tile", "rep", None))
    return jax.shard_map(shards, mesh=mesh, in_specs=in_specs, out_specs=out_specs, check_vma=False)
```

```python
import math

import jax
import jax.numpy as jnp
import ml_dtypes
import numpy as np
from jax import lax
from jax.experimental import pallas as pl
from jax.experimental.pallas import tpu as pltpu
from jax.sharding import PartitionSpec as P

HALO = 128
LANES = 128
AXES = ("section", "tile", "rep")

dead_time = 0.1
background = 0.1
loss_weight = 0.1
fresnel = 0.5

f32 = jnp.float32
bf16 = jnp.bfloat16

SMEM = pl.BlockSpec(memory_space=pltpu.SMEM)
VMEM = pl.BlockSpec(memory_space=pltpu.VMEM)
HBM = pl.BlockSpec(memory_space=pltpu.HBM)


def two_parts(matrix):
    high = matrix.astype(ml_dtypes.bfloat16)
    low = (matrix - high.astype(np.float64)).astype(ml_dtypes.bfloat16)
    return np.stack([high, low])


def from_left(matrix):
    return np.block([[matrix.real, -matrix.imag], [matrix.imag, matrix.real]])


def from_right(matrix):
    return np.block([[matrix.real, matrix.imag], [-matrix.imag, matrix.real]])


def wave_tables(length):
    half = length // 2
    indices = np.arange(length)
    shifted = np.where(indices < half, indices, indices - length)
    kernel = np.exp(1j * math.pi * fresnel * shifted.astype(np.float64) ** 2 / length)
    spread = np.fft.ifft(kernel)
    circulant = spread[(indices[:, None] - indices[None, :]) % length]
    first, second = circulant[:half, :half], circulant[:half, half:]
    plus, minus = (first + second) / 2, (first - second) / 2
    near = [from_left(plus), from_left(minus), from_right(plus), from_right(minus)]
    turns = np.outer(indices[:half], indices[:half]) % half
    even = np.exp(-2j * math.pi * turns / half) / math.sqrt(length)
    odd = even * np.exp(-2j * math.pi * indices[:half] / length)[None, :]
    far = [from_left(even), from_left(odd), from_right(even.T), from_right(odd.T)]
    back = [from_left(even.T), from_left(odd.T), from_right(even), from_right(odd)]
    sort = np.zeros((length, length))
    sort[np.arange(half), 2 * np.arange(half)] = 1
    sort[half + np.arange(half), 2 * np.arange(half) + 1] = 1
    tables = np.stack([two_parts(m) for m in near + far + back])
    return tables, np.stack([sort, sort.T]).astype(ml_dtypes.bfloat16)


def fitted(function, degree):
    top = math.pi**2
    fit = np.polynomial.chebyshev.Chebyshev.interpolate(function, degree, domain=[0.0, top])
    return [float(c) for c in fit.convert(kind=np.polynomial.Polynomial).coef]


def sine_ratio(u):
    angle = np.sqrt(np.maximum(u, 1e-12))
    return np.sin(angle) / angle


SINE = fitted(sine_ratio, 8)
COSINE = fitted(lambda u: np.cos(np.sqrt(np.maximum(u, 0.0))), 8)


def polynomial(coefficients, u):
    total = jnp.full_like(u, coefficients[-1])
    for c in coefficients[-2::-1]:
        total = total * u + c
    return total


def cos_sin(angle):
    square = angle * angle
    return polynomial(COSINE, square), angle * polynomial(SINE, square)


def halves(value):
    high = value.astype(bf16)
    return high, (value - high.astype(f32)).astype(bf16)


def dot(a, b):
    return jnp.dot(a, b, preferred_element_type=f32)


def left_by(tables, index, value):
    high, low = halves(value)
    return dot(tables[index, 0], high) + dot(tables[index, 1], high) + dot(tables[index, 0], low)


def right_by(tables, index, value):
    high, low = halves(value)
    return dot(high, tables[index, 0]) + dot(high, tables[index, 1]) + dot(low, tables[index, 0])


def propagate(tables, at, re, im, fold, unfold):
    half = re.shape[0] // 2
    re0, re1, im0, im1 = re[:half], re[half:], im[:half], im[half:]
    if fold:
        re0, re1, im0, im1 = re0 + re1, re0 - re1, im0 + im1, im0 - im1
    first = left_by(tables, at, jnp.concatenate([re0, im0], 0))
    second = left_by(tables, at + 1, jnp.concatenate([re1, im1], 0))
    if unfold:
        first, second = first + second, first - second
    re = jnp.concatenate([first[:half], second[:half]], 0)
    im = jnp.concatenate([first[half:], second[half:]], 0)
    re0, re1, im0, im1 = re[:, :half], re[:, half:], im[:, :half], im[:, half:]
    if fold:
        re0, re1, im0, im1 = re0 + re1, re0 - re1, im0 + im1, im0 - im1
    first = right_by(tables, at + 2, jnp.concatenate([re0, im0], 1))
    second = right_by(tables, at + 3, jnp.concatenate([re1, im1], 1))
    if unfold:
        first, second = first + second, first - second
    re = jnp.concatenate([first[:, :half], second[:, :half]], 1)
    im = jnp.concatenate([first[:, half:], second[:, half:]], 1)
    return re, im


def near_field(tables, re, im):
    return propagate(tables, 0, re, im, True, True)


def far_field(tables, re, im):
    return propagate(tables, 4, re, im, True, False)


def far_back(tables, re, im):
    return propagate(tables, 8, re, im, False, True)


def likelihood_seed(far_re, far_im, observed):
    intensity = far_re * far_re + far_im * far_im
    shifted_total = intensity + background
    denominator = 1.0 + dead_time * shifted_total
    model_rate = shifted_total / denominator
    slope_term = loss_weight * (1.0 - observed / model_rate) / (denominator * denominator)
    return (2.0 * slope_term * far_re, 2.0 * slope_term * far_im)


def in_band(index, offset, band):
    cell = index + (band // 2) * (2 * HALO)
    return (cell >= offset) & (cell < offset + 2 * HALO)


def row_at(ref, number=0):
    return ref[2 * number, :1, :1]


def column_at(ref, number=0):
    return ref[2 * number + 1, :1, :1]


def lane_index(shape):
    return lax.broadcasted_iota(jnp.int32, shape, len(shape) - 1)


def row_index(shape):
    return lax.broadcasted_iota(jnp.int32, shape, len(shape) - 2)


def choose_columns(bands, offset):
    lane = lane_index(bands[1].shape)
    first = jnp.where(
        in_band(lane, offset, 0), bands[0], jnp.where(in_band(lane, offset, 2), bands[2], bands[4])
    )
    second = jnp.where(in_band(lane + HALO, offset, 1), bands[1], bands[3])
    return jnp.concatenate([first, second], 1)


def part_of_band(value, offset, band):
    start = (band % 2) * HALO
    half = value[:, start : start + HALO]
    return jnp.where(in_band(lane_index(half.shape) + start, offset, band), half, 0.0)


class Copies:
    def __init__(self, semaphores):
        self.semaphores = semaphores
        self.count = 0

    def start(self, source, target):
        copy = pltpu.make_async_copy(source, target, self.semaphores.at[self.count])
        self.count += 1
        copy.start()
        return copy


def wait_for(copies):
    for copy in copies:
        copy.wait()


class Place:
    def __init__(self, grid_side):
        self.grid_side = grid_side
        self.ways = 1 if grid_side == 2 else 2

    def section(self):
        return lax.axis_index("section")

    def rep(self):
        return lax.axis_index("rep")

    def row(self):
        return lax.axis_index("tile") // self.grid_side

    def column(self):
        return lax.axis_index("tile") % self.grid_side

    def owner(self):
        return 1 + self.column() % 2

    def sent(self, index, way):
        return 1 - index if self.ways == 1 else way

    def received(self, index, way):
        return 1 - index if self.ways == 1 else 1 - way


def solution(mesh):
    sections, tiles, reps = (mesh.shape[a] for a in AXES)
    grid_side = math.isqrt(tiles)
    place = Place(grid_side)
    ways = place.ways

    def everywhere(target_of):
        pairs = []
        for s in range(sections):
            for t in range(tiles):
                for r in range(reps):
                    target = target_of(s, t // grid_side, t % grid_side, r)
                    if target is None:
                        continue
                    ts, ty, tx, tr = target
                    if not (0 <= ty < grid_side and 0 <= tx < grid_side):
                        continue
                    pairs.append(
                        ((s * tiles + t) * reps + r, (ts * tiles + ty * grid_side + tx) * reps + tr)
                    )
        return pairs

    def move(value, target_of):
        return lax.ppermute(value, AXES, everywhere(target_of))

    def trade_rows(values):
        if ways == 1:
            return [move(values[0], lambda s, y, x, r: (s, 1 - y, x, r))]
        return [
            move(values[0], lambda s, y, x, r: (s, y - 1, x, r)),
            move(values[1], lambda s, y, x, r: (s, y + 1, x, r)),
        ]

    def trade_columns(values):
        if ways == 1:
            return [move(values[0], lambda s, y, x, r: (s, y, 1 - x, r))]
        return [
            move(values[0], lambda s, y, x, r: (s, y, x - 1, r)),
            move(values[1], lambda s, y, x, r: (s, y, x + 1, r)),
        ]

    def owner_of(x):
        return 1 + x % 2

    def near_of(x):
        return 3 * (x % 2)

    def middle_of(x):
        return 3 - owner_of(x)

    def far_of(x):
        return 3 - near_of(x)

    def shards(phase_shift, absorption, probe_wave, positions, counts):
        width = phase_shift.shape[2]
        frame = probe_wave.shape[1]
        half_rows = width // reps
        phase = phase_shift.reshape(width, width)
        absorb = absorption.reshape(width, width)
        spot = positions.reshape(1, 2)
        def tiles_of(spots):
            return jnp.broadcast_to(spots.reshape(-1, 1, 1), (spots.size, 8, LANES))

        spot_tiles = tiles_of(spot)
        observed = counts.reshape(frame, frame)
        sds = jax.ShapeDtypeStruct
        small = pltpu.CompilerParams(vmem_limit_bytes=8 << 20)

        spots_rows = [tiles_of(spots) for spots in trade_rows([spot] * ways)]
        tile = jnp.stack([phase, absorb])

        def load_kernel(tile, *edges):
            for way in range(ways):
                start = place.sent(place.column(), way) * (width - HALO)
                columns = pl.ds(pl.multiple_of(start, LANES), HALO)
                for plane in range(2):
                    edges[plane * ways + way][...] = tile[plane, :, columns]

        edges = pl.pallas_call(
            load_kernel,
            out_shape=[sds((width, HALO), f32)] * (2 * ways),
            in_specs=[VMEM],
            out_specs=[VMEM] * (2 * ways),
            compiler_params=small,
            name="edges",
        )(tile)
        phase_edges, absorb_edges = edges[:ways], edges[ways:]
        absorb_edges, spots_rows = lax.optimization_barrier((absorb_edges, spots_rows))
        sides = trade_columns(phase_edges) + trade_columns(absorb_edges)

        def rows_of(refs, plane, rows):
            sides_here = refs[1 + plane * ways : 1 + (plane + 1) * ways]
            return refs[0][plane, rows, :], [side[rows, :] for side in sides_here]

        def bands_of(tile, margin):
            inner = [tile[:, i * HALO : (i + 1) * HALO] for i in range(3)]
            ends = []
            for side in range(2):
                if ways == 1:
                    there = place.received(place.column(), 0) == side
                    ends.append(jnp.where(there, margin[0], 0.0))
                else:
                    there = place.column() > 0 if side == 0 else place.column() < grid_side - 1
                    ends.append(jnp.where(there, margin[1 - side], 0.0))
            return [ends[0], *inner, ends[1]]

        def transmission(angle, loss):
            cosine, sine = cos_sin(angle)
            damping = jnp.exp(-loss)
            return damping * cosine, damping * sine

        def strip_kernel(*refs):
            loaded, spot_refs = refs[: 1 + 2 * ways], refs[1 + 2 * ways : 1 + 3 * ways]
            outs = refs[1 + 3 * ways :]
            for way in range(ways):
                below = place.sent(place.row(), way)
                rows = pl.ds(pl.multiple_of(below * (width - HALO), 8), HALO)
                column = column_at(spot_refs[way if ways == 1 else 1 - way])
                cut = [
                    choose_columns(bands_of(*rows_of(loaded, plane, rows)), column)
                    for plane in range(2)
                ]
                outs[way][0], outs[way][1] = transmission(*cut)

        strips = pl.pallas_call(
            strip_kernel,
            out_shape=[sds((2, HALO, frame), f32)] * ways,
            in_specs=[VMEM] * (1 + 3 * ways),
            out_specs=[VMEM] * ways,
            compiler_params=small,
            name="halo_rows",
        )(tile, *sides, *spots_rows)
        rims = trade_rows(strips)

        def window_kernel(spot_ref, *refs):
            loaded, (whole, part) = refs[:-2], refs[-2:]
            row, column = row_at(spot_ref), column_at(spot_ref)
            index = row_index((HALO, HALO))
            upper = in_band(index + HALO, row, 1)
            planes = []
            for plane in range(2):
                first = bands_of(*rows_of(loaded, plane, slice(0, HALO)))
                third = bands_of(*rows_of(loaded, plane, slice(2 * HALO, 3 * HALO)))
                bands = [jnp.where(upper, v, w) for v, w in zip(first, third)]
                planes.append(choose_columns(bands, column))
            whole[0], whole[1] = transmission(*planes)
            planes = []
            for plane in range(2):
                bands = bands_of(*rows_of(loaded, plane, slice(HALO, 2 * HALO)))
                planes.append(choose_columns(bands, column))
            real, imag = transmission(*planes)
            inside = in_band(row_index((HALO, frame)), row, 2)
            part[0], part[1] = jnp.where(inside, real, 1.0), jnp.where(inside, imag, 0.0)

        whole, part = pl.pallas_call(
            window_kernel,
            out_shape=[sds((2, HALO, frame), f32)] * 2,
            in_specs=[VMEM] * (2 + 2 * ways),
            out_specs=[VMEM] * 2,
            compiler_params=small,
            name="window",
        )(spot_tiles, tile, *sides)

        def to_owner(value):
            return [
                move(
                    value,
                    lambda s, y, x, r: (owner_of(x), y, x, r) if s == section_of(x) else None,
                )
                for section_of in (near_of, middle_of, far_of)
            ]

        wholes = to_owner(whole)

        def join_kernel(spot_ref, part_ref, *refs):
            rim_refs, out = refs[:ways], refs[ways]
            row = row_at(spot_ref)
            index = row_index((HALO, frame))
            out[...] = part_ref[...]
            for way in range(ways):
                side = place.received(place.row(), way)
                there = jnp.where(side == 0, place.row() > 0, place.row() < grid_side - 1)
                shifted = index + jnp.where(side == 0, 0, 2 * (2 * HALO))
                near = (shifted >= row) & (shifted < row + jnp.where(there, 2 * HALO, 0))
                for plane in range(2):
                    out[plane] = jnp.where(near, rim_refs[way][plane], out[plane])

        joined = pl.pallas_call(
            join_kernel,
            out_shape=sds((2, HALO, frame), f32),
            in_specs=[VMEM] * (2 + ways),
            out_specs=VMEM,
            compiler_params=small,
            name="join",
        )(spot_tiles, part, *rims)
        joined, probe_late = lax.optimization_barrier((joined, probe_wave))
        joineds = to_owner(joined)

        tables, sort = wave_tables(frame)

        def prepare_kernel(spot_ref, probe, seen, sort, rolled, counted):
            row, column = lax.rem(spot_ref[0, 0], frame), lax.rem(spot_ref[0, 1], frame)
            for plane in range(2):
                rolled[plane] = pltpu.roll(pltpu.roll(probe[plane], row, 0), column, 1)
            first = dot(sort[0], seen[...].astype(f32).astype(bf16)).astype(bf16)
            counted[...] = dot(first, sort[1])

        rolled, counted = pl.pallas_call(
            prepare_kernel,
            out_shape=[sds((2, frame, frame), f32), sds((frame, frame), f32)],
            in_specs=[SMEM] + [VMEM] * 3,
            out_specs=[VMEM] * 2,
            compiler_params=small,
            name="prepare",
        )(spot, probe_late, observed, sort)
        places, counted = lax.optimization_barrier(
            (jnp.concatenate([spot_tiles] + spots_rows, 0), counted)
        )
        spots_rep = move(places, lambda s, y, x, r: (s, y, x, 1 - r))

        def frame_kernel(partner_ref, probe, seen, tables, *refs):
            whole_refs, joined_refs, outs = refs[:4], refs[4:8], refs[8:12]
            fields, exits = refs[12:]
            own_is_second = place.owner() == 1
            far, middle, own, near = zip(joined_refs[::-1], whole_refs)
            choices = ((near, far), (own, middle), (middle, own), (far, near))

            def field(number, plane):
                first, second = choices[number]
                return jnp.concatenate(
                    [jnp.where(own_is_second, a[plane], b[plane]) for a, b in zip(first, second)], 0
                )

            re, im = probe[0], probe[1]
            for number in range(4):
                o_re, o_im = field(number, 0), field(number, 1)
                fields[number, 0], fields[number, 1] = o_re, o_im
                exit_re, exit_im = o_re * re - o_im * im, o_re * im + o_im * re
                exits[number, 0], exits[number, 1] = exit_re, exit_im
                if number < 3:
                    re, im = near_field(tables, exit_re, exit_im)
            re, im = far_field(tables, exit_re, exit_im)
            re, im = likelihood_seed(re, im, seen[...])
            im = -im
            for number in reversed(range(4)):
                if number == 3:
                    re, im = far_back(tables, re, im)
                else:
                    re, im = near_field(tables, re, im)
                exit_re, exit_im = exits[number, 0], exits[number, 1]
                found = -(re * exit_im + im * exit_re), im * exit_im - re * exit_re
                if number > 0:
                    o_re, o_im = fields[number, 0], fields[number, 1]
                    re, im = o_re * re - o_im * im, o_re * im + o_im * re
                one, other = (0, 3) if number in (0, 3) else (1, 2)
                for plane, term in enumerate(found):
                    if number >= 2:
                        outs[one][plane] = term
                        outs[other][plane] = term
                    else:
                        kept_term = outs[one][plane]
                        outs[one][plane] = jnp.where(own_is_second, term, kept_term)
                        outs[other][plane] = jnp.where(own_is_second, kept_term, term)

        terms = pl.pallas_call(
            frame_kernel,
            out_shape=[sds((2, frame, frame), f32)] * 4,
            in_specs=[VMEM] * 12,
            out_specs=[VMEM] * 4,
            scratch_shapes=[
                pltpu.VMEM((4, 2, frame, frame), f32),
                pltpu.VMEM((4, 2, frame, frame), f32),
            ],
            compiler_params=pltpu.CompilerParams(vmem_limit_bytes=16 << 20),
            name="frame",
        )(
            spots_rep, rolled, counted, tables,
            wholes[2], wholes[1], whole, wholes[0],
            joineds[0], joined, joineds[1], joineds[2],
        )

        def from_owner(value, section_of):
            return move(
                value,
                lambda s, y, x, r: (section_of(x), y, x, r) if s == owner_of(x) else None,
            )

        far_terms = from_owner(terms[3], far_of)
        back = (
            far_terms,
            from_owner(terms[0], near_of),
            from_owner(terms[2], middle_of),
            terms[1],
        )

        def load_term(refs, term):
            section, owner = place.section(), place.owner()
            near = 3 * (owner - 1)
            choice = jnp.where(
                section == 3 - near, 0, jnp.where(section == near, 1, jnp.where(section == owner, 3, 2))
            )
            for number, ref in enumerate(refs):

                @pl.when(choice == number)
                def _():
                    term[...] = ref[...]

        def rows_for(term, plane, row, rep):
            index = row_index((frame, frame))
            middle = jnp.where(in_band(index, row, 2), term[plane], 0.0)
            later = middle[HALO // 2 :]
            earlier = jnp.where(in_band(index, row, 0), term[plane], 0.0)
            earlier = jnp.concatenate([earlier[HALO:], middle[: HALO // 2]], 0)
            return jnp.where(rep == 0, earlier, later)

        def strips_of(term, plane, row):
            index = row_index((HALO, frame))
            first = term[plane, :HALO]
            bands = (in_band(index, row, band) for band in (0, 4))
            return [jnp.where(band, first, 0.0) for band in bands]

        def own_kernel(spot_ref, own, across):
            for plane in range(2):
                above, below = strips_of(own, plane, row_at(spot_ref))
                across[plane] = jnp.where(place.rep() == 1, below, above)

        def parts_kernel(spot_ref, *refs):
            back_refs, (give, straight, across, term) = refs[:4], refs[4:]
            load_term(back_refs, term)
            rep, row = place.rep(), row_at(spot_ref)
            for plane in range(2):
                give[plane] = rows_for(term, plane, row, 1 - rep)
                above, below = strips_of(term, plane, row)
                straight[plane] = jnp.where(rep == 1, above, below)
                across[plane] = jnp.where(rep == 1, below, above)

        routes = (
            lambda s, y, x, r: (s, y, x, 1 - r),
            lambda s, y, x, r: (s, y + 1 - 2 * r, x, r),
            lambda s, y, x, r: (s, y - 1 + 2 * r, x, 1 - r),
        )

        def exchange(value, number, owners=None):
            return move(
                value,
                lambda s, y, x, r: (
                    routes[number](s, y, x, r)
                    if owners is None or (s == owner_of(x)) == owners
                    else None
                ),
            )

        strip = sds((2, HALO, frame), f32)
        part_shapes = [sds((2, half_rows, frame), f32), strip, strip]
        own_across = pl.pallas_call(
            own_kernel,
            out_shape=strip,
            in_specs=[VMEM] * 2,
            out_specs=VMEM,
            compiler_params=small,
            name="own_parts",
        )(spot_tiles, terms[1])
        early_across = exchange(own_across, 2, True)
        give, straight, across = pl.pallas_call(
            parts_kernel,
            out_shape=part_shapes,
            in_specs=[VMEM] * 5,
            out_specs=[VMEM] * 3,
            scratch_shapes=[pltpu.VMEM((2, frame, frame), f32)],
            compiler_params=small,
            name="parts",
        )(spot_tiles, *back)
        given = exchange(give, 0)
        straight, across, early_across = lax.optimization_barrier((straight, across, early_across))
        came_straight, late_across = exchange(straight, 1), exchange(across, 2, False)

        def keep_kernel(spot_ref, *refs):
            back_refs, (mine, term) = refs[:4], refs[4:]
            load_term(back_refs, term)
            for plane in range(2):
                mine[plane] = rows_for(term, plane, row_at(spot_ref), place.rep())

        kept = pl.pallas_call(
            keep_kernel,
            out_shape=sds((2, half_rows, frame), f32),
            in_specs=[VMEM] * 5,
            out_specs=VMEM,
            scratch_shapes=[pltpu.VMEM((2, frame, frame), f32)],
            compiler_params=small,
            cost_estimate=pl.CostEstimate(flops=1 << 22, bytes_accessed=1 << 21, transcendentals=0),
            name="keep",
        )(spot_tiles, *back)

        def add_band(band, plane, refs):
            spot_ref, partner_ref, kept_ref, *spot_refs = refs[: 3 + ways]
            is_owner = place.section() == place.owner()
            given, straight, late, early = (ref[plane] for ref in refs[3 + ways : count])
            across = jnp.where(is_owner, early, late)
            rep = place.rep()
            if ways == 1:
                straight_column, across_column = column_at(spot_refs[0]), column_at(partner_ref, 1)
            else:
                straight_column = jnp.where(rep == 1, column_at(spot_refs[0]), column_at(spot_refs[1]))
                across_column = jnp.where(
                    rep == 1, column_at(partner_ref, 1), column_at(partner_ref, 2)
                )
            total = part_of_band(kept_ref[plane], column_at(spot_ref), band)
            total += part_of_band(given, column_at(partner_ref), band)
            strip = part_of_band(straight, straight_column, band)
            strip += part_of_band(across, across_column, band)
            gap = jnp.zeros((half_rows - HALO, HALO), f32)
            early, late = jnp.concatenate([strip, gap], 0), jnp.concatenate([gap, strip], 0)
            return total + jnp.where(rep == 1, late, early)

        pieces = (spot_tiles, spots_rep, kept, *spots_rows, given, came_straight, late_across, early_across)
        piece_specs = [VMEM] * len(pieces)
        count = len(piece_specs)

        def edge_kernel(*refs):
            for way in range(ways):
                for plane in range(2):
                    if ways == 1:
                        value = jnp.where(
                            place.column() == 0,
                            add_band(4, plane, refs),
                            add_band(0, plane, refs),
                        )
                    else:
                        value = add_band(4 * way, plane, refs)
                    refs[count + way][plane] = value

        leaving = pl.pallas_call(
            edge_kernel,
            out_shape=[sds((2, half_rows, HALO), f32)] * ways,
            in_specs=piece_specs,
            out_specs=[VMEM] * ways,
            compiler_params=small,
            name="edge_terms",
        )(*pieces)
        arrived = trade_columns(leaving)

        def inner_kernel(*refs):
            outs, inner, total, semaphores = refs[count : count + 2], *refs[count + 2 :]
            copies = Copies(semaphores)
            started = []
            for plane in range(2):
                bands = [add_band(band, plane, refs) for band in (1, 2, 3)]
                for number, value in enumerate(bands):
                    total[plane, :, number * HALO : (number + 1) * HALO] = value
                started.append(copies.start(total.at[plane], outs[plane]))
                for way in range(ways):
                    first = place.received(place.column(), way) == 0
                    inner[way, plane] = jnp.where(first, bands[0], bands[2])
            wait_for(started)

        *results, inner = pl.pallas_call(
            inner_kernel,
            out_shape=[sds((half_rows, width), f32)] * 2
            + [sds((ways, 2, half_rows, HALO), f32)],
            in_specs=piece_specs,
            out_specs=[HBM] * 2 + [VMEM],
            scratch_shapes=[
                pltpu.VMEM((2, half_rows, width), f32),
                pltpu.SemaphoreType.DMA((2,)),
            ],
            compiler_params=small,
            cost_estimate=pl.CostEstimate(flops=1 << 22, bytes_accessed=1 << 21, transcendentals=0),
            name="inner_terms",
        )(*pieces)

        def finish_kernel(phase_in, absorb_in, inner_ref, *refs):
            arrived_refs, outs = refs[:ways], refs[ways : ways + 2]
            strips, semaphores = refs[ways + 2 :]
            copies = Copies(semaphores)
            leaving = []
            for way in range(ways):
                start = place.received(place.column(), way) * (width - HALO)
                for plane in range(2):
                    strips[way, plane] = arrived_refs[way][plane] + inner_ref[way, plane]
                    target = outs[plane].at[:, pl.ds(pl.multiple_of(start, LANES), HALO)]
                    leaving.append(copies.start(strips.at[way, plane], target))
            wait_for(leaving)

        result = pl.pallas_call(
            finish_kernel,
            out_shape=[sds((half_rows, width), f32)] * 2,
            in_specs=[HBM, HBM, VMEM] + [VMEM] * ways,
            out_specs=[HBM] * 2,
            scratch_shapes=[
                pltpu.VMEM((ways, 2, half_rows, HALO), f32),
                pltpu.SemaphoreType.DMA((2 * ways,)),
            ],
            input_output_aliases={0: 0, 1: 1},
            compiler_params=small,
            name="finish",
        )(*results, inner, *arrived)
        return tuple(plane[None, None] for plane in result)

    in_specs = (
        P("section", "tile", None, None),
        P("section", "tile", None, None),
        P(),
        P("tile", "rep", None, None),
        P("tile", "rep", None, None, None),
    )
    out_specs = (P("section", "tile", "rep", None), P("section", "tile", "rep", None))
    return jax.shard_map(shards, mesh=mesh, in_specs=in_specs, out_specs=out_specs, check_vma=False)
```

```python
import math

import jax
import jax.numpy as jnp
import ml_dtypes
import numpy as np
from jax import lax
from jax.experimental import pallas as pl
from jax.experimental.pallas import tpu as pltpu
from jax.sharding import PartitionSpec as P

HALO = 128
LANES = 128
AXES = ("section", "tile", "rep")

dead_time = 0.1
background = 0.1
loss_weight = 0.1
fresnel = 0.5

f32 = jnp.float32
bf16 = jnp.bfloat16

SMEM = pl.BlockSpec(memory_space=pltpu.SMEM)
VMEM = pl.BlockSpec(memory_space=pltpu.VMEM)
HBM = pl.BlockSpec(memory_space=pltpu.HBM)


def two_parts(matrix):
    high = matrix.astype(ml_dtypes.bfloat16)
    low = (matrix - high.astype(np.float64)).astype(ml_dtypes.bfloat16)
    return np.stack([high, low])


def from_left(matrix):
    return np.block([[matrix.real, -matrix.imag], [matrix.imag, matrix.real]])


def from_right(matrix):
    return np.block([[matrix.real, matrix.imag], [-matrix.imag, matrix.real]])


def wave_tables(length):
    half = length // 2
    indices = np.arange(length)
    shifted = np.where(indices < half, indices, indices - length)
    kernel = np.exp(1j * math.pi * fresnel * shifted.astype(np.float64) ** 2 / length)
    spread = np.fft.ifft(kernel)
    circulant = spread[(indices[:, None] - indices[None, :]) % length]
    first, second = circulant[:half, :half], circulant[:half, half:]
    plus, minus = (first + second) / 2, (first - second) / 2
    near = [from_left(plus), from_left(minus), from_right(plus), from_right(minus)]
    turns = np.outer(indices[:half], indices[:half]) % half
    even = np.exp(-2j * math.pi * turns / half) / math.sqrt(length)
    odd = even * np.exp(-2j * math.pi * indices[:half] / length)[None, :]
    far = [from_left(even), from_left(odd), from_right(even.T), from_right(odd.T)]
    back = [from_left(even.T), from_left(odd.T), from_right(even), from_right(odd)]
    sort = np.zeros((length, length))
    sort[np.arange(half), 2 * np.arange(half)] = 1
    sort[half + np.arange(half), 2 * np.arange(half) + 1] = 1
    tables = np.stack([two_parts(m) for m in near + far + back])
    return tables, np.stack([sort, sort.T]).astype(ml_dtypes.bfloat16)


def fitted(function, degree):
    top = math.pi**2
    fit = np.polynomial.chebyshev.Chebyshev.interpolate(function, degree, domain=[0.0, top])
    return [float(c) for c in fit.convert(kind=np.polynomial.Polynomial).coef]


def sine_ratio(u):
    angle = np.sqrt(np.maximum(u, 1e-12))
    return np.sin(angle) / angle


SINE = fitted(sine_ratio, 8)
COSINE = fitted(lambda u: np.cos(np.sqrt(np.maximum(u, 0.0))), 8)


def polynomial(coefficients, u):
    total = jnp.full_like(u, coefficients[-1])
    for c in coefficients[-2::-1]:
        total = total * u + c
    return total


def cos_sin(angle):
    square = angle * angle
    return polynomial(COSINE, square), angle * polynomial(SINE, square)


def halves(value):
    high = value.astype(bf16)
    return high, (value - high.astype(f32)).astype(bf16)


def dot(a, b):
    return jnp.dot(a, b, preferred_element_type=f32)


def left_by(tables, index, value):
    high, low = halves(value)
    return dot(tables[index, 0], high) + dot(tables[index, 1], high) + dot(tables[index, 0], low)


def right_by(tables, index, value):
    high, low = halves(value)
    return dot(high, tables[index, 0]) + dot(high, tables[index, 1]) + dot(low, tables[index, 0])


def propagate(tables, at, re, im, fold, unfold):
    half = re.shape[0] // 2
    re0, re1, im0, im1 = re[:half], re[half:], im[:half], im[half:]
    if fold:
        re0, re1, im0, im1 = re0 + re1, re0 - re1, im0 + im1, im0 - im1
    first = left_by(tables, at, jnp.concatenate([re0, im0], 0))
    second = left_by(tables, at + 1, jnp.concatenate([re1, im1], 0))
    if unfold:
        first, second = first + second, first - second
    re = jnp.concatenate([first[:half], second[:half]], 0)
    im = jnp.concatenate([first[half:], second[half:]], 0)
    re0, re1, im0, im1 = re[:, :half], re[:, half:], im[:, :half], im[:, half:]
    if fold:
        re0, re1, im0, im1 = re0 + re1, re0 - re1, im0 + im1, im0 - im1
    first = right_by(tables, at + 2, jnp.concatenate([re0, im0], 1))
    second = right_by(tables, at + 3, jnp.concatenate([re1, im1], 1))
    if unfold:
        first, second = first + second, first - second
    re = jnp.concatenate([first[:, :half], second[:, :half]], 1)
    im = jnp.concatenate([first[:, half:], second[:, half:]], 1)
    return re, im


def near_field(tables, re, im):
    return propagate(tables, 0, re, im, True, True)


def far_field(tables, re, im):
    return propagate(tables, 4, re, im, True, False)


def far_back(tables, re, im):
    return propagate(tables, 8, re, im, False, True)


def likelihood_seed(far_re, far_im, observed):
    intensity = far_re * far_re + far_im * far_im
    shifted_total = intensity + background
    denominator = 1.0 + dead_time * shifted_total
    model_rate = shifted_total / denominator
    slope_term = loss_weight * (1.0 - observed / model_rate) / (denominator * denominator)
    return (2.0 * slope_term * far_re, 2.0 * slope_term * far_im)


def in_band(index, offset, band):
    cell = index + (band // 2) * (2 * HALO)
    return (cell >= offset) & (cell < offset + 2 * HALO)


def row_at(ref, number=0):
    return ref[2 * number, :1, :1]


def column_at(ref, number=0):
    return ref[2 * number + 1, :1, :1]


def lane_index(shape):
    return lax.broadcasted_iota(jnp.int32, shape, len(shape) - 1)


def row_index(shape):
    return lax.broadcasted_iota(jnp.int32, shape, len(shape) - 2)


def choose_columns(bands, offset):
    lane = lane_index(bands[1].shape)
    first = jnp.where(
        in_band(lane, offset, 0), bands[0], jnp.where(in_band(lane, offset, 2), bands[2], bands[4])
    )
    second = jnp.where(in_band(lane + HALO, offset, 1), bands[1], bands[3])
    return jnp.concatenate([first, second], 1)


def part_of_band(value, offset, band):
    start = (band % 2) * HALO
    half = value[:, start : start + HALO]
    return jnp.where(in_band(lane_index(half.shape) + start, offset, band), half, 0.0)


class Copies:
    def __init__(self, semaphores):
        self.semaphores = semaphores
        self.count = 0

    def start(self, source, target):
        copy = pltpu.make_async_copy(source, target, self.semaphores.at[self.count])
        self.count += 1
        copy.start()
        return copy


def wait_for(copies):
    for copy in copies:
        copy.wait()


class Place:
    def __init__(self, grid_side):
        self.grid_side = grid_side
        self.ways = 1 if grid_side == 2 else 2

    def section(self):
        return lax.axis_index("section")

    def rep(self):
        return lax.axis_index("rep")

    def row(self):
        return lax.axis_index("tile") // self.grid_side

    def column(self):
        return lax.axis_index("tile") % self.grid_side

    def owner(self):
        return 1 + self.column() % 2

    def sent(self, index, way):
        return 1 - index if self.ways == 1 else way

    def received(self, index, way):
        return 1 - index if self.ways == 1 else 1 - way


def solution(mesh):
    sections, tiles, reps = (mesh.shape[a] for a in AXES)
    grid_side = math.isqrt(tiles)
    place = Place(grid_side)
    ways = place.ways

    def everywhere(target_of):
        pairs = []
        for s in range(sections):
            for t in range(tiles):
                for r in range(reps):
                    target = target_of(s, t // grid_side, t % grid_side, r)
                    if target is None:
                        continue
                    ts, ty, tx, tr = target
                    if not (0 <= ty < grid_side and 0 <= tx < grid_side):
                        continue
                    pairs.append(
                        ((s * tiles + t) * reps + r, (ts * tiles + ty * grid_side + tx) * reps + tr)
                    )
        return pairs

    def move(value, target_of):
        return lax.ppermute(value, AXES, everywhere(target_of))

    def trade_rows(values):
        if ways == 1:
            return [move(values[0], lambda s, y, x, r: (s, 1 - y, x, r))]
        return [
            move(values[0], lambda s, y, x, r: (s, y - 1, x, r)),
            move(values[1], lambda s, y, x, r: (s, y + 1, x, r)),
        ]

    def trade_columns(values):
        if ways == 1:
            return [move(values[0], lambda s, y, x, r: (s, y, 1 - x, r))]
        return [
            move(values[0], lambda s, y, x, r: (s, y, x - 1, r)),
            move(values[1], lambda s, y, x, r: (s, y, x + 1, r)),
        ]

    def owner_of(x):
        return 1 + x % 2

    def near_of(x):
        return 3 * (x % 2)

    def middle_of(x):
        return 3 - owner_of(x)

    def far_of(x):
        return 3 - near_of(x)

    def shards(phase_shift, absorption, probe_wave, positions, counts):
        width = phase_shift.shape[2]
        frame = probe_wave.shape[1]
        half_rows = width // reps
        phase = phase_shift.reshape(width, width)
        absorb = absorption.reshape(width, width)
        spot = positions.reshape(1, 2)
        def tiles_of(spots):
            return jnp.broadcast_to(spots.reshape(-1, 1, 1), (spots.size, 8, LANES))

        spot_tiles = tiles_of(spot)
        observed = counts.reshape(frame, frame)
        sds = jax.ShapeDtypeStruct
        small = pltpu.CompilerParams(vmem_limit_bytes=8 << 20)

        spots_rows = [tiles_of(spots) for spots in trade_rows([spot] * ways)]
        tile = jnp.stack([phase, absorb])

        def load_kernel(tile, *edges):
            for way in range(ways):
                start = place.sent(place.column(), way) * (width - HALO)
                columns = pl.ds(pl.multiple_of(start, LANES), HALO)
                for plane in range(2):
                    edges[plane * ways + way][...] = tile[plane, :, columns]

        edges = pl.pallas_call(
            load_kernel,
            out_shape=[sds((width, HALO), f32)] * (2 * ways),
            in_specs=[VMEM],
            out_specs=[VMEM] * (2 * ways),
            compiler_params=small,
            name="edges",
        )(tile)
        phase_edges, absorb_edges = edges[:ways], edges[ways:]
        absorb_edges, spots_rows = lax.optimization_barrier((absorb_edges, spots_rows))
        sides = trade_columns(phase_edges) + trade_columns(absorb_edges)

        def rows_of(refs, plane, rows):
            sides_here = refs[1 + plane * ways : 1 + (plane + 1) * ways]
            return refs[0][plane, rows, :], [side[rows, :] for side in sides_here]

        def bands_of(tile, margin):
            inner = [tile[:, i * HALO : (i + 1) * HALO] for i in range(3)]
            ends = []
            for side in range(2):
                if ways == 1:
                    there = place.received(place.column(), 0) == side
                    ends.append(jnp.where(there, margin[0], 0.0))
                else:
                    there = place.column() > 0 if side == 0 else place.column() < grid_side - 1
                    ends.append(jnp.where(there, margin[1 - side], 0.0))
            return [ends[0], *inner, ends[1]]

        def transmission(angle, loss):
            cosine, sine = cos_sin(angle)
            damping = jnp.exp(-loss)
            return damping * cosine, damping * sine

        def strip_kernel(*refs):
            loaded, spot_refs = refs[: 1 + 2 * ways], refs[1 + 2 * ways : 1 + 3 * ways]
            outs = refs[1 + 3 * ways :]
            for way in range(ways):
                below = place.sent(place.row(), way)
                rows = pl.ds(pl.multiple_of(below * (width - HALO), 8), HALO)
                column = column_at(spot_refs[way if ways == 1 else 1 - way])
                cut = [
                    choose_columns(bands_of(*rows_of(loaded, plane, rows)), column)
                    for plane in range(2)
                ]
                outs[way][0], outs[way][1] = transmission(*cut)

        strips = pl.pallas_call(
            strip_kernel,
            out_shape=[sds((2, HALO, frame), f32)] * ways,
            in_specs=[VMEM] * (1 + 3 * ways),
            out_specs=[VMEM] * ways,
            compiler_params=small,
            name="halo_rows",
        )(tile, *sides, *spots_rows)
        rims = trade_rows(strips)

        def window_kernel(spot_ref, *refs):
            *loaded, whole = refs
            row, column = row_at(spot_ref), column_at(spot_ref)
            index = row_index((HALO, HALO))
            upper = in_band(index + HALO, row, 1)
            planes = []
            for plane in range(2):
                first = bands_of(*rows_of(loaded, plane, slice(0, HALO)))
                third = bands_of(*rows_of(loaded, plane, slice(2 * HALO, 3 * HALO)))
                bands = [jnp.where(upper, v, w) for v, w in zip(first, third)]
                planes.append(choose_columns(bands, column))
            whole[0], whole[1] = transmission(*planes)

        def part_kernel(spot_ref, *refs):
            *loaded, part = refs
            row, column = row_at(spot_ref), column_at(spot_ref)
            planes = []
            for plane in range(2):
                bands = bands_of(*rows_of(loaded, plane, slice(HALO, 2 * HALO)))
                planes.append(choose_columns(bands, column))
            real, imag = transmission(*planes)
            inside = in_band(row_index((HALO, frame)), row, 2)
            part[0], part[1] = jnp.where(inside, real, 1.0), jnp.where(inside, imag, 0.0)

        def half_window(kernel, name):
            return pl.pallas_call(
                kernel,
                out_shape=sds((2, HALO, frame), f32),
                in_specs=[VMEM] * (2 + 2 * ways),
                out_specs=VMEM,
                compiler_params=small,
                name=name,
            )(spot_tiles, tile, *sides)

        whole, part = half_window(window_kernel, "window"), half_window(part_kernel, "part")

        def to_owner(value):
            return [
                move(
                    value,
                    lambda s, y, x, r: (owner_of(x), y, x, r) if s == section_of(x) else None,
                )
                for section_of in (near_of, middle_of, far_of)
            ]

        wholes = to_owner(whole)

        def join_kernel(spot_ref, part_ref, *refs):
            rim_refs, out = refs[:ways], refs[ways]
            row = row_at(spot_ref)
            index = row_index((HALO, frame))
            out[...] = part_ref[...]
            for way in range(ways):
                side = place.received(place.row(), way)
                there = jnp.where(side == 0, place.row() > 0, place.row() < grid_side - 1)
                shifted = index + jnp.where(side == 0, 0, 2 * (2 * HALO))
                near = (shifted >= row) & (shifted < row + jnp.where(there, 2 * HALO, 0))
                for plane in range(2):
                    out[plane] = jnp.where(near, rim_refs[way][plane], out[plane])

        joined = pl.pallas_call(
            join_kernel,
            out_shape=sds((2, HALO, frame), f32),
            in_specs=[VMEM] * (2 + ways),
            out_specs=VMEM,
            compiler_params=small,
            name="join",
        )(spot_tiles, part, *rims)
        joined, probe_late = lax.optimization_barrier((joined, probe_wave))
        joineds = to_owner(joined)

        tables, sort = wave_tables(frame)

        def prepare_kernel(spot_ref, probe, seen, sort, rolled, counted):
            row, column = lax.rem(spot_ref[0, 0], frame), lax.rem(spot_ref[0, 1], frame)
            for plane in range(2):
                rolled[plane] = pltpu.roll(pltpu.roll(probe[plane], row, 0), column, 1)
            first = dot(sort[0], seen[...].astype(f32).astype(bf16)).astype(bf16)
            counted[...] = dot(first, sort[1])

        rolled, counted = pl.pallas_call(
            prepare_kernel,
            out_shape=[sds((2, frame, frame), f32), sds((frame, frame), f32)],
            in_specs=[SMEM] + [VMEM] * 3,
            out_specs=[VMEM] * 2,
            compiler_params=small,
            name="prepare",
        )(spot, probe_late, observed, sort)
        places, counted = lax.optimization_barrier(
            (jnp.concatenate([spot_tiles] + spots_rows, 0), counted)
        )
        spots_rep = move(places, lambda s, y, x, r: (s, y, x, 1 - r))

        def frame_kernel(partner_ref, probe, seen, tables, *refs):
            whole_refs, joined_refs, outs = refs[:4], refs[4:8], refs[8:12]
            fields, exits = refs[12:]
            own_is_second = place.owner() == 1
            far, middle, own, near = zip(joined_refs[::-1], whole_refs)
            choices = ((near, far), (own, middle), (middle, own), (far, near))

            def field(number, plane):
                first, second = choices[number]
                return jnp.concatenate(
                    [jnp.where(own_is_second, a[plane], b[plane]) for a, b in zip(first, second)], 0
                )

            re, im = probe[0], probe[1]
            for number in range(4):
                o_re, o_im = field(number, 0), field(number, 1)
                fields[number, 0], fields[number, 1] = o_re, o_im
                exit_re, exit_im = o_re * re - o_im * im, o_re * im + o_im * re
                exits[number, 0], exits[number, 1] = exit_re, exit_im
                if number < 3:
                    re, im = near_field(tables, exit_re, exit_im)
            re, im = far_field(tables, exit_re, exit_im)
            re, im = likelihood_seed(re, im, seen[...])
            im = -im
            for number in reversed(range(4)):
                if number == 3:
                    re, im = far_back(tables, re, im)
                else:
                    re, im = near_field(tables, re, im)
                exit_re, exit_im = exits[number, 0], exits[number, 1]
                found = -(re * exit_im + im * exit_re), im * exit_im - re * exit_re
                if number > 0:
                    o_re, o_im = fields[number, 0], fields[number, 1]
                    re, im = o_re * re - o_im * im, o_re * im + o_im * re
                one, other = (0, 3) if number in (0, 3) else (1, 2)
                for plane, term in enumerate(found):
                    if number >= 2:
                        outs[one][plane] = term
                        outs[other][plane] = term
                    else:
                        kept_term = outs[one][plane]
                        outs[one][plane] = jnp.where(own_is_second, term, kept_term)
                        outs[other][plane] = jnp.where(own_is_second, kept_term, term)

        terms = pl.pallas_call(
            frame_kernel,
            out_shape=[sds((2, frame, frame), f32)] * 4,
            in_specs=[VMEM] * 12,
            out_specs=[VMEM] * 4,
            scratch_shapes=[
                pltpu.VMEM((4, 2, frame, frame), f32),
                pltpu.VMEM((4, 2, frame, frame), f32),
            ],
            compiler_params=pltpu.CompilerParams(vmem_limit_bytes=16 << 20),
            name="frame",
        )(
            spots_rep, rolled, counted, tables,
            wholes[2], wholes[1], whole, wholes[0],
            joineds[0], joined, joineds[1], joineds[2],
        )

        def from_owner(value, section_of):
            return move(
                value,
                lambda s, y, x, r: (section_of(x), y, x, r) if s == owner_of(x) else None,
            )

        far_terms = from_owner(terms[3], far_of)
        back = (
            far_terms,
            from_owner(terms[0], near_of),
            from_owner(terms[2], middle_of),
            terms[1],
        )

        def load_term(refs, term):
            section, owner = place.section(), place.owner()
            near = 3 * (owner - 1)
            choice = jnp.where(
                section == 3 - near, 0, jnp.where(section == near, 1, jnp.where(section == owner, 3, 2))
            )
            for number, ref in enumerate(refs):

                @pl.when(choice == number)
                def _():
                    term[...] = ref[...]

        def rows_for(term, plane, row, rep):
            index = row_index((frame, frame))
            middle = jnp.where(in_band(index, row, 2), term[plane], 0.0)
            later = middle[HALO // 2 :]
            earlier = jnp.where(in_band(index, row, 0), term[plane], 0.0)
            earlier = jnp.concatenate([earlier[HALO:], middle[: HALO // 2]], 0)
            return jnp.where(rep == 0, earlier, later)

        def strips_of(term, plane, row):
            index = row_index((HALO, frame))
            first = term[plane, :HALO]
            bands = (in_band(index, row, band) for band in (0, 4))
            return [jnp.where(band, first, 0.0) for band in bands]

        def own_kernel(spot_ref, own, across):
            for plane in range(2):
                above, below = strips_of(own, plane, row_at(spot_ref))
                across[plane] = jnp.where(place.rep() == 1, below, above)

        def parts_kernel(spot_ref, *refs):
            back_refs, (give, straight, across, term) = refs[:4], refs[4:]
            load_term(back_refs, term)
            rep, row = place.rep(), row_at(spot_ref)
            for plane in range(2):
                give[plane] = rows_for(term, plane, row, 1 - rep)
                above, below = strips_of(term, plane, row)
                straight[plane] = jnp.where(rep == 1, above, below)
                across[plane] = jnp.where(rep == 1, below, above)

        routes = (
            lambda s, y, x, r: (s, y, x, 1 - r),
            lambda s, y, x, r: (s, y + 1 - 2 * r, x, r),
            lambda s, y, x, r: (s, y - 1 + 2 * r, x, 1 - r),
        )

        def exchange(value, number, owners=None):
            return move(
                value,
                lambda s, y, x, r: (
                    routes[number](s, y, x, r)
                    if owners is None or (s == owner_of(x)) == owners
                    else None
                ),
            )

        strip = sds((2, HALO, frame), f32)
        part_shapes = [sds((2, half_rows, frame), f32), strip, strip]
        own_across = pl.pallas_call(
            own_kernel,
            out_shape=strip,
            in_specs=[VMEM] * 2,
            out_specs=VMEM,
            compiler_params=small,
            name="own_parts",
        )(spot_tiles, terms[1])
        early_across = exchange(own_across, 2, True)
        give, straight, across = pl.pallas_call(
            parts_kernel,
            out_shape=part_shapes,
            in_specs=[VMEM] * 5,
            out_specs=[VMEM] * 3,
            scratch_shapes=[pltpu.VMEM((2, frame, frame), f32)],
            compiler_params=small,
            name="parts",
        )(spot_tiles, *back)
        given = exchange(give, 0)
        straight, across, early_across = lax.optimization_barrier((straight, across, early_across))
        came_straight, late_across = exchange(straight, 1), exchange(across, 2, False)

        def keep_kernel(spot_ref, *refs):
            back_refs, (mine, term) = refs[:4], refs[4:]
            load_term(back_refs, term)
            for plane in range(2):
                mine[plane] = rows_for(term, plane, row_at(spot_ref), place.rep())

        kept = pl.pallas_call(
            keep_kernel,
            out_shape=sds((2, half_rows, frame), f32),
            in_specs=[VMEM] * 5,
            out_specs=VMEM,
            scratch_shapes=[pltpu.VMEM((2, frame, frame), f32)],
            compiler_params=small,
            cost_estimate=pl.CostEstimate(flops=1 << 22, bytes_accessed=1 << 21, transcendentals=0),
            name="keep",
        )(spot_tiles, *back)

        def add_band(band, plane, refs):
            spot_ref, partner_ref, kept_ref, *spot_refs = refs[: 3 + ways]
            is_owner = place.section() == place.owner()
            given, straight, late, early = (ref[plane] for ref in refs[3 + ways : count])
            across = jnp.where(is_owner, early, late)
            rep = place.rep()
            if ways == 1:
                straight_column, across_column = column_at(spot_refs[0]), column_at(partner_ref, 1)
            else:
                straight_column = jnp.where(rep == 1, column_at(spot_refs[0]), column_at(spot_refs[1]))
                across_column = jnp.where(
                    rep == 1, column_at(partner_ref, 1), column_at(partner_ref, 2)
                )
            total = part_of_band(kept_ref[plane], column_at(spot_ref), band)
            total += part_of_band(given, column_at(partner_ref), band)
            strip = part_of_band(straight, straight_column, band)
            strip += part_of_band(across, across_column, band)
            gap = jnp.zeros((half_rows - HALO, HALO), f32)
            early, late = jnp.concatenate([strip, gap], 0), jnp.concatenate([gap, strip], 0)
            return total + jnp.where(rep == 1, late, early)

        pieces = (spot_tiles, spots_rep, kept, *spots_rows, given, came_straight, late_across, early_across)
        piece_specs = [VMEM] * len(pieces)
        count = len(piece_specs)

        def edge_kernel(*refs):
            for way in range(ways):
                for plane in range(2):
                    if ways == 1:
                        value = jnp.where(
                            place.column() == 0,
                            add_band(4, plane, refs),
                            add_band(0, plane, refs),
                        )
                    else:
                        value = add_band(4 * way, plane, refs)
                    refs[count + way][plane] = value

        leaving = pl.pallas_call(
            edge_kernel,
            out_shape=[sds((2, half_rows, HALO), f32)] * ways,
            in_specs=piece_specs,
            out_specs=[VMEM] * ways,
            compiler_params=small,
            name="edge_terms",
        )(*pieces)
        arrived = trade_columns(leaving)

        def inner_kernel(*refs):
            outs, inner, total, semaphores = refs[count : count + 2], *refs[count + 2 :]
            copies = Copies(semaphores)
            started = []
            for plane in range(2):
                bands = [add_band(band, plane, refs) for band in (1, 2, 3)]
                for number, value in enumerate(bands):
                    total[plane, :, number * HALO : (number + 1) * HALO] = value
                started.append(copies.start(total.at[plane], outs[plane]))
                for way in range(ways):
                    first = place.received(place.column(), way) == 0
                    inner[way, plane] = jnp.where(first, bands[0], bands[2])
            wait_for(started)

        *results, inner = pl.pallas_call(
            inner_kernel,
            out_shape=[sds((half_rows, width), f32)] * 2
            + [sds((ways, 2, half_rows, HALO), f32)],
            in_specs=piece_specs,
            out_specs=[HBM] * 2 + [VMEM],
            scratch_shapes=[
                pltpu.VMEM((2, half_rows, width), f32),
                pltpu.SemaphoreType.DMA((2,)),
            ],
            compiler_params=small,
            cost_estimate=pl.CostEstimate(flops=1 << 22, bytes_accessed=1 << 21, transcendentals=0),
            name="inner_terms",
        )(*pieces)

        def finish_kernel(phase_in, absorb_in, inner_ref, *refs):
            arrived_refs, outs = refs[:ways], refs[ways : ways + 2]
            strips, semaphores = refs[ways + 2 :]
            copies = Copies(semaphores)
            leaving = []
            for way in range(ways):
                start = place.received(place.column(), way) * (width - HALO)
                for plane in range(2):
                    strips[way, plane] = arrived_refs[way][plane] + inner_ref[way, plane]
                    target = outs[plane].at[:, pl.ds(pl.multiple_of(start, LANES), HALO)]
                    leaving.append(copies.start(strips.at[way, plane], target))
            wait_for(leaving)

        result = pl.pallas_call(
            finish_kernel,
            out_shape=[sds((half_rows, width), f32)] * 2,
            in_specs=[HBM, HBM, VMEM] + [VMEM] * ways,
            out_specs=[HBM] * 2,
            scratch_shapes=[
                pltpu.VMEM((ways, 2, half_rows, HALO), f32),
                pltpu.SemaphoreType.DMA((2 * ways,)),
            ],
            input_output_aliases={0: 0, 1: 1},
            compiler_params=small,
            name="finish",
        )(*results, inner, *arrived)
        return tuple(plane[None, None] for plane in result)

    in_specs = (
        P("section", "tile", None, None),
        P("section", "tile", None, None),
        P(),
        P("tile", "rep", None, None),
        P("tile", "rep", None, None, None),
    )
    out_specs = (P("section", "tile", "rep", None), P("section", "tile", "rep", None))
    return jax.shard_map(shards, mesh=mesh, in_specs=in_specs, out_specs=out_specs, check_vma=False)
```

```python
import math

import jax
import jax.numpy as jnp
import ml_dtypes
import numpy as np
from jax import lax
from jax.experimental import pallas as pl
from jax.experimental.pallas import tpu as pltpu
from jax.sharding import PartitionSpec as P

HALO = 128
LANES = 128
AXES = ("section", "tile", "rep")

dead_time = 0.1
background = 0.1
loss_weight = 0.1
fresnel = 0.5

f32 = jnp.float32
bf16 = jnp.bfloat16

SMEM = pl.BlockSpec(memory_space=pltpu.SMEM)
VMEM = pl.BlockSpec(memory_space=pltpu.VMEM)
HBM = pl.BlockSpec(memory_space=pltpu.HBM)


def two_parts(matrix):
    high = matrix.astype(ml_dtypes.bfloat16)
    low = (matrix - high.astype(np.float64)).astype(ml_dtypes.bfloat16)
    return np.stack([high, low])


def from_left(matrix):
    return np.block([[matrix.real, -matrix.imag], [matrix.imag, matrix.real]])


def from_right(matrix):
    return np.block([[matrix.real, matrix.imag], [-matrix.imag, matrix.real]])


def wave_tables(length):
    half = length // 2
    indices = np.arange(length)
    shifted = np.where(indices < half, indices, indices - length)
    kernel = np.exp(1j * math.pi * fresnel * shifted.astype(np.float64) ** 2 / length)
    spread = np.fft.ifft(kernel)
    circulant = spread[(indices[:, None] - indices[None, :]) % length]
    first, second = circulant[:half, :half], circulant[:half, half:]
    plus, minus = (first + second) / 2, (first - second) / 2
    near = [from_left(plus), from_left(minus), from_right(plus), from_right(minus)]
    turns = np.outer(indices[:half], indices[:half]) % half
    even = np.exp(-2j * math.pi * turns / half) / math.sqrt(length)
    odd = even * np.exp(-2j * math.pi * indices[:half] / length)[None, :]
    far = [from_left(even), from_left(odd), from_right(even.T), from_right(odd.T)]
    back = [from_left(even.T), from_left(odd.T), from_right(even), from_right(odd)]
    sort = np.zeros((length, length))
    sort[np.arange(half), 2 * np.arange(half)] = 1
    sort[half + np.arange(half), 2 * np.arange(half) + 1] = 1
    tables = np.stack([two_parts(m) for m in near + far + back])
    return tables, np.stack([sort, sort.T]).astype(ml_dtypes.bfloat16)


def fitted(function, degree):
    top = math.pi**2
    fit = np.polynomial.chebyshev.Chebyshev.interpolate(function, degree, domain=[0.0, top])
    return [float(c) for c in fit.convert(kind=np.polynomial.Polynomial).coef]


def sine_ratio(u):
    angle = np.sqrt(np.maximum(u, 1e-12))
    return np.sin(angle) / angle


SINE = fitted(sine_ratio, 8)
COSINE = fitted(lambda u: np.cos(np.sqrt(np.maximum(u, 0.0))), 8)


def polynomial(coefficients, u):
    total = jnp.full_like(u, coefficients[-1])
    for c in coefficients[-2::-1]:
        total = total * u + c
    return total


def cos_sin(angle):
    square = angle * angle
    return polynomial(COSINE, square), angle * polynomial(SINE, square)


def halves(value):
    high = value.astype(bf16)
    return high, (value - high.astype(f32)).astype(bf16)


def dot(a, b):
    return jnp.dot(a, b, preferred_element_type=f32)


def left_by(tables, index, value):
    high, low = halves(value)
    return dot(tables[index, 0], high) + dot(tables[index, 1], high) + dot(tables[index, 0], low)


def right_by(tables, index, value):
    high, low = halves(value)
    return dot(high, tables[index, 0]) + dot(high, tables[index, 1]) + dot(low, tables[index, 0])


def propagate(tables, at, re, im, fold, unfold):
    half = re.shape[0] // 2
    re0, re1, im0, im1 = re[:half], re[half:], im[:half], im[half:]
    if fold:
        re0, re1, im0, im1 = re0 + re1, re0 - re1, im0 + im1, im0 - im1
    first = left_by(tables, at, jnp.concatenate([re0, im0], 0))
    second = left_by(tables, at + 1, jnp.concatenate([re1, im1], 0))
    if unfold:
        first, second = first + second, first - second
    re = jnp.concatenate([first[:half], second[:half]], 0)
    im = jnp.concatenate([first[half:], second[half:]], 0)
    re0, re1, im0, im1 = re[:, :half], re[:, half:], im[:, :half], im[:, half:]
    if fold:
        re0, re1, im0, im1 = re0 + re1, re0 - re1, im0 + im1, im0 - im1
    first = right_by(tables, at + 2, jnp.concatenate([re0, im0], 1))
    second = right_by(tables, at + 3, jnp.concatenate([re1, im1], 1))
    if unfold:
        first, second = first + second, first - second
    re = jnp.concatenate([first[:, :half], second[:, :half]], 1)
    im = jnp.concatenate([first[:, half:], second[:, half:]], 1)
    return re, im


def near_field(tables, re, im):
    return propagate(tables, 0, re, im, True, True)


def far_field(tables, re, im):
    return propagate(tables, 4, re, im, True, False)


def far_back(tables, re, im):
    return propagate(tables, 8, re, im, False, True)


def likelihood_seed(far_re, far_im, observed):
    intensity = far_re * far_re + far_im * far_im
    shifted_total = intensity + background
    denominator = 1.0 + dead_time * shifted_total
    model_rate = shifted_total / denominator
    slope_term = loss_weight * (1.0 - observed / model_rate) / (denominator * denominator)
    return (2.0 * slope_term * far_re, 2.0 * slope_term * far_im)


def in_band(index, offset, band):
    cell = index + (band // 2) * (2 * HALO)
    return (cell >= offset) & (cell < offset + 2 * HALO)


def row_at(ref, number=0):
    return ref[2 * number, :1, :1]


def column_at(ref, number=0):
    return ref[2 * number + 1, :1, :1]


def lane_index(shape):
    return lax.broadcasted_iota(jnp.int32, shape, len(shape) - 1)


def row_index(shape):
    return lax.broadcasted_iota(jnp.int32, shape, len(shape) - 2)


def choose_columns(bands, offset):
    lane = lane_index(bands[1].shape)
    first = jnp.where(
        in_band(lane, offset, 0), bands[0], jnp.where(in_band(lane, offset, 2), bands[2], bands[4])
    )
    second = jnp.where(in_band(lane + HALO, offset, 1), bands[1], bands[3])
    return jnp.concatenate([first, second], 1)


def part_of_band(value, offset, band):
    start = (band % 2) * HALO
    half = value[:, start : start + HALO]
    return jnp.where(in_band(lane_index(half.shape) + start, offset, band), half, 0.0)


class Copies:
    def __init__(self, semaphores):
        self.semaphores = semaphores
        self.count = 0

    def start(self, source, target):
        copy = pltpu.make_async_copy(source, target, self.semaphores.at[self.count])
        self.count += 1
        copy.start()
        return copy


def wait_for(copies):
    for copy in copies:
        copy.wait()


class Place:
    def __init__(self, grid_side):
        self.grid_side = grid_side
        self.ways = 1 if grid_side == 2 else 2

    def section(self):
        return lax.axis_index("section")

    def rep(self):
        return lax.axis_index("rep")

    def row(self):
        return lax.axis_index("tile") // self.grid_side

    def column(self):
        return lax.axis_index("tile") % self.grid_side

    def owner(self):
        return 1 + self.column() % 2

    def sent(self, index, way):
        return 1 - index if self.ways == 1 else way

    def received(self, index, way):
        return 1 - index if self.ways == 1 else 1 - way


def solution(mesh):
    sections, tiles, reps = (mesh.shape[a] for a in AXES)
    grid_side = math.isqrt(tiles)
    place = Place(grid_side)
    ways = place.ways

    def everywhere(target_of):
        pairs = []
        for s in range(sections):
            for t in range(tiles):
                for r in range(reps):
                    target = target_of(s, t // grid_side, t % grid_side, r)
                    if target is None:
                        continue
                    ts, ty, tx, tr = target
                    if not (0 <= ty < grid_side and 0 <= tx < grid_side):
                        continue
                    pairs.append(
                        ((s * tiles + t) * reps + r, (ts * tiles + ty * grid_side + tx) * reps + tr)
                    )
        return pairs

    def move(value, target_of):
        return lax.ppermute(value, AXES, everywhere(target_of))

    def trade_rows(values):
        if ways == 1:
            return [move(values[0], lambda s, y, x, r: (s, 1 - y, x, r))]
        return [
            move(values[0], lambda s, y, x, r: (s, y - 1, x, r)),
            move(values[1], lambda s, y, x, r: (s, y + 1, x, r)),
        ]

    def trade_columns(values):
        if ways == 1:
            return [move(values[0], lambda s, y, x, r: (s, y, 1 - x, r))]
        return [
            move(values[0], lambda s, y, x, r: (s, y, x - 1, r)),
            move(values[1], lambda s, y, x, r: (s, y, x + 1, r)),
        ]

    def owner_of(x):
        return 1 + x % 2

    def near_of(x):
        return 3 * (x % 2)

    def middle_of(x):
        return 3 - owner_of(x)

    def far_of(x):
        return 3 - near_of(x)

    def shards(phase_shift, absorption, probe_wave, positions, counts):
        width = phase_shift.shape[2]
        frame = probe_wave.shape[1]
        half_rows = width // reps
        phase = phase_shift.reshape(width, width)
        absorb = absorption.reshape(width, width)
        spot = positions.reshape(1, 2)
        def tiles_of(spots):
            return jnp.broadcast_to(spots.reshape(-1, 1, 1), (spots.size, 8, LANES))

        spot_tiles = tiles_of(spot)
        observed = counts.reshape(frame, frame)
        sds = jax.ShapeDtypeStruct
        small = pltpu.CompilerParams(vmem_limit_bytes=8 << 20)

        spots_rows = [tiles_of(spots) for spots in trade_rows([spot] * ways)]
        tile = jnp.stack([phase, absorb])

        def load_kernel(tile, *edges):
            for way in range(ways):
                start = place.sent(place.column(), way) * (width - HALO)
                columns = pl.ds(pl.multiple_of(start, LANES), HALO)
                for plane in range(2):
                    edges[plane * ways + way][...] = tile[plane, :, columns]

        edges = pl.pallas_call(
            load_kernel,
            out_shape=[sds((width, HALO), f32)] * (2 * ways),
            in_specs=[VMEM],
            out_specs=[VMEM] * (2 * ways),
            compiler_params=small,
            name="edges",
        )(tile)
        phase_edges, absorb_edges = edges[:ways], edges[ways:]
        absorb_edges, spots_rows = lax.optimization_barrier((absorb_edges, spots_rows))
        sides = trade_columns(phase_edges) + trade_columns(absorb_edges)

        def rows_of(refs, plane, rows):
            sides_here = refs[1 + plane * ways : 1 + (plane + 1) * ways]
            return refs[0][plane, rows, :], [side[rows, :] for side in sides_here]

        def bands_of(tile, margin):
            inner = [tile[:, i * HALO : (i + 1) * HALO] for i in range(3)]
            ends = []
            for side in range(2):
                if ways == 1:
                    there = place.received(place.column(), 0) == side
                    ends.append(jnp.where(there, margin[0], 0.0))
                else:
                    there = place.column() > 0 if side == 0 else place.column() < grid_side - 1
                    ends.append(jnp.where(there, margin[1 - side], 0.0))
            return [ends[0], *inner, ends[1]]

        def transmission(angle, loss):
            cosine, sine = cos_sin(angle)
            damping = jnp.exp(-loss)
            return damping * cosine, damping * sine

        def strip_kernel(*refs):
            loaded, spot_refs = refs[: 1 + 2 * ways], refs[1 + 2 * ways : 1 + 3 * ways]
            outs = refs[1 + 3 * ways :]
            for way in range(ways):
                below = place.sent(place.row(), way)
                rows = pl.ds(pl.multiple_of(below * (width - HALO), 8), HALO)
                column = column_at(spot_refs[way if ways == 1 else 1 - way])
                cut = [
                    choose_columns(bands_of(*rows_of(loaded, plane, rows)), column)
                    for plane in range(2)
                ]
                outs[way][0], outs[way][1] = transmission(*cut)

        strips = pl.pallas_call(
            strip_kernel,
            out_shape=[sds((2, HALO, frame), f32)] * ways,
            in_specs=[VMEM] * (1 + 3 * ways),
            out_specs=[VMEM] * ways,
            compiler_params=small,
            name="halo_rows",
        )(tile, *sides, *spots_rows)
        rims = trade_rows(strips)

        def window_kernel(spot_ref, *refs):
            loaded, (whole, part) = refs[:-2], refs[-2:]
            row, column = row_at(spot_ref), column_at(spot_ref)
            index = row_index((HALO, HALO))
            upper = in_band(index + HALO, row, 1)
            planes = []
            for plane in range(2):
                first = bands_of(*rows_of(loaded, plane, slice(0, HALO)))
                third = bands_of(*rows_of(loaded, plane, slice(2 * HALO, 3 * HALO)))
                bands = [jnp.where(upper, v, w) for v, w in zip(first, third)]
                planes.append(choose_columns(bands, column))
            whole[0], whole[1] = transmission(*planes)
            planes = []
            for plane in range(2):
                bands = bands_of(*rows_of(loaded, plane, slice(HALO, 2 * HALO)))
                planes.append(choose_columns(bands, column))
            real, imag = transmission(*planes)
            inside = in_band(row_index((HALO, frame)), row, 2)
            part[0], part[1] = jnp.where(inside, real, 1.0), jnp.where(inside, imag, 0.0)

        whole, part = pl.pallas_call(
            window_kernel,
            out_shape=[sds((2, HALO, frame), f32)] * 2,
            in_specs=[VMEM] * (2 + 2 * ways),
            out_specs=[VMEM] * 2,
            compiler_params=small,
            name="window",
        )(spot_tiles, tile, *sides)

        def to_owner(value):
            return [
                move(
                    value,
                    lambda s, y, x, r: (owner_of(x), y, x, r) if s == section_of(x) else None,
                )
                for section_of in (near_of, middle_of, far_of)
            ]

        wholes = to_owner(whole)

        def join_kernel(spot_ref, part_ref, *refs):
            rim_refs, out = refs[:ways], refs[ways]
            row = row_at(spot_ref)
            index = row_index((HALO, frame))
            out[...] = part_ref[...]
            for way in range(ways):
                side = place.received(place.row(), way)
                there = jnp.where(side == 0, place.row() > 0, place.row() < grid_side - 1)
                shifted = index + jnp.where(side == 0, 0, 2 * (2 * HALO))
                near = (shifted >= row) & (shifted < row + jnp.where(there, 2 * HALO, 0))
                for plane in range(2):
                    out[plane] = jnp.where(near, rim_refs[way][plane], out[plane])

        joined = pl.pallas_call(
            join_kernel,
            out_shape=sds((2, HALO, frame), f32),
            in_specs=[VMEM] * (2 + ways),
            out_specs=VMEM,
            compiler_params=small,
            name="join",
        )(spot_tiles, part, *rims)
        joined, probe_late = lax.optimization_barrier((joined, probe_wave))
        joineds = to_owner(joined)

        tables, sort = wave_tables(frame)

        def prepare_kernel(spot_ref, probe, seen, sort, rolled, counted):
            row, column = lax.rem(spot_ref[0, 0], frame), lax.rem(spot_ref[0, 1], frame)
            for plane in range(2):
                rolled[plane] = pltpu.roll(pltpu.roll(probe[plane], row, 0), column, 1)
            first = dot(sort[0], seen[...].astype(f32).astype(bf16)).astype(bf16)
            counted[...] = dot(first, sort[1])

        rolled, counted = pl.pallas_call(
            prepare_kernel,
            out_shape=[sds((2, frame, frame), f32), sds((frame, frame), f32)],
            in_specs=[SMEM] + [VMEM] * 3,
            out_specs=[VMEM] * 2,
            compiler_params=small,
            name="prepare",
        )(spot, probe_late, observed, sort)
        places, counted = lax.optimization_barrier(
            (jnp.concatenate([spot_tiles] + spots_rows, 0), counted)
        )
        spots_rep = move(places, lambda s, y, x, r: (s, y, x, 1 - r))

        def frame_kernel(partner_ref, probe, seen, tables, *refs):
            whole_refs, joined_refs, outs = refs[:4], refs[4:8], refs[8:12]
            fields, exits = refs[12:]
            own_is_second = place.owner() == 1
            far, middle, own, near = zip(joined_refs[::-1], whole_refs)
            choices = ((near, far), (own, middle), (middle, own), (far, near))

            def field(number, plane):
                first, second = choices[number]
                return jnp.concatenate(
                    [jnp.where(own_is_second, a[plane], b[plane]) for a, b in zip(first, second)], 0
                )

            re, im = probe[0], probe[1]
            for number in range(4):
                o_re, o_im = field(number, 0), field(number, 1)
                fields[number, 0], fields[number, 1] = o_re, o_im
                exit_re, exit_im = o_re * re - o_im * im, o_re * im + o_im * re
                exits[number, 0], exits[number, 1] = exit_re, exit_im
                if number < 3:
                    re, im = near_field(tables, exit_re, exit_im)
            re, im = far_field(tables, exit_re, exit_im)
            re, im = likelihood_seed(re, im, seen[...])
            im = -im
            for number in reversed(range(4)):
                if number == 3:
                    re, im = far_back(tables, re, im)
                else:
                    re, im = near_field(tables, re, im)
                exit_re, exit_im = exits[number, 0], exits[number, 1]
                found = -(re * exit_im + im * exit_re), im * exit_im - re * exit_re
                if number > 0:
                    o_re, o_im = fields[number, 0], fields[number, 1]
                    re, im = o_re * re - o_im * im, o_re * im + o_im * re
                one, other = (0, 3) if number in (0, 3) else (1, 2)
                for plane, term in enumerate(found):
                    if number >= 2:
                        outs[one][plane] = term
                        outs[other][plane] = term
                    else:
                        kept_term = outs[one][plane]
                        outs[one][plane] = jnp.where(own_is_second, term, kept_term)
                        outs[other][plane] = jnp.where(own_is_second, kept_term, term)

        terms = pl.pallas_call(
            frame_kernel,
            out_shape=[sds((2, frame, frame), f32)] * 4,
            in_specs=[VMEM] * 12,
            out_specs=[VMEM] * 4,
            scratch_shapes=[
                pltpu.VMEM((4, 2, frame, frame), f32),
                pltpu.VMEM((4, 2, frame, frame), f32),
            ],
            compiler_params=pltpu.CompilerParams(vmem_limit_bytes=16 << 20),
            name="frame",
        )(
            spots_rep, rolled, counted, tables,
            wholes[2], wholes[1], whole, wholes[0],
            joineds[0], joined, joineds[1], joineds[2],
        )

        def from_owner(value, section_of):
            return move(
                value,
                lambda s, y, x, r: (section_of(x), y, x, r) if s == owner_of(x) else None,
            )

        far_terms = from_owner(terms[3], far_of)
        back = (
            far_terms,
            from_owner(terms[2], middle_of),
            from_owner(terms[0], near_of),
            terms[1],
        )

        def load_term(refs, term):
            section, owner = place.section(), place.owner()
            near = 3 * (owner - 1)
            choice = jnp.where(
                section == 3 - near, 0, jnp.where(section == near, 2, jnp.where(section == owner, 3, 1))
            )
            for number, ref in enumerate(refs):

                @pl.when(choice == number)
                def _():
                    term[...] = ref[...]

        def rows_for(term, plane, row, rep):
            index = row_index((frame, frame))
            middle = jnp.where(in_band(index, row, 2), term[plane], 0.0)
            later = middle[HALO // 2 :]
            earlier = jnp.where(in_band(index, row, 0), term[plane], 0.0)
            earlier = jnp.concatenate([earlier[HALO:], middle[: HALO // 2]], 0)
            return jnp.where(rep == 0, earlier, later)

        def strips_of(term, plane, row):
            index = row_index((HALO, frame))
            first = term[plane, :HALO]
            bands = (in_band(index, row, band) for band in (0, 4))
            return [jnp.where(band, first, 0.0) for band in bands]

        def own_kernel(spot_ref, own, across):
            for plane in range(2):
                above, below = strips_of(own, plane, row_at(spot_ref))
                across[plane] = jnp.where(place.rep() == 1, below, above)

        def parts_kernel(spot_ref, *refs):
            back_refs, (give, straight, across, term) = refs[:4], refs[4:]
            load_term(back_refs, term)
            rep, row = place.rep(), row_at(spot_ref)
            for plane in range(2):
                give[plane] = rows_for(term, plane, row, 1 - rep)
                above, below = strips_of(term, plane, row)
                straight[plane] = jnp.where(rep == 1, above, below)
                across[plane] = jnp.where(rep == 1, below, above)

        routes = (
            lambda s, y, x, r: (s, y, x, 1 - r),
            lambda s, y, x, r: (s, y + 1 - 2 * r, x, r),
            lambda s, y, x, r: (s, y - 1 + 2 * r, x, 1 - r),
        )

        def exchange(value, number, owners=None):
            return move(
                value,
                lambda s, y, x, r: (
                    routes[number](s, y, x, r)
                    if owners is None or (s == owner_of(x)) == owners
                    else None
                ),
            )

        strip = sds((2, HALO, frame), f32)
        part_shapes = [sds((2, half_rows, frame), f32), strip, strip]
        own_across = pl.pallas_call(
            own_kernel,
            out_shape=strip,
            in_specs=[VMEM] * 2,
            out_specs=VMEM,
            compiler_params=small,
            name="own_parts",
        )(spot_tiles, terms[1])
        early_across = exchange(own_across, 2, True)
        give, straight, across = pl.pallas_call(
            parts_kernel,
            out_shape=part_shapes,
            in_specs=[VMEM] * 5,
            out_specs=[VMEM] * 3,
            scratch_shapes=[pltpu.VMEM((2, frame, frame), f32)],
            compiler_params=small,
            name="parts",
        )(spot_tiles, *back)
        given = exchange(give, 0)
        straight, across, early_across = lax.optimization_barrier((straight, across, early_across))
        came_straight, late_across = exchange(straight, 1), exchange(across, 2, False)

        def keep_kernel(spot_ref, *refs):
            back_refs, (mine, term) = refs[:4], refs[4:]
            load_term(back_refs, term)
            for plane in range(2):
                mine[plane] = rows_for(term, plane, row_at(spot_ref), place.rep())

        kept = pl.pallas_call(
            keep_kernel,
            out_shape=sds((2, half_rows, frame), f32),
            in_specs=[VMEM] * 5,
            out_specs=VMEM,
            scratch_shapes=[pltpu.VMEM((2, frame, frame), f32)],
            compiler_params=small,
            cost_estimate=pl.CostEstimate(flops=1 << 22, bytes_accessed=1 << 21, transcendentals=0),
            name="keep",
        )(spot_tiles, *back)

        def add_band(band, plane, refs):
            spot_ref, partner_ref, kept_ref, *spot_refs = refs[: 3 + ways]
            is_owner = place.section() == place.owner()
            given, straight, late, early = (ref[plane] for ref in refs[3 + ways : count])
            across = jnp.where(is_owner, early, late)
            rep = place.rep()
            if ways == 1:
                straight_column, across_column = column_at(spot_refs[0]), column_at(partner_ref, 1)
            else:
                straight_column = jnp.where(rep == 1, column_at(spot_refs[0]), column_at(spot_refs[1]))
                across_column = jnp.where(
                    rep == 1, column_at(partner_ref, 1), column_at(partner_ref, 2)
                )
            total = part_of_band(kept_ref[plane], column_at(spot_ref), band)
            total += part_of_band(given, column_at(partner_ref), band)
            strip = part_of_band(straight, straight_column, band)
            strip += part_of_band(across, across_column, band)
            gap = jnp.zeros((half_rows - HALO, HALO), f32)
            early, late = jnp.concatenate([strip, gap], 0), jnp.concatenate([gap, strip], 0)
            return total + jnp.where(rep == 1, late, early)

        pieces = (spot_tiles, spots_rep, kept, *spots_rows, given, came_straight, late_across, early_across)
        piece_specs = [VMEM] * len(pieces)
        count = len(piece_specs)

        def edge_kernel(*refs):
            for way in range(ways):
                for plane in range(2):
                    if ways == 1:
                        value = jnp.where(
                            place.column() == 0,
                            add_band(4, plane, refs),
                            add_band(0, plane, refs),
                        )
                    else:
                        value = add_band(4 * way, plane, refs)
                    refs[count + way][plane] = value

        leaving = pl.pallas_call(
            edge_kernel,
            out_shape=[sds((2, half_rows, HALO), f32)] * ways,
            in_specs=piece_specs,
            out_specs=[VMEM] * ways,
            compiler_params=small,
            name="edge_terms",
        )(*pieces)
        arrived = trade_columns(leaving)

        def inner_kernel(*refs):
            outs, inner, total, semaphores = refs[count : count + 2], *refs[count + 2 :]
            copies = Copies(semaphores)
            started = []
            for plane in range(2):
                bands = [add_band(band, plane, refs) for band in (1, 2, 3)]
                for number, value in enumerate(bands):
                    total[plane, :, number * HALO : (number + 1) * HALO] = value
                started.append(copies.start(total.at[plane], outs[plane]))
                for way in range(ways):
                    first = place.received(place.column(), way) == 0
                    inner[way, plane] = jnp.where(first, bands[0], bands[2])
            wait_for(started)

        *results, inner = pl.pallas_call(
            inner_kernel,
            out_shape=[sds((half_rows, width), f32)] * 2
            + [sds((ways, 2, half_rows, HALO), f32)],
            in_specs=piece_specs,
            out_specs=[HBM] * 2 + [VMEM],
            scratch_shapes=[
                pltpu.VMEM((2, half_rows, width), f32),
                pltpu.SemaphoreType.DMA((2,)),
            ],
            compiler_params=small,
            cost_estimate=pl.CostEstimate(flops=1 << 22, bytes_accessed=1 << 21, transcendentals=0),
            name="inner_terms",
        )(*pieces)

        def finish_kernel(phase_in, absorb_in, inner_ref, *refs):
            arrived_refs, outs = refs[:ways], refs[ways : ways + 2]
            strips, semaphores = refs[ways + 2 :]
            copies = Copies(semaphores)
            leaving = []
            for way in range(ways):
                start = place.received(place.column(), way) * (width - HALO)
                for plane in range(2):
                    strips[way, plane] = arrived_refs[way][plane] + inner_ref[way, plane]
                    target = outs[plane].at[:, pl.ds(pl.multiple_of(start, LANES), HALO)]
                    leaving.append(copies.start(strips.at[way, plane], target))
            wait_for(leaving)

        result = pl.pallas_call(
            finish_kernel,
            out_shape=[sds((half_rows, width), f32)] * 2,
            in_specs=[HBM, HBM, VMEM] + [VMEM] * ways,
            out_specs=[HBM] * 2,
            scratch_shapes=[
                pltpu.VMEM((ways, 2, half_rows, HALO), f32),
                pltpu.SemaphoreType.DMA((2 * ways,)),
            ],
            input_output_aliases={0: 0, 1: 1},
            compiler_params=small,
            name="finish",
        )(*results, inner, *arrived)
        return tuple(plane[None, None] for plane in result)

    in_specs = (
        P("section", "tile", None, None),
        P("section", "tile", None, None),
        P(),
        P("tile", "rep", None, None),
        P("tile", "rep", None, None, None),
    )
    out_specs = (P("section", "tile", "rep", None), P("section", "tile", "rep", None))
    return jax.shard_map(shards, mesh=mesh, in_specs=in_specs, out_specs=out_specs, check_vma=False)
```

```python
import math

import jax
import jax.numpy as jnp
import ml_dtypes
import numpy as np
from jax import lax
from jax.experimental import pallas as pl
from jax.experimental.pallas import tpu as pltpu
from jax.sharding import PartitionSpec as P

HALO = 128
LANES = 128
AXES = ("section", "tile", "rep")

dead_time = 0.1
background = 0.1
loss_weight = 0.1
fresnel = 0.5

f32 = jnp.float32
bf16 = jnp.bfloat16

SMEM = pl.BlockSpec(memory_space=pltpu.SMEM)
VMEM = pl.BlockSpec(memory_space=pltpu.VMEM)
HBM = pl.BlockSpec(memory_space=pltpu.HBM)


def two_parts(matrix):
    high = matrix.astype(ml_dtypes.bfloat16)
    low = (matrix - high.astype(np.float64)).astype(ml_dtypes.bfloat16)
    return np.stack([high, low])


def from_left(matrix):
    return np.block([[matrix.real, -matrix.imag], [matrix.imag, matrix.real]])


def from_right(matrix):
    return np.block([[matrix.real, matrix.imag], [-matrix.imag, matrix.real]])


def wave_tables(length):
    half = length // 2
    indices = np.arange(length)
    shifted = np.where(indices < half, indices, indices - length)
    kernel = np.exp(1j * math.pi * fresnel * shifted.astype(np.float64) ** 2 / length)
    spread = np.fft.ifft(kernel)
    circulant = spread[(indices[:, None] - indices[None, :]) % length]
    first, second = circulant[:half, :half], circulant[:half, half:]
    plus, minus = (first + second) / 2, (first - second) / 2
    near = [from_left(plus), from_left(minus), from_right(plus), from_right(minus)]
    turns = np.outer(indices[:half], indices[:half]) % half
    even = np.exp(-2j * math.pi * turns / half) / math.sqrt(length)
    odd = even * np.exp(-2j * math.pi * indices[:half] / length)[None, :]
    far = [from_left(even), from_left(odd), from_right(even.T), from_right(odd.T)]
    back = [from_left(even.T), from_left(odd.T), from_right(even), from_right(odd)]
    sort = np.zeros((length, length))
    sort[np.arange(half), 2 * np.arange(half)] = 1
    sort[half + np.arange(half), 2 * np.arange(half) + 1] = 1
    tables = np.stack([two_parts(m) for m in near + far + back])
    return tables, np.stack([sort, sort.T]).astype(ml_dtypes.bfloat16)


def fitted(function, degree):
    top = math.pi**2
    fit = np.polynomial.chebyshev.Chebyshev.interpolate(function, degree, domain=[0.0, top])
    return [float(c) for c in fit.convert(kind=np.polynomial.Polynomial).coef]


def sine_ratio(u):
    angle = np.sqrt(np.maximum(u, 1e-12))
    return np.sin(angle) / angle


SINE = fitted(sine_ratio, 8)
COSINE = fitted(lambda u: np.cos(np.sqrt(np.maximum(u, 0.0))), 8)


def polynomial(coefficients, u):
    total = jnp.full_like(u, coefficients[-1])
    for c in coefficients[-2::-1]:
        total = total * u + c
    return total


def cos_sin(angle):
    square = angle * angle
    return polynomial(COSINE, square), angle * polynomial(SINE, square)


def halves(value):
    high = value.astype(bf16)
    return high, (value - high.astype(f32)).astype(bf16)


def dot(a, b):
    return jnp.dot(a, b, preferred_element_type=f32)


def left_by(tables, index, value):
    high, low = halves(value)
    return dot(tables[index, 0], high) + dot(tables[index, 1], high) + dot(tables[index, 0], low)


def right_by(tables, index, value):
    high, low = halves(value)
    return dot(high, tables[index, 0]) + dot(high, tables[index, 1]) + dot(low, tables[index, 0])


def propagate(tables, at, re, im, fold, unfold):
    half = re.shape[0] // 2
    re0, re1, im0, im1 = re[:half], re[half:], im[:half], im[half:]
    if fold:
        re0, re1, im0, im1 = re0 + re1, re0 - re1, im0 + im1, im0 - im1
    first = left_by(tables, at, jnp.concatenate([re0, im0], 0))
    second = left_by(tables, at + 1, jnp.concatenate([re1, im1], 0))
    if unfold:
        first, second = first + second, first - second
    re = jnp.concatenate([first[:half], second[:half]], 0)
    im = jnp.concatenate([first[half:], second[half:]], 0)
    re0, re1, im0, im1 = re[:, :half], re[:, half:], im[:, :half], im[:, half:]
    if fold:
        re0, re1, im0, im1 = re0 + re1, re0 - re1, im0 + im1, im0 - im1
    first = right_by(tables, at + 2, jnp.concatenate([re0, im0], 1))
    second = right_by(tables, at + 3, jnp.concatenate([re1, im1], 1))
    if unfold:
        first, second = first + second, first - second
    re = jnp.concatenate([first[:, :half], second[:, :half]], 1)
    im = jnp.concatenate([first[:, half:], second[:, half:]], 1)
    return re, im


def near_field(tables, re, im):
    return propagate(tables, 0, re, im, True, True)


def far_field(tables, re, im):
    return propagate(tables, 4, re, im, True, False)


def far_back(tables, re, im):
    return propagate(tables, 8, re, im, False, True)


def likelihood_seed(far_re, far_im, observed):
    intensity = far_re * far_re + far_im * far_im
    shifted_total = intensity + background
    denominator = 1.0 + dead_time * shifted_total
    model_rate = shifted_total / denominator
    slope_term = loss_weight * (1.0 - observed / model_rate) / (denominator * denominator)
    return (2.0 * slope_term * far_re, 2.0 * slope_term * far_im)


def in_band(index, offset, band):
    cell = index + (band // 2) * (2 * HALO)
    return (cell >= offset) & (cell < offset + 2 * HALO)


def row_at(ref, number=0):
    return ref[2 * number, :1, :1]


def column_at(ref, number=0):
    return ref[2 * number + 1, :1, :1]


def lane_index(shape):
    return lax.broadcasted_iota(jnp.int32, shape, len(shape) - 1)


def row_index(shape):
    return lax.broadcasted_iota(jnp.int32, shape, len(shape) - 2)


def choose_columns(bands, offset):
    lane = lane_index(bands[1].shape)
    first = jnp.where(
        in_band(lane, offset, 0), bands[0], jnp.where(in_band(lane, offset, 2), bands[2], bands[4])
    )
    second = jnp.where(in_band(lane + HALO, offset, 1), bands[1], bands[3])
    return jnp.concatenate([first, second], 1)


def part_of_band(value, offset, band):
    start = (band % 2) * HALO
    half = value[:, start : start + HALO]
    return jnp.where(in_band(lane_index(half.shape) + start, offset, band), half, 0.0)


class Copies:
    def __init__(self, semaphores):
        self.semaphores = semaphores
        self.count = 0

    def start(self, source, target):
        copy = pltpu.make_async_copy(source, target, self.semaphores.at[self.count])
        self.count += 1
        copy.start()
        return copy


def wait_for(copies):
    for copy in copies:
        copy.wait()


class Place:
    def __init__(self, grid_side):
        self.grid_side = grid_side
        self.ways = 1 if grid_side == 2 else 2

    def section(self):
        return lax.axis_index("section")

    def rep(self):
        return lax.axis_index("rep")

    def row(self):
        return lax.axis_index("tile") // self.grid_side

    def column(self):
        return lax.axis_index("tile") % self.grid_side

    def owner(self):
        return 1 + self.column() % 2

    def sent(self, index, way):
        return 1 - index if self.ways == 1 else way

    def received(self, index, way):
        return 1 - index if self.ways == 1 else 1 - way


def solution(mesh):
    sections, tiles, reps = (mesh.shape[a] for a in AXES)
    grid_side = math.isqrt(tiles)
    place = Place(grid_side)
    ways = place.ways

    def everywhere(target_of):
        pairs = []
        for s in range(sections):
            for t in range(tiles):
                for r in range(reps):
                    target = target_of(s, t // grid_side, t % grid_side, r)
                    if target is None:
                        continue
                    ts, ty, tx, tr = target
                    if not (0 <= ty < grid_side and 0 <= tx < grid_side):
                        continue
                    pairs.append(
                        ((s * tiles + t) * reps + r, (ts * tiles + ty * grid_side + tx) * reps + tr)
                    )
        return pairs

    def move(value, target_of):
        return lax.ppermute(value, AXES, everywhere(target_of))

    def trade_rows(values):
        if ways == 1:
            return [move(values[0], lambda s, y, x, r: (s, 1 - y, x, r))]
        return [
            move(values[0], lambda s, y, x, r: (s, y - 1, x, r)),
            move(values[1], lambda s, y, x, r: (s, y + 1, x, r)),
        ]

    def trade_columns(values):
        if ways == 1:
            return [move(values[0], lambda s, y, x, r: (s, y, 1 - x, r))]
        return [
            move(values[0], lambda s, y, x, r: (s, y, x - 1, r)),
            move(values[1], lambda s, y, x, r: (s, y, x + 1, r)),
        ]

    def owner_of(x):
        return 1 + x % 2

    def near_of(x):
        return 3 * (x % 2)

    def middle_of(x):
        return 3 - owner_of(x)

    def far_of(x):
        return 3 - near_of(x)

    def shards(phase_shift, absorption, probe_wave, positions, counts):
        width = phase_shift.shape[2]
        frame = probe_wave.shape[1]
        half_rows = width // reps
        phase = phase_shift.reshape(width, width)
        absorb = absorption.reshape(width, width)
        spot = positions.reshape(1, 2)
        def tiles_of(spots):
            return jnp.broadcast_to(spots.reshape(-1, 1, 1), (spots.size, 8, LANES))

        spot_tiles = tiles_of(spot)
        observed = counts.reshape(frame, frame)
        sds = jax.ShapeDtypeStruct
        small = pltpu.CompilerParams(vmem_limit_bytes=8 << 20)

        spots_rows = [tiles_of(spots) for spots in trade_rows([spot] * ways)]
        tile = jnp.stack([phase, absorb])

        def load_kernel(tile, *edges):
            for way in range(ways):
                start = place.sent(place.column(), way) * (width - HALO)
                columns = pl.ds(pl.multiple_of(start, LANES), HALO)
                for plane in range(2):
                    edges[plane * ways + way][...] = tile[plane, :, columns]

        edges = pl.pallas_call(
            load_kernel,
            out_shape=[sds((width, HALO), f32)] * (2 * ways),
            in_specs=[VMEM],
            out_specs=[VMEM] * (2 * ways),
            compiler_params=small,
            name="edges",
        )(tile)
        phase_edges, absorb_edges = edges[:ways], edges[ways:]
        absorb_edges, spots_rows = lax.optimization_barrier((absorb_edges, spots_rows))
        sides = trade_columns(phase_edges) + trade_columns(absorb_edges)

        def rows_of(refs, plane, rows):
            sides_here = refs[1 + plane * ways : 1 + (plane + 1) * ways]
            return refs[0][plane, rows, :], [side[rows, :] for side in sides_here]

        def bands_of(tile, margin):
            inner = [tile[:, i * HALO : (i + 1) * HALO] for i in range(3)]
            ends = []
            for side in range(2):
                if ways == 1:
                    there = place.received(place.column(), 0) == side
                    ends.append(jnp.where(there, margin[0], 0.0))
                else:
                    there = place.column() > 0 if side == 0 else place.column() < grid_side - 1
                    ends.append(jnp.where(there, margin[1 - side], 0.0))
            return [ends[0], *inner, ends[1]]

        def transmission(angle, loss):
            cosine, sine = cos_sin(angle)
            damping = jnp.exp(-loss)
            return damping * cosine, damping * sine

        def strip_kernel(*refs):
            loaded, spot_refs = refs[: 1 + 2 * ways], refs[1 + 2 * ways : 1 + 3 * ways]
            outs = refs[1 + 3 * ways :]
            for way in range(ways):
                below = place.sent(place.row(), way)
                rows = pl.ds(pl.multiple_of(below * (width - HALO), 8), HALO)
                column = column_at(spot_refs[way if ways == 1 else 1 - way])
                cut = [
                    choose_columns(bands_of(*rows_of(loaded, plane, rows)), column)
                    for plane in range(2)
                ]
                outs[way][0], outs[way][1] = transmission(*cut)

        strips = pl.pallas_call(
            strip_kernel,
            out_shape=[sds((2, HALO, frame), f32)] * ways,
            in_specs=[VMEM] * (1 + 3 * ways),
            out_specs=[VMEM] * ways,
            compiler_params=small,
            name="halo_rows",
        )(tile, *sides, *spots_rows)
        rims = trade_rows(strips)

        def window_kernel(spot_ref, *refs):
            loaded, (whole, part) = refs[:-2], refs[-2:]
            row, column = row_at(spot_ref), column_at(spot_ref)
            index = row_index((HALO, HALO))
            upper = in_band(index + HALO, row, 1)
            planes = []
            for plane in range(2):
                first = bands_of(*rows_of(loaded, plane, slice(0, HALO)))
                third = bands_of(*rows_of(loaded, plane, slice(2 * HALO, 3 * HALO)))
                bands = [jnp.where(upper, v, w) for v, w in zip(first, third)]
                planes.append(choose_columns(bands, column))
            whole[0], whole[1] = transmission(*planes)
            planes = []
            for plane in range(2):
                bands = bands_of(*rows_of(loaded, plane, slice(HALO, 2 * HALO)))
                planes.append(choose_columns(bands, column))
            real, imag = transmission(*planes)
            inside = in_band(row_index((HALO, frame)), row, 2)
            part[0], part[1] = jnp.where(inside, real, 1.0), jnp.where(inside, imag, 0.0)

        whole, part = pl.pallas_call(
            window_kernel,
            out_shape=[sds((2, HALO, frame), f32)] * 2,
            in_specs=[VMEM] * (2 + 2 * ways),
            out_specs=[VMEM] * 2,
            compiler_params=small,
            name="window",
        )(spot_tiles, tile, *sides)

        def to_owner(value):
            return [
                move(
                    value,
                    lambda s, y, x, r: (owner_of(x), y, x, r) if s == section_of(x) else None,
                )
                for section_of in (near_of, middle_of, far_of)
            ]

        wholes = to_owner(whole)

        def join_kernel(spot_ref, part_ref, *refs):
            rim_refs, out = refs[:ways], refs[ways]
            row = row_at(spot_ref)
            index = row_index((HALO, frame))
            out[...] = part_ref[...]
            for way in range(ways):
                side = place.received(place.row(), way)
                there = jnp.where(side == 0, place.row() > 0, place.row() < grid_side - 1)
                shifted = index + jnp.where(side == 0, 0, 2 * (2 * HALO))
                near = (shifted >= row) & (shifted < row + jnp.where(there, 2 * HALO, 0))
                for plane in range(2):
                    out[plane] = jnp.where(near, rim_refs[way][plane], out[plane])

        joined = pl.pallas_call(
            join_kernel,
            out_shape=sds((2, HALO, frame), f32),
            in_specs=[VMEM] * (2 + ways),
            out_specs=VMEM,
            compiler_params=small,
            name="join",
        )(spot_tiles, part, *rims)
        joined, probe_late = lax.optimization_barrier((joined, probe_wave))
        joineds = to_owner(joined)

        tables, sort = wave_tables(frame)

        def prepare_kernel(spot_ref, probe, seen, sort, rolled, counted):
            row, column = lax.rem(spot_ref[0, 0], frame), lax.rem(spot_ref[0, 1], frame)
            for plane in range(2):
                rolled[plane] = pltpu.roll(pltpu.roll(probe[plane], row, 0), column, 1)
            first = dot(sort[0], seen[...].astype(f32).astype(bf16)).astype(bf16)
            counted[...] = dot(first, sort[1])

        rolled, counted = pl.pallas_call(
            prepare_kernel,
            out_shape=[sds((2, frame, frame), f32), sds((frame, frame), f32)],
            in_specs=[SMEM] + [VMEM] * 3,
            out_specs=[VMEM] * 2,
            compiler_params=small,
            name="prepare",
        )(spot, probe_late, observed, sort)
        places, counted = lax.optimization_barrier(
            (jnp.concatenate([spot_tiles] + spots_rows, 0), counted)
        )
        spots_rep = move(places, lambda s, y, x, r: (s, y, x, 1 - r))

        def frame_kernel(partner_ref, probe, seen, tables, *refs):
            whole_refs, joined_refs, outs = refs[:4], refs[4:8], refs[8:12]
            fields, exits = refs[12:]
            own_is_second = place.owner() == 1
            far, middle, own, near = zip(joined_refs[::-1], whole_refs)
            choices = ((near, far), (own, middle), (middle, own), (far, near))

            def field(number, plane):
                first, second = choices[number]
                return jnp.concatenate(
                    [jnp.where(own_is_second, a[plane], b[plane]) for a, b in zip(first, second)], 0
                )

            re, im = probe[0], probe[1]
            for number in range(4):
                o_re, o_im = field(number, 0), field(number, 1)
                fields[number, 0], fields[number, 1] = o_re, o_im
                exit_re, exit_im = o_re * re - o_im * im, o_re * im + o_im * re
                exits[number, 0], exits[number, 1] = exit_re, exit_im
                if number < 3:
                    re, im = near_field(tables, exit_re, exit_im)
            re, im = far_field(tables, exit_re, exit_im)
            re, im = likelihood_seed(re, im, seen[...])
            im = -im
            for number in reversed(range(4)):
                if number == 3:
                    re, im = far_back(tables, re, im)
                else:
                    re, im = near_field(tables, re, im)
                exit_re, exit_im = exits[number, 0], exits[number, 1]
                found = -(re * exit_im + im * exit_re), im * exit_im - re * exit_re
                if number > 0:
                    o_re, o_im = fields[number, 0], fields[number, 1]
                    re, im = o_re * re - o_im * im, o_re * im + o_im * re
                one, other = (0, 3) if number in (0, 3) else (1, 2)
                for plane, term in enumerate(found):
                    if number >= 2:
                        outs[one][plane] = term
                        outs[other][plane] = term
                    else:
                        kept_term = outs[one][plane]
                        outs[one][plane] = jnp.where(own_is_second, term, kept_term)
                        outs[other][plane] = jnp.where(own_is_second, kept_term, term)

        terms = pl.pallas_call(
            frame_kernel,
            out_shape=[sds((2, frame, frame), f32)] * 4,
            in_specs=[VMEM] * 12,
            out_specs=[VMEM] * 4,
            scratch_shapes=[
                pltpu.VMEM((4, 2, frame, frame), f32),
                pltpu.VMEM((4, 2, frame, frame), f32),
            ],
            compiler_params=pltpu.CompilerParams(vmem_limit_bytes=16 << 20),
            name="frame",
        )(
            spots_rep, rolled, counted, tables,
            wholes[2], wholes[1], whole, wholes[0],
            joineds[0], joined, joineds[1], joineds[2],
        )

        def from_owner(value, section_of):
            return move(
                value,
                lambda s, y, x, r: (section_of(x), y, x, r) if s == owner_of(x) else None,
            )

        far_terms = from_owner(terms[3], far_of)
        back = (
            far_terms,
            from_owner(terms[0], near_of),
            from_owner(terms[2], middle_of),
            terms[1],
        )

        def load_term(refs, term):
            section, owner = place.section(), place.owner()
            near = 3 * (owner - 1)
            choice = jnp.where(
                section == 3 - near, 0, jnp.where(section == near, 1, jnp.where(section == owner, 3, 2))
            )
            for number, ref in enumerate(refs):

                @pl.when(choice == number)
                def _():
                    term[...] = ref[...]

        def rows_for(term, plane, row, rep):
            index = row_index((frame, frame))
            middle = jnp.where(in_band(index, row, 2), term[plane], 0.0)
            later = middle[HALO // 2 :]
            earlier = jnp.where(in_band(index, row, 0), term[plane], 0.0)
            earlier = jnp.concatenate([earlier[HALO:], middle[: HALO // 2]], 0)
            return jnp.where(rep == 0, earlier, later)

        def strips_of(term, plane, row):
            index = row_index((HALO, frame))
            first = term[plane, :HALO]
            bands = (in_band(index, row, band) for band in (0, 4))
            return [jnp.where(band, first, 0.0) for band in bands]

        def own_kernel(spot_ref, own, across):
            for plane in range(2):
                above, below = strips_of(own, plane, row_at(spot_ref))
                across[plane] = jnp.where(place.rep() == 1, below, above)

        def parts_kernel(spot_ref, *refs):
            back_refs, (give, straight, across, term) = refs[:4], refs[4:]
            load_term(back_refs, term)
            rep, row = place.rep(), row_at(spot_ref)
            for plane in range(2):
                give[plane] = rows_for(term, plane, row, 1 - rep)
                above, below = strips_of(term, plane, row)
                straight[plane] = jnp.where(rep == 1, above, below)
                across[plane] = jnp.where(rep == 1, below, above)

        routes = (
            lambda s, y, x, r: (s, y, x, 1 - r),
            lambda s, y, x, r: (s, y + 1 - 2 * r, x, r),
            lambda s, y, x, r: (s, y - 1 + 2 * r, x, 1 - r),
        )

        def exchange(value, number, owners=None):
            return move(
                value,
                lambda s, y, x, r: (
                    routes[number](s, y, x, r)
                    if owners is None or (s == owner_of(x)) == owners
                    else None
                ),
            )

        strip = sds((2, HALO, frame), f32)
        part_shapes = [sds((2, half_rows, frame), f32), strip, strip]
        own_across = pl.pallas_call(
            own_kernel,
            out_shape=strip,
            in_specs=[VMEM] * 2,
            out_specs=VMEM,
            compiler_params=small,
            name="own_parts",
        )(spot_tiles, terms[1])
        early_across = exchange(own_across, 2, True)
        give, straight, across = pl.pallas_call(
            parts_kernel,
            out_shape=part_shapes,
            in_specs=[VMEM] * 5,
            out_specs=[VMEM] * 3,
            scratch_shapes=[pltpu.VMEM((2, frame, frame), f32)],
            compiler_params=small,
            name="parts",
        )(spot_tiles, *back)
        given = exchange(give, 0)
        straight, across, early_across = lax.optimization_barrier((straight, across, early_across))
        came_straight, late_across = exchange(straight, 1), exchange(across, 2, False)

        def keep_kernel(spot_ref, *refs):
            back_refs, (mine, term) = refs[:4], refs[4:]
            load_term(back_refs, term)
            for plane in range(2):
                mine[plane] = rows_for(term, plane, row_at(spot_ref), place.rep())

        kept = pl.pallas_call(
            keep_kernel,
            out_shape=sds((2, half_rows, frame), f32),
            in_specs=[VMEM] * 5,
            out_specs=VMEM,
            scratch_shapes=[pltpu.VMEM((2, frame, frame), f32)],
            compiler_params=small,
            cost_estimate=pl.CostEstimate(flops=1 << 22, bytes_accessed=1 << 21, transcendentals=0),
            name="keep",
        )(spot_tiles, *back)

        def add_band(band, plane, refs):
            spot_ref, partner_ref, kept_ref, *spot_refs = refs[: 3 + ways]
            is_owner = place.section() == place.owner()
            straight, given, late, early = (ref[plane] for ref in refs[3 + ways : count])
            across = jnp.where(is_owner, early, late)
            rep = place.rep()
            if ways == 1:
                straight_column, across_column = column_at(spot_refs[0]), column_at(partner_ref, 1)
            else:
                straight_column = jnp.where(rep == 1, column_at(spot_refs[0]), column_at(spot_refs[1]))
                across_column = jnp.where(
                    rep == 1, column_at(partner_ref, 1), column_at(partner_ref, 2)
                )
            total = part_of_band(kept_ref[plane], column_at(spot_ref), band)
            total += part_of_band(given, column_at(partner_ref), band)
            strip = part_of_band(straight, straight_column, band)
            strip += part_of_band(across, across_column, band)
            gap = jnp.zeros((half_rows - HALO, HALO), f32)
            early, late = jnp.concatenate([strip, gap], 0), jnp.concatenate([gap, strip], 0)
            return total + jnp.where(rep == 1, late, early)

        pieces = (spot_tiles, spots_rep, kept, *spots_rows, came_straight, given, late_across, early_across)
        piece_specs = [VMEM] * len(pieces)
        count = len(piece_specs)

        def edge_kernel(*refs):
            for way in range(ways):
                for plane in range(2):
                    if ways == 1:
                        value = jnp.where(
                            place.column() == 0,
                            add_band(4, plane, refs),
                            add_band(0, plane, refs),
                        )
                    else:
                        value = add_band(4 * way, plane, refs)
                    refs[count + way][plane] = value

        leaving = pl.pallas_call(
            edge_kernel,
            out_shape=[sds((2, half_rows, HALO), f32)] * ways,
            in_specs=piece_specs,
            out_specs=[VMEM] * ways,
            compiler_params=small,
            name="edge_terms",
        )(*pieces)
        arrived = trade_columns(leaving)

        def inner_kernel(*refs):
            outs, inner, total, semaphores = refs[count : count + 2], *refs[count + 2 :]
            copies = Copies(semaphores)
            started = []
            for plane in range(2):
                bands = [add_band(band, plane, refs) for band in (1, 2, 3)]
                for number, value in enumerate(bands):
                    total[plane, :, number * HALO : (number + 1) * HALO] = value
                started.append(copies.start(total.at[plane], outs[plane]))
                for way in range(ways):
                    first = place.received(place.column(), way) == 0
                    inner[way, plane] = jnp.where(first, bands[0], bands[2])
            wait_for(started)

        *results, inner = pl.pallas_call(
            inner_kernel,
            out_shape=[sds((half_rows, width), f32)] * 2
            + [sds((ways, 2, half_rows, HALO), f32)],
            in_specs=piece_specs,
            out_specs=[HBM] * 2 + [VMEM],
            scratch_shapes=[
                pltpu.VMEM((2, half_rows, width), f32),
                pltpu.SemaphoreType.DMA((2,)),
            ],
            compiler_params=small,
            cost_estimate=pl.CostEstimate(flops=1 << 22, bytes_accessed=1 << 21, transcendentals=0),
            name="inner_terms",
        )(*pieces)

        def finish_kernel(phase_in, absorb_in, inner_ref, *refs):
            arrived_refs, outs = refs[:ways], refs[ways : ways + 2]
            strips, semaphores = refs[ways + 2 :]
            copies = Copies(semaphores)
            leaving = []
            for way in range(ways):
                start = place.received(place.column(), way) * (width - HALO)
                for plane in range(2):
                    strips[way, plane] = arrived_refs[way][plane] + inner_ref[way, plane]
                    target = outs[plane].at[:, pl.ds(pl.multiple_of(start, LANES), HALO)]
                    leaving.append(copies.start(strips.at[way, plane], target))
            wait_for(leaving)

        result = pl.pallas_call(
            finish_kernel,
            out_shape=[sds((half_rows, width), f32)] * 2,
            in_specs=[HBM, HBM, VMEM] + [VMEM] * ways,
            out_specs=[HBM] * 2,
            scratch_shapes=[
                pltpu.VMEM((ways, 2, half_rows, HALO), f32),
                pltpu.SemaphoreType.DMA((2 * ways,)),
            ],
            input_output_aliases={0: 0, 1: 1},
            compiler_params=small,
            name="finish",
        )(*results, inner, *arrived)
        return tuple(plane[None, None] for plane in result)

    in_specs = (
        P("section", "tile", None, None),
        P("section", "tile", None, None),
        P(),
        P("tile", "rep", None, None),
        P("tile", "rep", None, None, None),
    )
    out_specs = (P("section", "tile", "rep", None), P("section", "tile", "rep", None))
    return jax.shard_map(shards, mesh=mesh, in_specs=in_specs, out_specs=out_specs, check_vma=False)
```
